32 devices in a mesh: grp: 2 (over x), fsdp: 16 (over z, y, core).
Axes of the slice: x: 2, y: 2, z: 4, core: 2. Of those that a mesh axis runs over, the one named last changes fastest.
Arguments:
- token_states: bfloat16 [2, 48, 128, 4096], P('grp', 'fsdp'), may hold values from -250 to 250
- token_ids: int32 [2, 48, 128], P('grp', 'fsdp'), may hold values from 0 to 31999, as said below
- master: float32 [2, 4096, 1024], P('grp', 'fsdp'), may hold values from -0.09375 to 0.09375
- gain: float32 [4096], replicated, may hold values from 0.25 to 4.5
- cand_ids: int32 [48, 8], P('fsdp'), may hold values from 0 to 47, all different within a row
- slab_owner: int32 [48], replicated, may hold values from 0 to 15, as said below
Outputs:
- weights_out: float32 [2, 4096, 1024], P('grp', 'fsdp')
The draws below stay inside these ranges and needn't reach their ends.
Inputs may be any that keep to these rules, and one draw needn't show every extreme that they name: `token_ids`: 0 marks padding, which only follows a sequence's tokens; every sequence has 16 or more tokens. `slab_owner`: each fsdp index owns exactly 3 slab rows; the passages of slot 1 on the device with that index are the rows it owns, in increasing order. `cand_ids`: the ids of one row differ, and every slab row is some query's candidate.
All inputs are finite; a program needn't handle non-finite values.
Results may differ from the reference program's by a relative error of at most 0.012.
The reference program's roundings to bfloat16 on the way count: a program that leaves them out, or rounds other values in their place, can miss the bound.
Values may be sent and summed in bfloat16 or wider, within the bound.
No kernel may reach another device: no remote copies, remote signals or barrier semaphores. Data moves between devices by JAX's collectives and lax.ppermute only.
A program may use at most 64 MiB of HBM per device.

```python
import math
import jax
import jax.numpy as jnp
from jax import lax

D = 4096
E = 1024
VOCAB = 32000
LEN = 128
CANDS = 8
SEQ_DEV = 3
SEQS = 48
N_FSDP = 16


def draw_token_states(key, part):
    base_key = jax.random.fold_in(key, 11)
    key_base, key_row, key_column = jax.random.split(base_key, 3)
    values = jnp.clip(jax.random.normal(key_base, (2, SEQS, LEN, D), jnp.float32), -4.0, 4.0)
    row_scale = jnp.exp(jax.random.uniform(key_row, (2, SEQS, LEN, 1), jnp.float32, 0.0, math.log(10.0)))
    column_scale = jnp.exp(jax.random.uniform(key_column, (2, 1, 1, D), jnp.float32, math.log(0.5), math.log(5.0)))
    return (values * row_scale * column_scale).astype(jnp.bfloat16)


def draw_gain(key, part):
    gain_key = jax.random.fold_in(key, 23)
    ramp = jnp.arange(D, dtype=jnp.float32) / (D - 1)
    factor = jnp.exp(jax.random.uniform(gain_key, (D,), jnp.float32, -0.3, 0.3))
    return 0.6 * jnp.power(3.0, ramp) * factor


def draw_token_ids(key, part):
    id_key = jax.random.fold_in(key, 37)
    key_length, key_token = jax.random.split(id_key, 2)
    lengths = jax.random.randint(key_length, (2, SEQS, 1), LEN // 8, LEN + 1)
    tokens = jax.random.randint(key_token, (2, SEQS, LEN), 1, VOCAB)
    places = jnp.arange(LEN)[None, None, :]
    return jnp.where(places < lengths, tokens, 0).astype(jnp.int32)


def draw_slab_owner(key, part):
    shuffled = jax.random.permutation(jax.random.fold_in(key, 41), SEQS)
    return (shuffled // SEQ_DEV).astype(jnp.int32)


def levels(rng, dims, cuts, least, top_value):
    loudness = 1.0
    for position, parts in cuts:
        steps = jax.random.uniform(jax.random.fold_in(jax.random.fold_in(rng, 6), position), (parts,), jnp.float32, least / len(cuts), top_value / len(cuts))
        loudness = loudness * jnp.repeat(jnp.exp(steps), dims[position] // parts).reshape((-1,) + (1,) * (len(dims) - 1 - position))
    return loudness


def distinct(rng, rows, amount, top, lift):
    order = jax.random.permutation(jax.random.fold_in(rng, 1), amount)
    boost = order
    for power in range(3):
        boost = boost * boost // amount
    boost = boost * lift // amount
    lots = jax.random.randint(jax.random.fold_in(rng, 2), (rows, amount), 0, 4096) + boost
    sure = jax.random.permutation(jax.random.fold_in(rng, 3), rows)[jnp.arange(amount) % rows]
    lots = jnp.where(jnp.arange(rows)[:, None] == sure[None, :], 1 << 14, lots)
    score = lots * amount + jnp.arange(amount)
    return lax.top_k(score.astype(jnp.int32), top)[1].astype(jnp.int32)


def normal_values(rng, shape, spread, limit, shards=(), kind=jnp.bfloat16):
    entries = jax.random.normal(rng, shape, jnp.float32) * spread
    if len(shards) > 0:
        entries = levels(rng, shape, shards, -0.22, 0.18) * entries
    return jnp.clip(entries, min=-limit, max=limit).astype(kind)


def setup_inputs(seed: int = 0) -> dict:
    streams_of = jax.random.split(jax.random.key(seed), 7)
    token_states = draw_token_states(jax.random.fold_in(streams_of[6], 71), 0)
    token_ids = draw_token_ids(jax.random.fold_in(streams_of[6], 71), 0)
    master = normal_values(streams_of[2], (2, D, E), D ** -0.5, 0.09375, ((0, 2), (1, 16)), jnp.float32)
    gain = draw_gain(jax.random.fold_in(streams_of[6], 71), 0)
    cand_ids = distinct(streams_of[4], SEQS, SEQS, CANDS, 2730)
    slab_owner = draw_slab_owner(jax.random.fold_in(streams_of[6], 71), 0)
    return {"token_states": token_states, "token_ids": token_ids, "master": master, "gain": gain, "cand_ids": cand_ids, "slab_owner": slab_owner}


sharpness = 20.0

def normalize_tokens(states, gain):
    states_wide = states.astype(jnp.float32)
    mean_square = lax.optimization_barrier(jnp.mean(states_wide * states_wide, axis=-1, keepdims=True))
    return (states_wide * lax.rsqrt(mean_square + 1e-05) * gain).astype(jnp.bfloat16)

def block_forward(states, token_ids, weight_bf, gain):
    blocks, length, width = states.shape
    normed = normalize_tokens(states, gain).reshape(blocks * length, width)
    hidden = jnp.dot(normed, weight_bf, preferred_element_type=jnp.float32)
    active = jnp.tanh(hidden).reshape(blocks, length, -1)
    valid = (token_ids != 0).astype(jnp.float32)
    counts = lax.optimization_barrier(jnp.sum(valid, axis=1))
    pooled = lax.optimization_barrier(jnp.sum(active * valid[:, :, None], axis=1)) / counts[:, None]
    return (normed, active, valid, counts, pooled)

def encode(states, token_ids, weight_bf, gain):
    grouped = states.reshape(SEQS // 16, 16, LEN, D)
    grouped_ids = token_ids.reshape(SEQS // 16, 16, LEN)

    def one_block(pair):
        return block_forward(pair[0], pair[1], weight_bf, gain)[4]
    pooled = lax.map(one_block, (grouped, grouped_ids))
    return pooled.reshape(SEQS, E)

def unit_rows(pooled):
    mean_square = lax.optimization_barrier(jnp.mean(pooled * pooled, axis=-1, keepdims=True))
    scale = lax.rsqrt(mean_square + 1e-06)
    return (pooled * scale, scale)

def reference(token_states, token_ids, master, gain, cand_ids, slab_owner):
    query_weight = master[0].astype(jnp.bfloat16)
    passage_weight = master[1].astype(jnp.bfloat16)
    query_pool = encode(token_states[0], token_ids[0], query_weight, gain)
    passage_pool = encode(token_states[1], token_ids[1], passage_weight, gain)
    query_unit, query_scale = unit_rows(query_pool)
    passage_unit, passage_scale = unit_rows(passage_pool)
    stored = passage_unit.astype(jnp.bfloat16)
    owners = jnp.arange(N_FSDP, dtype=jnp.int32)
    onehot = (slab_owner[:, None] == owners[None, :]).astype(jnp.int32)
    ranks = lax.optimization_barrier(jnp.sum((jnp.cumsum(onehot, axis=0) - onehot) * onehot, axis=1))
    places = (slab_owner * SEQ_DEV + ranks).astype(jnp.int32)
    chosen = stored[places[cand_ids]].astype(jnp.float32)
    logits = sharpness / E * jnp.einsum('qe,qje->qj', query_unit, chosen, precision=lax.Precision.HIGHEST)
    exponent = jnp.exp(logits)
    probs = exponent / lax.optimization_barrier(jnp.sum(exponent, axis=-1, keepdims=True))
    target = (jnp.arange(CANDS) == 0).astype(jnp.float32)
    logit_grad = probs - target[None, :]
    unit_grad = sharpness / E * jnp.einsum('qj,qje->qe', logit_grad, chosen, precision=lax.Precision.HIGHEST)
    inner = lax.optimization_barrier(jnp.sum(query_pool * unit_grad, axis=-1, keepdims=True))
    pooled_grad = query_scale * unit_grad - query_pool * (query_scale * query_scale * query_scale) * inner / E
    grouped = token_states[0].reshape(SEQS // 16, 16, LEN, D)
    grouped_ids = token_ids[0].reshape(SEQS // 16, 16, LEN)
    grouped_grad = pooled_grad.reshape(SEQS // 16, 16, E)

    def accumulate(running, triple):
        normed, active, valid, counts, pooled = block_forward(triple[0], triple[1], query_weight, gain)
        delta = (valid / counts[:, None])[:, :, None] * triple[2][:, None, :] * (1.0 - active * active)
        delta = delta.astype(jnp.bfloat16).reshape(-1, E)
        return (running + jnp.dot(normed.T, delta, preferred_element_type=jnp.float32), None)
    grad, unused = lax.scan(accumulate, jnp.zeros((D, E), jnp.float32), (grouped, grouped_ids, grouped_grad))
    row_square = lax.optimization_barrier(jnp.mean(grad * grad, axis=1, keepdims=True))
    normalized = grad * lax.rsqrt(row_square + 1e-06)
    copied = lax.optimization_barrier(query_weight).astype(jnp.float32)
    return jnp.stack([normalized, copied])
```

```python
import jax
import jax.numpy as jnp
from jax import lax
from jax.sharding import PartitionSpec as P

sharpness = 20.0


def passed_along(shard, axis, by):
    size = lax.axis_size(axis)
    pairs = [(i, i + by) for i in range(size) if 0 <= i + by < size]
    return lax.ppermute(shard, axis, pairs)


def shards(token_states, token_ids, master, gain, cand_ids, slab_owner):
    trainer = lax.axis_index("grp") == 0
    devices_fsdp = lax.axis_size("fsdp")
    states = token_states[0]
    seq_dev, length, width = states.shape
    embedding = master.shape[2]
    shard_rows = master.shape[1]
    tokens_dev = seq_dev * length
    states_wide = states.astype(jnp.float32)
    mean_square = jnp.mean(states_wide * states_wide, axis=-1, keepdims=True)
    normed = (
        (states_wide * lax.rsqrt(mean_square + 1e-05) * gain)
        .astype(jnp.bfloat16)
        .reshape(tokens_dev, width)
    )
    weight_bf = master[0].astype(jnp.bfloat16)
    hidden = jnp.dot(
        normed,
        lax.all_gather(weight_bf, "fsdp", axis=0, tiled=True),
        preferred_element_type=jnp.float32,
    )
    copied = passed_along(weight_bf, "grp", 1)
    active = jnp.tanh(hidden).reshape(seq_dev, length, embedding)
    valid = (token_ids[0] != 0).astype(jnp.float32)
    counts = jnp.sum(valid, axis=1)
    pooled = jnp.sum(active * valid[:, :, None], axis=1) / counts[:, None]
    pooled_square = jnp.mean(pooled * pooled, axis=-1, keepdims=True)
    scale = lax.rsqrt(pooled_square + 1e-06)
    unit = pooled * scale
    stored = unit.astype(jnp.bfloat16)
    owners = jnp.arange(devices_fsdp, dtype=jnp.int32)
    onehot = (slab_owner[:, None] == owners[None, :]).astype(jnp.int32)
    ranks = jnp.sum((jnp.cumsum(onehot, axis=0) - onehot) * onehot, axis=1)
    places = slab_owner * seq_dev + ranks
    wanted = places[cand_ids]
    mine = passed_along(stored, "grp", -1)
    slab = lax.all_gather(mine, "fsdp", axis=0, tiled=True)
    chosen = slab[wanted]
    chosen_wide = chosen.astype(jnp.float32)
    logits = (
        sharpness
        / embedding
        * jnp.einsum("qe,qje->qj", unit, chosen_wide, precision=lax.Precision.HIGHEST)
    )
    exponent = jnp.exp(logits)
    probs = exponent / jnp.sum(exponent, axis=-1, keepdims=True)
    target = (jnp.arange(chosen.shape[1]) == 0).astype(jnp.float32)
    logit_grad = probs - target[None, :]
    unit_grad = (
        sharpness
        / embedding
        * jnp.einsum("qj,qje->qe", logit_grad, chosen_wide, precision=lax.Precision.HIGHEST)
    )
    inner = jnp.sum(pooled * unit_grad, axis=-1, keepdims=True)
    pooled_grad = scale * unit_grad - pooled * (scale * scale * scale) * inner / embedding
    delta = (
        (valid / counts[:, None])[:, :, None] * pooled_grad[:, None, :] * (1.0 - active * active)
    )
    delta = delta.astype(jnp.bfloat16).reshape(tokens_dev, embedding)

    def compute():
        return lax.dot_general(
            normed, delta, (((0,), (0,)), ((), ())), preferred_element_type=jnp.float32
        ).astype(jnp.bfloat16)

    shard = lax.psum_scatter(
        lax.cond(
            trainer,
            compute,
            lambda: jnp.zeros((lax.axis_size("fsdp") * shard_rows, embedding), jnp.bfloat16),
        ),
        "fsdp",
        scatter_dimension=0,
        tiled=True,
    ).astype(jnp.float32)
    row_square = jnp.mean(shard * shard, axis=1, keepdims=True)
    normalized = shard * lax.rsqrt(row_square + 1e-06)
    result = jnp.where(trainer, normalized, copied.astype(jnp.float32))
    return result[None]


def solution(mesh):
    placed = (
        P("grp", "fsdp", None, None),
        P("grp", "fsdp", None),
        P("grp", "fsdp", None),
        P(),
        P("fsdp", None),
        P(),
    )
    return jax.shard_map(
        shards, mesh=mesh, in_specs=placed, out_specs=P("grp", "fsdp", None), check_vma=False
    )
```

```python
import jax
import jax.numpy as jnp
from jax import lax
from jax.sharding import Mesh, PartitionSpec as P

sharpness = 20.0
cores = 2
longest_ring = 16


def ring_order(chips):
    return list(range(0, chips, 2)) + list(range(1, chips, 2))[::-1]


def ring_place(chip, chips):
    return jnp.where(chip % 2 == 0, chip // 2, chips - 1 - chip // 2)


def ring_chip(place, chips):
    place = lax.rem(place + 2 * chips, chips)
    return jnp.where(place < chips // 2, 2 * place, 2 * (chips - 1 - place) + 1)


def along_ring(block, by):
    order = ring_order(lax.axis_size("chip"))
    pairs = [(chip, order[(i + by) % len(order)]) for i, chip in enumerate(order)]
    return lax.ppermute(block, "chip", pairs)


def from_sibling(block):
    return lax.ppermute(block, "core", [(0, 1), (1, 0)])


def in_core_order(mine, other, core, axis=0):
    return jnp.where(
        core == 0,
        jnp.concatenate([mine, other], axis=axis),
        jnp.concatenate([other, mine], axis=axis),
    )


def shards(token_states, token_ids, master, gain, cand_ids, slab_owner):
    trainer = lax.axis_index("grp") == 0
    chips = lax.axis_size("chip")
    chip = lax.axis_index("chip")
    core = lax.axis_index("core")
    place = ring_place(chip, chips)
    states = token_states[0]
    seq_dev, length, width = states.shape
    rows, embedding = master.shape[1:]
    half = embedding // cores
    tokens_dev = seq_dev * length
    seqs = cores * seq_dev

    weight_bf = master[0].astype(jnp.bfloat16)
    own = lax.dynamic_slice(weight_bf, (0, core * half), (rows, half))
    sibling = from_sibling(lax.dynamic_slice(weight_bf, (0, (1 - core) * half), (rows, half)))
    copied = lax.ppermute(weight_bf, "grp", [(0, 1)])

    states_wide = states.astype(jnp.float32)
    mean_square = jnp.mean(states_wide * states_wide, axis=-1, keepdims=True)
    normed = (
        (states_wide * lax.rsqrt(mean_square + 1e-05) * gain)
        .astype(jnp.bfloat16)
        .reshape(tokens_dev, width)
    )
    normed = jnp.concatenate([normed, from_sibling(normed)])
    ids = jnp.concatenate([token_ids[0], cand_ids], axis=1)
    ids = jnp.concatenate([ids, from_sibling(ids)])
    valid = (ids[:, :length] != 0).astype(jnp.float32)
    counts = jnp.sum(valid, axis=1)
    weighted = valid / counts[:, None]
    cands = ids[:, length:]

    def columns(offset, part):
        first = (ring_chip(place + offset, chips) * cores + part) * rows
        return lax.dynamic_slice(normed, (0, first), (seqs * length, rows))

    def product(offset, part, block):
        return jnp.dot(columns(offset, part), block, preferred_element_type=jnp.float32)

    parts = (core, 1 - core)
    if chips <= longest_ring:
        hidden = product(0, parts[0], own) + product(0, parts[1], sibling)
        moving = {(i, by): block for by in (1, -1) for i, block in enumerate((own, sibling))}
        for step in range(1, chips // 2 + 1):
            for i, by in ((0, 1), (1, -1), (1, 1), (0, -1)):
                if step == chips // 2 and (i, by) not in ((0, 1), (1, -1)):
                    continue
                moving[i, by] = along_ring(moving[i, by], by)
                hidden = hidden + product(-by * step, parts[i], moving[i, by])
    else:
        both = in_core_order(own, sibling, core)
        gathered = lax.all_gather(both, "chip", axis=0, tiled=True)
        hidden = jnp.dot(normed, gathered, preferred_element_type=jnp.float32)

    active = jnp.tanh(hidden).reshape(seqs, length, half)
    pooled = jnp.sum(active * valid[:, :, None], axis=1) / counts[:, None]
    pooled_other = from_sibling(pooled)
    pooled_other = jnp.concatenate([pooled_other[seq_dev:], pooled_other[:seq_dev]])
    whole = in_core_order(pooled, pooled_other, core, axis=1)
    pooled_square = jnp.mean(whole * whole, axis=-1, keepdims=True)
    scale = lax.rsqrt(pooled_square + 1e-06)
    unit = whole * scale
    stored = unit.astype(jnp.bfloat16)
    stored = in_core_order(stored[:seq_dev], stored[seq_dev:], core)

    devices_fsdp = chips * cores
    owners = jnp.arange(devices_fsdp, dtype=jnp.int32)
    onehot = (slab_owner[:, None] == owners[None, :]).astype(jnp.int32)
    ranks = jnp.sum((jnp.cumsum(onehot, axis=0) - onehot) * onehot, axis=1)
    places = slab_owner * seq_dev + ranks
    wanted = places[cands]
    groups = lax.axis_size("grp")
    spread = jnp.broadcast_to(stored[None], (groups * chips,) + stored.shape)
    spread = lax.all_to_all(spread, ("grp", "chip"), 0, 0)
    slab = spread[(groups - 1) * chips :].reshape(devices_fsdp * seq_dev, embedding)

    chosen = slab[wanted].astype(jnp.float32)
    logits = (
        sharpness
        / embedding
        * jnp.einsum("qe,qje->qj", unit, chosen, precision=lax.Precision.HIGHEST)
    )
    exponent = jnp.exp(logits)
    probs = exponent / jnp.sum(exponent, axis=-1, keepdims=True)
    target = (jnp.arange(chosen.shape[1]) == 0).astype(jnp.float32)
    logit_grad = probs - target[None, :]
    unit_grad = (
        sharpness
        / embedding
        * jnp.einsum("qj,qje->qe", logit_grad, chosen, precision=lax.Precision.HIGHEST)
    )
    inner = jnp.sum(whole * unit_grad, axis=-1, keepdims=True)
    pooled_grad = scale * unit_grad - whole * (scale * scale * scale) * inner / embedding
    pooled_grad = lax.dynamic_slice(pooled_grad, (0, core * half), (seqs, half))
    delta = weighted[:, :, None] * pooled_grad[:, None, :] * (1.0 - active * active)
    delta = delta.astype(jnp.bfloat16).reshape(seqs * length, half)

    def term(offset, part):
        return lax.dot_general(
            columns(offset, part),
            delta,
            (((0,), (0,)), ((), ())),
            preferred_element_type=jnp.float32,
        )

    if chips <= longest_ring:
        arrived = {}
        for step in range(chips // 2, 0, -1):
            for i, by in ((1, -1), (0, 1), (1, 1), (0, -1)):
                if step == chips // 2 and (i, by) not in ((0, 1), (1, -1)):
                    continue
                total = term(by * step, parts[i])
                if (i, by) in arrived:
                    total = total + arrived[i, by].astype(jnp.float32)
                arrived[i, by] = along_ring(total.astype(jnp.bfloat16), by)
        mine, other = [
            term(0, parts[i])
            + arrived[i, 1].astype(jnp.float32)
            + arrived[i, -1].astype(jnp.float32)
            for i in range(2)
        ]
    else:
        grad = lax.dot_general(
            normed, delta, (((0,), (0,)), ((), ())), preferred_element_type=jnp.float32
        )
        reduced = lax.psum_scatter(grad, "chip", scatter_dimension=0, tiled=True)
        mine, other = [lax.dynamic_slice(reduced, (i * rows, 0), (rows, half)) for i in parts]
    other = from_sibling(other)
    shard = in_core_order(mine, other, core, axis=1)
    row_square = jnp.mean(shard * shard, axis=1, keepdims=True)
    normalized = shard * lax.rsqrt(row_square + 1e-06)
    result = jnp.where(trainer, normalized, copied.astype(jnp.float32))
    return result[None]


def solution(mesh):
    groups, devices_fsdp = mesh.devices.shape
    finer = Mesh(
        mesh.devices.reshape(groups, devices_fsdp // cores, cores), ("grp", "chip", "core")
    )
    fsdp = ("chip", "core")
    placed = (
        P("grp", fsdp, None, None),
        P("grp", fsdp, None),
        P("grp", fsdp, None),
        P(),
        P(fsdp, None),
        P(),
    )
    return jax.shard_map(
        shards, mesh=finer, in_specs=placed, out_specs=P("grp", fsdp, None), check_vma=False
    )
```

```python
import jax
import jax.numpy as jnp
from jax import lax
from jax.sharding import Mesh, PartitionSpec as P

sharpness = 20.0
cores = 2
longest_ring = 16


def ring_order(chips):
    return list(range(0, chips, 2)) + list(range(1, chips, 2))[::-1]


def ring_place(chip, chips):
    return jnp.where(chip % 2 == 0, chip // 2, chips - 1 - chip // 2)


def ring_chip(place, chips):
    place = lax.rem(place + 2 * chips, chips)
    return jnp.where(place < chips // 2, 2 * place, 2 * (chips - 1 - place) + 1)


def along_ring(block, by):
    order = ring_order(lax.axis_size("chip"))
    pairs = [(chip, order[(i + by) % len(order)]) for i, chip in enumerate(order)]
    return lax.ppermute(block, "chip", pairs)


def after(first, block):
    return lax.optimization_barrier((first, block))[1]


def from_sibling(block):
    return lax.ppermute(block, "core", [(0, 1), (1, 0)])


def slab_blocks(stored, chips, core):
    order = ring_order(chips)
    kept = []
    for j in range(chips // cores):
        pairs = []
        for i, chip in enumerate(order):
            for c in range(cores):
                source = order[(i + j + c * (chips // cores)) % chips]
                pairs.append(((chips + source) * cores + c, chip * cores + c))
        kept.append(lax.ppermute(stored, ("grp", "chip", "core"), pairs))
    kept = jnp.concatenate(kept)
    other = from_sibling(kept)
    return [jnp.where(core == 0, kept, other), jnp.where(core == 0, other, kept)]


def in_core_order(mine, other, core, axis=0):
    return jnp.where(
        core == 0,
        jnp.concatenate([mine, other], axis=axis),
        jnp.concatenate([other, mine], axis=axis),
    )


def normalize(states, gain):
    states_wide = states.astype(jnp.float32)
    mean_square = jnp.mean(states_wide * states_wide, axis=-1, keepdims=True)
    return (states_wide * lax.rsqrt(mean_square + 1e-05) * gain).astype(jnp.bfloat16)


def shards(token_states, token_ids, master, gain, cand_ids, slab_owner):
    trainer = lax.axis_index("grp") == 0
    chips = lax.axis_size("chip")
    chip = lax.axis_index("chip")
    core = lax.axis_index("core")
    place = ring_place(chip, chips)
    states = token_states[0]
    seq_dev, length, width = states.shape
    rows, embedding = master.shape[1:]
    half = embedding // cores
    seqs = cores * seq_dev

    weights = master[0]
    own = lax.dynamic_slice(weights, (0, core * half), (rows, half)).astype(jnp.bfloat16)
    given = lax.dynamic_slice(weights, (0, (1 - core) * half), (rows, half))
    given = given.astype(jnp.bfloat16)
    sibling = from_sibling(given)

    normed = normalize(states, gain)
    normed, weights = lax.optimization_barrier((normed, weights))
    copied = lax.ppermute(weights.astype(jnp.bfloat16), "grp", [(0, 1)])
    normed = jnp.concatenate([normed, normalize(from_sibling(states), gain)])
    normed = normed.reshape(seqs * length, width)
    ids = jnp.concatenate([token_ids[0], cand_ids], axis=1)
    ids = jnp.concatenate([ids, from_sibling(ids)])
    valid = (ids[:, :length] != 0).astype(jnp.float32)
    counts = jnp.sum(valid, axis=1)
    weighted = valid / counts[:, None]
    cands = ids[:, length:]

    def columns(offset, part):
        first = (ring_chip(place + offset, chips) * cores + part) * rows
        return lax.dynamic_slice(normed, (0, first), (seqs * length, rows))

    def product(offset, part, block):
        return jnp.dot(columns(offset, part), block, preferred_element_type=jnp.float32)

    parts = (core, 1 - core)
    if chips <= longest_ring:
        moving = {(i, by): block for by in (1, -1) for i, block in enumerate((own, sibling))}
        sums = [None]
        for step in range(1, chips // 2 + 1):
            sent = [(0, 1), (1, -1), (1, 1), (0, -1)]
            if step == chips // 2:
                sent = sent[:2]
            if step == 1:
                total = product(0, parts[0], own) + product(0, parts[1], sibling)
            else:
                total = sums[-1]
            for i, by in sent:
                if step > 2:
                    moving[i, by] = after(sums[step - 2], moving[i, by])
                moving[i, by] = along_ring(moving[i, by], by)
                total = total + product(-by * step, parts[i], moving[i, by])
            sums.append(total)
        hidden = sums[-1]
    else:
        both = in_core_order(own, sibling, core)
        gathered = lax.all_gather(both, "chip", axis=0, tiled=True)
        hidden = jnp.dot(normed, gathered, preferred_element_type=jnp.float32)

    active = jnp.tanh(hidden).reshape(seqs, length, half)
    pooled = jnp.sum(active * valid[:, :, None], axis=1) / counts[:, None]
    pooled, copied = lax.optimization_barrier((pooled, copied))
    pooled_other = from_sibling(pooled)
    pooled_other = jnp.concatenate([pooled_other[seq_dev:], pooled_other[:seq_dev]])
    whole = in_core_order(pooled, pooled_other, core, axis=1)
    pooled_square = jnp.mean(whole * whole, axis=-1, keepdims=True)
    scale = lax.rsqrt(pooled_square + 1e-06)
    unit = whole * scale
    stored = unit.astype(jnp.bfloat16)
    stored = in_core_order(stored[:seq_dev], stored[seq_dev:], core)

    devices_fsdp = chips * cores
    owners = jnp.arange(devices_fsdp, dtype=jnp.int32)
    onehot = (slab_owner[:, None] == owners[None, :]).astype(jnp.int32)
    ranks = jnp.sum((jnp.cumsum(onehot, axis=0) - onehot) * onehot, axis=1)
    places = slab_owner * seq_dev + ranks
    wanted = places[cands]
    slab = jnp.concatenate(slab_blocks(stored, chips, core))
    seen = lax.rem(ring_place(wanted // seqs, chips) - place + chips, chips)
    wanted = seen * seqs + lax.rem(wanted, seqs)
    chosen = slab[wanted].astype(jnp.float32)
    logits = (
        sharpness
        / embedding
        * jnp.einsum("qe,qje->qj", unit, chosen, precision=lax.Precision.HIGHEST)
    )
    exponent = jnp.exp(logits)
    probs = exponent / jnp.sum(exponent, axis=-1, keepdims=True)
    target = (jnp.arange(chosen.shape[1]) == 0).astype(jnp.float32)
    logit_grad = probs - target[None, :]
    unit_grad = (
        sharpness
        / embedding
        * jnp.einsum("qj,qje->qe", logit_grad, chosen, precision=lax.Precision.HIGHEST)
    )
    inner = jnp.sum(whole * unit_grad, axis=-1, keepdims=True)
    pooled_grad = scale * unit_grad - whole * (scale * scale * scale) * inner / embedding
    pooled_grad = lax.dynamic_slice(pooled_grad, (0, core * half), (seqs, half))
    delta = weighted[:, :, None] * pooled_grad[:, None, :] * (1.0 - active * active)
    delta = delta.astype(jnp.bfloat16).reshape(seqs * length, half)

    def term(offset, part):
        return lax.dot_general(
            columns(offset, part),
            delta,
            (((0,), (0,)), ((), ())),
            preferred_element_type=jnp.float32,
        )

    if chips <= longest_ring:
        arrived = {}
        for step in range(chips // 2, 0, -1):
            for i, by in ((1, -1), (0, 1), (1, 1), (0, -1)):
                if step == chips // 2 and (i, by) not in ((0, 1), (1, -1)):
                    continue
                total = term(by * step, parts[i])
                if (i, by) in arrived:
                    total = total + arrived[i, by].astype(jnp.float32)
                arrived[i, by] = along_ring(total.astype(jnp.bfloat16), by)
        mine, other = [
            term(0, parts[i])
            + arrived[i, 1].astype(jnp.float32)
            + arrived[i, -1].astype(jnp.float32)
            for i in range(2)
        ]
    else:
        grad = lax.dot_general(
            normed, delta, (((0,), (0,)), ((), ())), preferred_element_type=jnp.float32
        )
        reduced = lax.psum_scatter(grad, "chip", scatter_dimension=0, tiled=True)
        mine, other = [lax.dynamic_slice(reduced, (i * rows, 0), (rows, half)) for i in parts]
    other = from_sibling(other)
    shard = in_core_order(mine, other, core, axis=1)
    row_square = jnp.mean(shard * shard, axis=1, keepdims=True)
    normalized = shard * lax.rsqrt(row_square + 1e-06)
    result = jnp.where(trainer, normalized, copied.astype(jnp.float32))
    return result[None]


def solution(mesh):
    groups, devices_fsdp = mesh.devices.shape
    finer = Mesh(
        mesh.devices.reshape(groups, devices_fsdp // cores, cores), ("grp", "chip", "core")
    )
    fsdp = ("chip", "core")
    placed = (
        P("grp", fsdp, None, None),
        P("grp", fsdp, None),
        P("grp", fsdp, None),
        P(),
        P(fsdp, None),
        P(),
    )
    return jax.shard_map(
        shards, mesh=finer, in_specs=placed, out_specs=P("grp", fsdp, None), check_vma=False
    )
```

```python
import functools

import jax
import jax.numpy as jnp
from jax import lax
from jax.experimental import pallas as pl
from jax.experimental.pallas import tpu as pltpu
from jax.sharding import Mesh, PartitionSpec as P

sharpness = 20.0
cores = 2
longest_ring = 16
vmem_limit = 32 << 20


def ring_order(chips):
    return list(range(0, chips, 2)) + list(range(1, chips, 2))[::-1]


def ring_place(chip, chips):
    return jnp.where(chip % 2 == 0, chip // 2, chips - 1 - chip // 2)


def ring_chip(place, chips):
    place = lax.rem(place + 2 * chips, chips)
    return jnp.where(place < chips // 2, 2 * place, 2 * (chips - 1 - place) + 1)


def along_ring(block, by):
    order = ring_order(lax.axis_size("chip"))
    pairs = [(chip, order[(i + by) % len(order)]) for i, chip in enumerate(order)]
    return lax.ppermute(block, "chip", pairs)


def after(first, block):
    return lax.optimization_barrier((first, block))[1]


def from_sibling(block):
    return lax.ppermute(block, "core", [(0, 1), (1, 0)])


def slab_blocks(stored, chips, core):
    order = ring_order(chips)
    kept = []
    for j in range(chips // cores):
        pairs = []
        for i, chip in enumerate(order):
            for c in range(cores):
                source = order[(i + j + c * (chips // cores)) % chips]
                pairs.append(((chips + source) * cores + c, chip * cores + c))
        kept.append(lax.ppermute(stored, ("grp", "chip", "core"), pairs))
    kept = jnp.concatenate(kept)
    other = from_sibling(kept)
    return [jnp.where(core == 0, kept, other), jnp.where(core == 0, other, kept)]


def in_core_order(mine, other, core, axis=0):
    return jnp.where(
        core == 0,
        jnp.concatenate([mine, other], axis=axis),
        jnp.concatenate([other, mine], axis=axis),
    )


def normalize_kernel(seqs, chunk, mine_ref, other_ref, gain_ref, out_ref):
    length = mine_ref.shape[1]

    def run(ref):
        @pl.loop(0, length // chunk)
        def _(i):
            at = pl.ds(pl.multiple_of(i * chunk, chunk), chunk)
            wide = ref[0, at, :].astype(jnp.float32)
            mean_square = jnp.mean(wide * wide, axis=-1, keepdims=True)
            wide = wide * lax.rsqrt(mean_square + 1e-05) * gain_ref[...]
            out_ref[at, :] = wide.astype(jnp.bfloat16)

    @pl.when(pl.program_id(0) < seqs)
    def _():
        run(mine_ref)

    @pl.when(pl.program_id(0) >= seqs)
    def _():
        run(other_ref)


def normalize_both(mine, other, gain):
    seqs, length, width = mine.shape
    tokens = 2 * seqs * length
    return pl.pallas_call(
        functools.partial(normalize_kernel, seqs, 16),
        grid=(2 * seqs,),
        in_specs=[
            pl.BlockSpec((1, length, width), lambda i: (jnp.minimum(i, seqs - 1), 0, 0)),
            pl.BlockSpec((1, length, width), lambda i: (jnp.maximum(i - seqs, 0), 0, 0)),
            pl.BlockSpec((1, width), lambda i: (0, 0)),
        ],
        out_specs=pl.BlockSpec((length, width), lambda i: (i, 0)),
        out_shape=jax.ShapeDtypeStruct((tokens, width), jnp.bfloat16),
        compiler_params=pltpu.CompilerParams(vmem_limit_bytes=vmem_limit),
        cost_estimate=pl.CostEstimate(
            flops=6 * tokens * width, bytes_accessed=4 * tokens * width, transcendentals=tokens
        ),
    )(mine, other, gain[None])


def blocks_kernel(amount, has_total, last, length, offsets_ref, counts_ref, *refs):
    columns, blocks, rest = refs[:amount], refs[amount : 2 * amount], refs[2 * amount :]
    total = None
    for column, block in zip(columns, blocks):
        term = jnp.dot(column[...], block[...], preferred_element_type=jnp.float32)
        total = term if total is None else total + term
    if has_total:
        total = total + rest[0][...]
        rest = rest[1:]
    if not last:
        rest[0][...] = total
        return
    slope_ref, pooled_ref = rest
    active = jnp.tanh(total)
    seqs = active.shape[0] // length
    active = active.reshape(seqs, length, active.shape[1])
    for i in range(seqs):
        count = counts_ref[pl.program_id(0) * seqs + i]
        there = lax.broadcasted_iota(jnp.int32, active.shape[1:], 0) < count
        part = jnp.where(there, active[i], 0.0)
        pooled_ref[i] = jnp.sum(part, axis=0, keepdims=True)
        slope_ref[pl.ds(i * length, length), :] = jnp.where(there, 1.0 - part * part, 0.0)


def add_blocks(normed, offsets, blocks, total, counts, length, last):
    tokens = normed.shape[0]
    rows, half = blocks[0].shape
    amount = len(blocks)
    tile = 2 * length if tokens % (2 * length) == 0 else length
    in_specs = [
        pl.BlockSpec((tile, rows), lambda i, offsets, counts, b=b: (i, offsets[b]))
        for b in range(amount)
    ]
    in_specs += [pl.BlockSpec((rows, half), lambda i, offsets, counts: (0, 0))] * amount
    operands = [normed] * amount + list(blocks)
    whole = pl.BlockSpec((tile, half), lambda i, offsets, counts: (i, 0))
    if total is not None:
        in_specs.append(whole)
        operands.append(total)
    out_specs = whole
    out_shape = jax.ShapeDtypeStruct((tokens, half), jnp.float32)
    if last:
        out_specs = [whole, pl.BlockSpec((tile // length, 1, half), lambda i, offsets, counts: (i, 0, 0))]
        out_shape = [out_shape, jax.ShapeDtypeStruct((tokens // length, 1, half), jnp.float32)]
    return pl.pallas_call(
        functools.partial(blocks_kernel, amount, total is not None, last, length),
        grid_spec=pltpu.PrefetchScalarGridSpec(
            num_scalar_prefetch=2, grid=(tokens // tile,), in_specs=in_specs, out_specs=out_specs
        ),
        out_shape=out_shape,
        compiler_params=pltpu.CompilerParams(vmem_limit_bytes=vmem_limit),
        cost_estimate=pl.CostEstimate(
            flops=2 * tokens * rows * half * amount,
            bytes_accessed=2 * amount * rows * (tokens + half) + 8 * tokens * half,
            transcendentals=tokens * half if last else 0,
        ),
    )(offsets, counts, *operands)


def shards(token_states, token_ids, master, gain, cand_ids, slab_owner):
    trainer = lax.axis_index("grp") == 0
    chips = lax.axis_size("chip")
    chip = lax.axis_index("chip")
    core = lax.axis_index("core")
    place = ring_place(chip, chips)
    states = token_states[0]
    seq_dev, length, width = states.shape
    rows, embedding = master.shape[1:]
    half = embedding // cores
    seqs = cores * seq_dev

    weights = master[0]
    own = lax.dynamic_slice(weights, (0, core * half), (rows, half)).astype(jnp.bfloat16)
    given = lax.dynamic_slice(weights, (0, (1 - core) * half), (rows, half))
    given = given.astype(jnp.bfloat16)
    sibling = from_sibling(given)

    normed = normalize_both(states, from_sibling(states), gain)
    ids = jnp.concatenate([token_ids[0], cand_ids], axis=1)
    ids = jnp.concatenate([ids, from_sibling(ids)])
    lengths = jnp.sum((ids[:, :length] != 0).astype(jnp.int32), axis=1)
    counts = lengths.astype(jnp.float32)
    cands = ids[:, length:]

    def first_column(offset, part):
        return ring_chip(place + offset, chips) * cores + part

    def columns(offset, part):
        first = first_column(offset, part) * rows
        return lax.dynamic_slice(normed, (0, first), (seqs * length, rows))

    parts = (core, 1 - core)
    if chips <= longest_ring:
        moving = {(i, by): block for by in (1, -1) for i, block in enumerate((own, sibling))}
        sums = [None]
        blocks, offsets = [own, sibling], [first_column(0, part) for part in parts]
        for step in range(1, chips // 2 + 1):
            last = step == chips // 2
            sent = [(0, 1), (1, -1)] if last else [(0, 1), (0, -1), (1, 1), (1, -1)]
            for i, by in sent:
                if step > 2 and i == 1:
                    moving[i, by] = after(sums[step - 2], moving[i, by])
                moving[i, by] = along_ring(moving[i, by], by)
                blocks.append(moving[i, by])
                offsets.append(first_column(-by * step, parts[i]))
            total = add_blocks(
                normed, jnp.stack(offsets), blocks, sums[-1], lengths, length, last
            )
            sums.append(total)
            blocks, offsets = [], []
        slope, pooled = sums[-1]
        pooled = pooled[:, 0] / counts[:, None]
    else:
        both = in_core_order(own, sibling, core)
        gathered = lax.all_gather(both, "chip", axis=0, tiled=True)
        hidden = jnp.dot(normed, gathered, preferred_element_type=jnp.float32)
        active = jnp.tanh(hidden).reshape(seqs, length, half)
        there = jnp.arange(length)[None, :, None] < lengths[:, None, None]
        active = jnp.where(there, active, 0.0)
        pooled = jnp.sum(active, axis=1) / counts[:, None]
        slope = jnp.where(there, 1.0 - active * active, 0.0).reshape(seqs * length, half)

    pooled_other = from_sibling(pooled)
    pooled_other = jnp.concatenate([pooled_other[seq_dev:], pooled_other[:seq_dev]])
    whole = in_core_order(pooled, pooled_other, core, axis=1)
    pooled_square = jnp.mean(whole * whole, axis=-1, keepdims=True)
    scale = lax.rsqrt(pooled_square + 1e-06)
    unit = whole * scale
    stored = unit.astype(jnp.bfloat16)
    stored = in_core_order(stored[:seq_dev], stored[seq_dev:], core)

    slab = jnp.concatenate(slab_blocks(stored, chips, core))
    slab_rows = slab.shape[0]
    earlier = jnp.arange(slab_rows)[:, None] < jnp.arange(slab_rows)[None, :]
    same = slab_owner[:, None] == slab_owner[None, :]
    ranks = jnp.sum((earlier & same).astype(jnp.int32), axis=0)
    owner_place = ring_place(slab_owner // cores, chips)
    seen = lax.rem(owner_place - place + chips, chips)
    slots = seen * seqs + lax.rem(slab_owner, cores) * seq_dev + ranks
    positive, candidate = [
        jnp.sum(
            (slots[picked][:, :, None] == jnp.arange(slab_rows)).astype(jnp.float32), axis=1
        )
        for picked in (cands[:, :1], cands)
    ]

    slab_wide = slab.astype(jnp.float32)
    logits = (
        sharpness / embedding * jnp.dot(unit, slab_wide.T, precision=lax.Precision.HIGHEST)
    )
    exponent = jnp.where(candidate > 0, jnp.exp(logits), 0.0)
    probs = exponent / jnp.sum(exponent, axis=-1, keepdims=True)
    logit_grad = probs - positive
    unit_grad = (
        sharpness / embedding * jnp.dot(logit_grad, slab_wide, precision=lax.Precision.HIGHEST)
    )
    inner = jnp.sum(whole * unit_grad, axis=-1, keepdims=True)
    pooled_grad = scale * unit_grad - whole * (scale * scale * scale) * inner / embedding
    pooled_grad = lax.dynamic_slice(pooled_grad, (0, core * half), (seqs, half))
    delta = (pooled_grad / counts[:, None])[:, None, :] * slope.reshape(seqs, length, half)
    delta = delta.astype(jnp.bfloat16).reshape(seqs * length, half)
    delta, weights = lax.optimization_barrier((delta, weights))
    copied = lax.ppermute(weights.astype(jnp.bfloat16), "grp", [(0, 1)])

    def term(offset, part, delta):
        return lax.dot_general(
            columns(offset, part),
            delta,
            (((0,), (0,)), ((), ())),
            preferred_element_type=jnp.float32,
        )

    if chips <= longest_ring:
        arrived = {}
        late = delta
        for step in range(chips // 2, 0, -1):
            for i, by in ((0, 1), (1, -1), (1, 1), (0, -1)):
                if step == chips // 2 and (i, by) not in ((0, 1), (1, -1)):
                    continue
                total = term(by * step, parts[i], delta)
                if (i, by) in arrived:
                    total = total + arrived[i, by].astype(jnp.float32)
                if step == 1 and i == 0:
                    total = after(copied, total)
                arrived[i, by] = along_ring(total.astype(jnp.bfloat16), by)
            if step == chips // 2:
                late = after(arrived[0, 1], delta)
        mine, other = [
            term(0, parts[i], late)
            + arrived[i, 1].astype(jnp.float32)
            + arrived[i, -1].astype(jnp.float32)
            for i in range(2)
        ]
    else:
        grad = lax.dot_general(
            normed, delta, (((0,), (0,)), ((), ())), preferred_element_type=jnp.float32
        )
        reduced = lax.psum_scatter(grad, "chip", scatter_dimension=0, tiled=True)
        mine, other = [lax.dynamic_slice(reduced, (i * rows, 0), (rows, half)) for i in parts]
    other = from_sibling(other)
    shard = in_core_order(mine, other, core, axis=1)
    row_square = jnp.mean(shard * shard, axis=1, keepdims=True)
    normalized = shard * lax.rsqrt(row_square + 1e-06)
    result = jnp.where(trainer, normalized, copied.astype(jnp.float32))
    return result[None]


def solution(mesh):
    groups, devices_fsdp = mesh.devices.shape
    finer = Mesh(
        mesh.devices.reshape(groups, devices_fsdp // cores, cores), ("grp", "chip", "core")
    )
    fsdp = ("chip", "core")
    placed = (
        P("grp", fsdp, None, None),
        P("grp", fsdp, None),
        P("grp", fsdp, None),
        P(),
        P(fsdp, None),
        P(),
    )
    return jax.shard_map(
        shards, mesh=finer, in_specs=placed, out_specs=P("grp", fsdp, None), check_vma=False
    )
```

```python
import functools

import jax
import jax.numpy as jnp
from jax import lax
from jax.experimental import pallas as pl
from jax.experimental.pallas import tpu as pltpu
from jax.sharding import Mesh, PartitionSpec as P

sharpness = 20.0
cores = 2
longest_ring = 16
vmem_limit = 60 << 20


def ring_order(chips):
    return list(range(0, chips, 2)) + list(range(1, chips, 2))[::-1]


def ring_place(chip, chips):
    return jnp.where(chip % 2 == 0, chip // 2, chips - 1 - chip // 2)


def ring_chip(place, chips):
    place = lax.rem(place + 2 * chips, chips)
    return jnp.where(place < chips // 2, 2 * place, 2 * (chips - 1 - place) + 1)


def along_ring(block, by):
    order = ring_order(lax.axis_size("chip"))
    pairs = [(chip, order[(i + by) % len(order)]) for i, chip in enumerate(order)]
    return lax.ppermute(block, "chip", pairs)


def after(first, block):
    return lax.optimization_barrier((first, block))[1]


def from_sibling(block):
    return lax.ppermute(block, "core", [(0, 1), (1, 0)])


def slab_blocks(stored, chips, core):
    order = ring_order(chips)
    kept = []
    for j in range(chips // cores):
        pairs = []
        for i, chip in enumerate(order):
            for c in range(cores):
                source = order[(i + j + c * (chips // cores)) % chips]
                pairs.append(((chips + source) * cores + c, chip * cores + c))
        kept.append(lax.ppermute(stored, ("grp", "chip", "core"), pairs))
    kept = jnp.concatenate(kept)
    other = from_sibling(kept)
    return [jnp.where(core == 0, kept, other), jnp.where(core == 0, other, kept)]


def in_core_order(mine, other, core, axis=0):
    return jnp.where(
        core == 0,
        jnp.concatenate([mine, other], axis=axis),
        jnp.concatenate([other, mine], axis=axis),
    )


def halves_kernel(core_ref, own_ref, other_ref, own_out, other_out):
    own_out[...] = own_ref[...].astype(jnp.bfloat16)
    other_out[...] = other_ref[...].astype(jnp.bfloat16)


def cut_halves(weights, core):
    rows, embedding = weights.shape
    half = embedding // cores
    tile = rows // 4 if rows % 64 == 0 else rows
    read = (tile, half)
    written = pl.BlockSpec((tile, half), lambda i, core: (i, 0))
    return pl.pallas_call(
        halves_kernel,
        grid_spec=pltpu.PrefetchScalarGridSpec(
            num_scalar_prefetch=1,
            grid=(rows // tile,),
            in_specs=[
                pl.BlockSpec(read, lambda i, core: (i, core[0])),
                pl.BlockSpec(read, lambda i, core: (i, 1 - core[0])),
            ],
            out_specs=[written, written],
        ),
        out_shape=[jax.ShapeDtypeStruct((rows, half), jnp.bfloat16)] * 2,
        compiler_params=pltpu.CompilerParams(vmem_limit_bytes=vmem_limit),
        cost_estimate=pl.CostEstimate(
            flops=0, bytes_accessed=6 * rows * embedding, transcendentals=0
        ),
    )(core[None].astype(jnp.int32), weights, weights)


def normalize_kernel(chunk, states_ref, gain_ref, *refs):
    out_ref = refs[-1]

    @pl.loop(0, states_ref.shape[1] // chunk)
    def _(i):
        at = pl.ds(pl.multiple_of(i * chunk, chunk), chunk)
        wide = states_ref[0, at, :].astype(jnp.float32)
        mean_square = jnp.mean(wide * wide, axis=-1, keepdims=True)
        wide = wide * lax.rsqrt(mean_square + 1e-05) * gain_ref[...]
        out_ref[at, :] = wide.astype(jnp.bfloat16)


def normalize(states, gain, part, filled=None):
    seqs, length, width = states.shape
    tokens = seqs * length
    in_specs = [
        pl.BlockSpec((1, length, width), lambda i: (i, 0, 0)),
        pl.BlockSpec((1, width), lambda i: (0, 0)),
    ]
    operands = [states, gain[None]]
    if filled is not None:
        in_specs.append(pl.BlockSpec(memory_space=pl.ANY))
        operands.append(filled)
    return pl.pallas_call(
        functools.partial(normalize_kernel, 16),
        grid=(seqs,),
        in_specs=in_specs,
        out_specs=pl.BlockSpec((length, width), lambda i: (part * seqs + i, 0)),
        out_shape=jax.ShapeDtypeStruct((cores * tokens, width), jnp.bfloat16),
        input_output_aliases={} if filled is None else {2: 0},
        compiler_params=pltpu.CompilerParams(vmem_limit_bytes=vmem_limit),
        cost_estimate=pl.CostEstimate(
            flops=6 * tokens * width, bytes_accessed=4 * tokens * width, transcendentals=tokens
        ),
    )(*operands)


def blocks_kernel(amount, has_total, last, length, offsets_ref, counts_ref, *refs):
    columns, blocks, rest = refs[:amount], refs[amount : 2 * amount], refs[2 * amount :]
    total = None
    for column, block in zip(columns, blocks):
        term = jnp.dot(column[...], block[...], preferred_element_type=jnp.float32)
        total = term if total is None else total + term
    if has_total:
        total = total + rest[0][...]
        rest = rest[1:]
    if not last:
        rest[0][...] = total
        return
    slope_ref, pooled_ref = rest
    active = jnp.tanh(total)
    seqs = active.shape[0] // length
    active = active.reshape(seqs, length, active.shape[1])
    for i in range(seqs):
        count = counts_ref[pl.program_id(0) * seqs + i]
        there = lax.broadcasted_iota(jnp.int32, active.shape[1:], 0) < count
        part = jnp.where(there, active[i], 0.0)
        pooled_ref[i] = jnp.sum(part, axis=0, keepdims=True)
        slope_ref[pl.ds(i * length, length), :] = jnp.where(there, 1.0 - part * part, 0.0)


def add_blocks(normed, offsets, blocks, total, counts, length, last):
    tokens = normed.shape[0]
    rows, half = blocks[0].shape
    amount = len(blocks)
    tile = 2 * length if tokens % (2 * length) == 0 else length
    in_specs = [
        pl.BlockSpec((tile, rows), lambda i, offsets, counts, b=b: (i, offsets[b]))
        for b in range(amount)
    ]
    in_specs += [pl.BlockSpec((rows, half), lambda i, offsets, counts: (0, 0))] * amount
    operands = [normed] * amount + list(blocks)
    whole = pl.BlockSpec((tile, half), lambda i, offsets, counts: (i, 0))
    if total is not None:
        in_specs.append(whole)
        operands.append(total)
    out_specs = whole
    out_shape = jax.ShapeDtypeStruct((tokens, half), jnp.float32)
    if last:
        out_specs = [whole, pl.BlockSpec((tile // length, 1, half), lambda i, offsets, counts: (i, 0, 0))]
        out_shape = [out_shape, jax.ShapeDtypeStruct((tokens // length, 1, half), jnp.float32)]
    return pl.pallas_call(
        functools.partial(blocks_kernel, amount, total is not None, last, length),
        grid_spec=pltpu.PrefetchScalarGridSpec(
            num_scalar_prefetch=2, grid=(tokens // tile,), in_specs=in_specs, out_specs=out_specs
        ),
        out_shape=out_shape,
        compiler_params=pltpu.CompilerParams(vmem_limit_bytes=vmem_limit),
        cost_estimate=pl.CostEstimate(
            flops=2 * tokens * rows * half * amount,
            bytes_accessed=2 * amount * rows * (tokens + half) + 8 * tokens * half,
            transcendentals=tokens * half if last else 0,
        ),
    )(offsets, counts, *operands)


def shards(token_states, token_ids, master, gain, cand_ids, slab_owner):
    trainer = lax.axis_index("grp") == 0
    chips = lax.axis_size("chip")
    chip = lax.axis_index("chip")
    core = lax.axis_index("core")
    place = ring_place(chip, chips)
    states = token_states[0]
    seq_dev, length, width = states.shape
    rows, embedding = master.shape[1:]
    half = embedding // cores
    seqs = cores * seq_dev

    weights = master[0]
    own, given = cut_halves(weights, core)
    sibling = from_sibling(given)

    normed = normalize(states, gain, 0)
    normed = normalize(from_sibling(states), gain, 1, normed)
    first_sent = along_ring(own, 1)
    ids, cand_ids = token_ids[0], after(first_sent, cand_ids)
    ids = jnp.concatenate([ids, cand_ids], axis=1)
    ids = jnp.concatenate([ids, from_sibling(ids)])
    lengths = jnp.sum((ids[:, :length] != 0).astype(jnp.int32), axis=1)
    counts = lengths.astype(jnp.float32)
    cands = ids[:, length:]

    def first_column(offset, part):
        return ring_chip(place + offset, chips) * cores + part

    def columns(offset, part):
        first = first_column(offset, part) * rows
        return lax.dynamic_slice(normed, (0, first), (seqs * length, rows))

    parts = (core, 1 - core)
    if chips <= longest_ring:
        moving = {(i, by): block for by in (1, -1) for i, block in enumerate((own, sibling))}
        total, first = None, None
        blocks, offsets = [own, sibling], [first_column(0, part) for part in parts]
        for step in range(1, chips // 2 + 1):
            last = step == chips // 2
            sent = [(0, 1), (1, -1)] if last else [(0, 1), (0, -1), (1, 1), (1, -1)]
            for i, by in sent:
                if (step, i, by) == (1, 0, 1):
                    moving[i, by] = first_sent
                else:
                    if last and i == 1:
                        moving[i, by] = after(first, moving[i, by])
                    elif step == 3 and i == 0:
                        moving[i, by] = after(normed, moving[i, by])
                    moving[i, by] = along_ring(moving[i, by], by)
                blocks.append(moving[i, by])
                offsets.append(first_column(-by * step, parts[i]))
            if step == 1:
                continue
            total = add_blocks(normed, jnp.stack(offsets), blocks, total, lengths, length, last)
            first = total if first is None else first
            blocks, offsets = [], []
        slope, pooled = total
        pooled = pooled[:, 0] / counts[:, None]
    else:
        both = in_core_order(own, sibling, core)
        gathered = lax.all_gather(both, "chip", axis=0, tiled=True)
        hidden = jnp.dot(normed, gathered, preferred_element_type=jnp.float32)
        active = jnp.tanh(hidden).reshape(seqs, length, half)
        there = jnp.arange(length)[None, :, None] < lengths[:, None, None]
        active = jnp.where(there, active, 0.0)
        pooled = jnp.sum(active, axis=1) / counts[:, None]
        slope = jnp.where(there, 1.0 - active * active, 0.0).reshape(seqs * length, half)

    pooled_other = from_sibling(pooled)
    pooled_other = jnp.concatenate([pooled_other[seq_dev:], pooled_other[:seq_dev]])
    whole = in_core_order(pooled, pooled_other, core, axis=1)
    pooled_square = jnp.mean(whole * whole, axis=-1, keepdims=True)
    scale = lax.rsqrt(pooled_square + 1e-06)
    unit = whole * scale
    stored = unit.astype(jnp.bfloat16)
    stored = in_core_order(stored[:seq_dev], stored[seq_dev:], core)

    slab = jnp.concatenate(slab_blocks(stored, chips, core))
    slab_rows = slab.shape[0]
    earlier = jnp.arange(slab_rows)[:, None] < jnp.arange(slab_rows)[None, :]
    same = slab_owner[:, None] == slab_owner[None, :]
    ranks = jnp.sum((earlier & same).astype(jnp.int32), axis=0)
    owner_place = ring_place(slab_owner // cores, chips)
    seen = lax.rem(owner_place - place + chips, chips)
    slots = seen * seqs + lax.rem(slab_owner, cores) * seq_dev + ranks
    positive, candidate = [
        jnp.sum(
            (slots[picked][:, :, None] == jnp.arange(slab_rows)).astype(jnp.float32), axis=1
        )
        for picked in (cands[:, :1], cands)
    ]

    slab_wide = slab.astype(jnp.float32)
    logits = (
        sharpness / embedding * jnp.dot(unit, slab_wide.T, precision=lax.Precision.HIGHEST)
    )
    exponent = jnp.where(candidate > 0, jnp.exp(logits), 0.0)
    probs = exponent / jnp.sum(exponent, axis=-1, keepdims=True)
    logit_grad = probs - positive
    unit_grad = (
        sharpness / embedding * jnp.dot(logit_grad, slab_wide, precision=lax.Precision.HIGHEST)
    )
    inner = jnp.sum(whole * unit_grad, axis=-1, keepdims=True)
    pooled_grad = scale * unit_grad - whole * (scale * scale * scale) * inner / embedding
    pooled_grad = lax.dynamic_slice(pooled_grad, (0, core * half), (seqs, half))
    delta = (pooled_grad / counts[:, None])[:, None, :] * slope.reshape(seqs, length, half)
    delta = delta.astype(jnp.bfloat16).reshape(seqs * length, half)
    delta, weights = lax.optimization_barrier((delta, weights))
    copied = lax.ppermute(weights.astype(jnp.bfloat16), "grp", [(0, 1)])

    def term(offset, part, delta):
        return lax.dot_general(
            columns(offset, part),
            delta,
            (((0,), (0,)), ((), ())),
            preferred_element_type=jnp.float32,
        )

    if chips <= longest_ring:
        arrived = {}
        late = delta
        for step in range(chips // 2, 0, -1):
            for i, by in ((0, 1), (1, -1), (1, 1), (0, -1)):
                if step == chips // 2 and (i, by) not in ((0, 1), (1, -1)):
                    continue
                total = term(by * step, parts[i], delta)
                if (i, by) in arrived:
                    total = total + arrived[i, by].astype(jnp.float32)
                if step == 1 and i == 0:
                    total = after(copied, total)
                arrived[i, by] = along_ring(total.astype(jnp.bfloat16), by)
            if step == chips // 2:
                late = after(arrived[0, 1], delta)
        mine, other = [
            term(0, parts[i], late)
            + arrived[i, 1].astype(jnp.float32)
            + arrived[i, -1].astype(jnp.float32)
            for i in range(2)
        ]
    else:
        grad = lax.dot_general(
            normed, delta, (((0,), (0,)), ((), ())), preferred_element_type=jnp.float32
        )
        reduced = lax.psum_scatter(grad, "chip", scatter_dimension=0, tiled=True)
        mine, other = [lax.dynamic_slice(reduced, (i * rows, 0), (rows, half)) for i in parts]
    other = from_sibling(other)
    shard = in_core_order(mine, other, core, axis=1)
    row_square = jnp.mean(shard * shard, axis=1, keepdims=True)
    normalized = shard * lax.rsqrt(row_square + 1e-06)
    result = jnp.where(trainer, normalized, copied.astype(jnp.float32))
    return result[None]


def solution(mesh):
    groups, devices_fsdp = mesh.devices.shape
    finer = Mesh(
        mesh.devices.reshape(groups, devices_fsdp // cores, cores), ("grp", "chip", "core")
    )
    fsdp = ("chip", "core")
    placed = (
        P("grp", fsdp, None, None),
        P("grp", fsdp, None),
        P("grp", fsdp, None),
        P(),
        P(fsdp, None),
        P(),
    )
    return jax.shard_map(
        shards, mesh=finer, in_specs=placed, out_specs=P("grp", fsdp, None), check_vma=False
    )
```

```python
import functools

import jax
import jax.numpy as jnp
from jax import lax
from jax.experimental import pallas as pl
from jax.experimental.pallas import tpu as pltpu
from jax.sharding import Mesh, PartitionSpec as P

sharpness = 20.0
cores = 2
longest_ring = 16
vmem_limit = 63 << 20


def ring_order(chips):
    return list(range(0, chips, 2)) + list(range(1, chips, 2))[::-1]


def ring_place(chip, chips):
    return jnp.where(chip % 2 == 0, chip // 2, chips - 1 - chip // 2)


def ring_chip(place, chips):
    place = lax.rem(place + 2 * chips, chips)
    return jnp.where(place < chips // 2, 2 * place, 2 * (chips - 1 - place) + 1)


def along_ring(block, by):
    order = ring_order(lax.axis_size("chip"))
    pairs = [(chip, order[(i + by) % len(order)]) for i, chip in enumerate(order)]
    return lax.ppermute(block, "chip", pairs)


def after(first, block):
    return lax.optimization_barrier((first, block))[1]


def from_sibling(block):
    return lax.ppermute(block, "core", [(0, 1), (1, 0)])


def slab_blocks(stored, chips, core):
    order = ring_order(chips)
    kept = []
    for j in range(chips // cores):
        pairs = []
        for i, chip in enumerate(order):
            for c in range(cores):
                source = order[(i + j + c * (chips // cores)) % chips]
                pairs.append(((chips + source) * cores + c, chip * cores + c))
        kept.append(lax.ppermute(stored, ("grp", "chip", "core"), pairs))
    kept = jnp.concatenate(kept)
    other = from_sibling(kept)
    return [jnp.where(core == 0, kept, other), jnp.where(core == 0, other, kept)]


def in_core_order(mine, other, core, axis=0):
    return jnp.where(
        core == 0,
        jnp.concatenate([mine, other], axis=axis),
        jnp.concatenate([other, mine], axis=axis),
    )


def normalize_kernel(chunk, states_ref, gain_ref, *refs):
    out_ref = refs[-1]

    @pl.loop(0, states_ref.shape[0] // chunk)
    def _(i):
        at = pl.ds(pl.multiple_of(i * chunk, chunk), chunk)
        wide = states_ref[at, :].astype(jnp.float32)
        mean_square = jnp.mean(wide * wide, axis=-1, keepdims=True)
        wide = wide * lax.rsqrt(mean_square + 1e-05) * gain_ref[...]
        out_ref[at, :] = wide.astype(jnp.bfloat16)


def normalize(states, gain, part, filled=None):
    seqs, length, width = states.shape
    tokens = seqs * length
    tile = 32 if length % 32 == 0 else length
    steps = tokens // tile
    in_specs = [
        pl.BlockSpec((tile, width), lambda i: (i, 0)),
        pl.BlockSpec((1, width), lambda i: (0, 0)),
    ]
    operands = [states.reshape(tokens, width), gain[None]]
    if filled is not None:
        in_specs.append(pl.BlockSpec(memory_space=pl.ANY))
        operands.append(filled)
    return pl.pallas_call(
        functools.partial(normalize_kernel, 16),
        grid=(steps,),
        in_specs=in_specs,
        out_specs=pl.BlockSpec((tile, width), lambda i: (part * steps + i, 0)),
        out_shape=jax.ShapeDtypeStruct((cores * tokens, width), jnp.bfloat16),
        input_output_aliases={} if filled is None else {2: 0},
        compiler_params=pltpu.CompilerParams(vmem_limit_bytes=vmem_limit),
        cost_estimate=pl.CostEstimate(
            flops=6 * tokens * width, bytes_accessed=4 * tokens * width, transcendentals=tokens
        ),
    )(*operands)


def blocks_kernel(sources, chips, has_total, last, where_ref, counts_ref, normed_ref, *refs):
    blocks, rest = refs[: len(sources)], refs[len(sources) :]
    rows = blocks[0].shape[0]
    place, core = where_ref[0], where_ref[1]
    total = None
    for (offset, part), block in zip(sources, blocks):
        part = core if part == 0 else 1 - core
        first = (ring_chip(place + offset, chips) * cores + part) * rows
        columns = normed_ref[:, pl.ds(pl.multiple_of(first, rows), rows)]
        term = jnp.dot(columns, block[...], preferred_element_type=jnp.float32)
        total = term if total is None else total + term
    if has_total:
        total = total + rest[0][...]
        rest = rest[1:]
    if not last:
        rest[0][...] = total
        return
    slope_ref, pooled_ref = rest
    there = lax.broadcasted_iota(jnp.int32, total.shape, 0) < counts_ref[pl.program_id(0)]
    active = jnp.where(there, jnp.tanh(total), 0.0)
    pooled_ref[0] = jnp.sum(active, axis=0, keepdims=True)
    slope_ref[...] = jnp.where(there, 1.0 - active * active, 0.0)


def add_blocks(normed, where, sources, blocks, total, counts, chips, length, last):
    tokens, width = normed.shape
    rows, half = blocks[0].shape
    whole = pl.BlockSpec((length, half), lambda i, where, counts: (i, 0))
    in_specs = [pl.BlockSpec((length, width), lambda i, where, counts: (i, 0))]
    in_specs += [pl.BlockSpec((rows, half), lambda i, where, counts: (0, 0))] * len(blocks)
    operands = [normed] + list(blocks)
    if total is not None:
        in_specs.append(whole)
        operands.append(total)
    out_specs = whole
    out_shape = jax.ShapeDtypeStruct((tokens, half), jnp.float32)
    if last:
        out_specs = [whole, pl.BlockSpec((1, 1, half), lambda i, where, counts: (i, 0, 0))]
        out_shape = [out_shape, jax.ShapeDtypeStruct((tokens // length, 1, half), jnp.float32)]
    return pl.pallas_call(
        functools.partial(blocks_kernel, sources, chips, total is not None, last),
        grid_spec=pltpu.PrefetchScalarGridSpec(
            num_scalar_prefetch=2, grid=(tokens // length,), in_specs=in_specs, out_specs=out_specs
        ),
        out_shape=out_shape,
        compiler_params=pltpu.CompilerParams(vmem_limit_bytes=vmem_limit),
        cost_estimate=pl.CostEstimate(
            flops=2 * tokens * rows * half * len(blocks),
            bytes_accessed=2 * tokens * width + 2 * len(blocks) * rows * half + 8 * tokens * half,
            transcendentals=tokens * half if last else 0,
        ),
    )(where, counts, *operands)


def shards(token_states, token_ids, master, gain, cand_ids, slab_owner):
    trainer = lax.axis_index("grp") == 0
    chips = lax.axis_size("chip")
    chip = lax.axis_index("chip")
    core = lax.axis_index("core")
    place = ring_place(chip, chips)
    states = token_states[0]
    seq_dev, length, width = states.shape
    rows, embedding = master.shape[1:]
    half = embedding // cores
    seqs = cores * seq_dev

    weights = master[0]
    own = lax.dynamic_slice(weights, (0, core * half), (rows, half)).astype(jnp.bfloat16)
    given = lax.dynamic_slice(weights, (0, (1 - core) * half), (rows, half))
    given = given.astype(jnp.bfloat16)
    sibling = from_sibling(given)

    normed = normalize(states, gain, 0)
    normed = normalize(from_sibling(states), gain, 1, normed)
    first_sent = along_ring(own, 1)
    ids, cand_ids = token_ids[0], after(first_sent, cand_ids)
    ids = jnp.concatenate([ids, cand_ids], axis=1)
    ids = jnp.concatenate([ids, from_sibling(ids)])
    lengths = jnp.sum((ids[:, :length] != 0).astype(jnp.int32), axis=1)
    counts = lengths.astype(jnp.float32)
    cands = ids[:, length:]

    def columns(offset, part):
        first = (ring_chip(place + offset, chips) * cores + part) * rows
        return lax.dynamic_slice(normed, (0, first), (seqs * length, rows))

    parts = (core, 1 - core)
    if chips <= longest_ring:
        moving = {(i, by): block for by in (1, -1) for i, block in enumerate((own, sibling))}
        total, first = None, None
        where = jnp.stack([place, core]).astype(jnp.int32)
        blocks, sources = [own, sibling], [(0, 0), (0, 1)]
        for step in range(1, chips // 2 + 1):
            last = step == chips // 2
            sent = [(0, 1), (1, -1)] if last else [(0, 1), (0, -1), (1, 1), (1, -1)]
            for i, by in sent:
                if (step, i, by) == (1, 0, 1):
                    moving[i, by] = first_sent
                else:
                    if last and i == 1 and first is not None:
                        moving[i, by] = after(first, moving[i, by])
                    elif step == 3 and i == 0:
                        moving[i, by] = after(normed, moving[i, by])
                    moving[i, by] = along_ring(moving[i, by], by)
                blocks.append(moving[i, by])
                sources.append((-by * step, i))
            if last or step == chips // 2 - 2:
                total = add_blocks(
                    normed, where, sources, blocks, total, lengths, chips, length, last
                )
                first = total
                blocks, sources = [], []
        slope, pooled = total
        pooled = pooled[:, 0] / counts[:, None]
    else:
        both = in_core_order(own, sibling, core)
        gathered = lax.all_gather(both, "chip", axis=0, tiled=True)
        hidden = jnp.dot(normed, gathered, preferred_element_type=jnp.float32)
        active = jnp.tanh(hidden).reshape(seqs, length, half)
        there = jnp.arange(length)[None, :, None] < lengths[:, None, None]
        active = jnp.where(there, active, 0.0)
        pooled = jnp.sum(active, axis=1) / counts[:, None]
        slope = jnp.where(there, 1.0 - active * active, 0.0).reshape(seqs * length, half)

    pooled_other = from_sibling(pooled)
    pooled_other = jnp.concatenate([pooled_other[seq_dev:], pooled_other[:seq_dev]])
    whole = in_core_order(pooled, pooled_other, core, axis=1)
    pooled_square = jnp.mean(whole * whole, axis=-1, keepdims=True)
    scale = lax.rsqrt(pooled_square + 1e-06)
    unit = whole * scale
    stored = unit.astype(jnp.bfloat16)
    stored = in_core_order(stored[:seq_dev], stored[seq_dev:], core)

    slab = jnp.concatenate(slab_blocks(stored, chips, core))
    slab_rows = slab.shape[0]
    earlier = jnp.arange(slab_rows)[:, None] < jnp.arange(slab_rows)[None, :]
    same = slab_owner[:, None] == slab_owner[None, :]
    ranks = jnp.sum((earlier & same).astype(jnp.int32), axis=0)
    owner_place = ring_place(slab_owner // cores, chips)
    seen = lax.rem(owner_place - place + chips, chips)
    slots = seen * seqs + lax.rem(slab_owner, cores) * seq_dev + ranks
    positive, candidate = [
        jnp.sum(
            (slots[picked][:, :, None] == jnp.arange(slab_rows)).astype(jnp.float32), axis=1
        )
        for picked in (cands[:, :1], cands)
    ]

    slab_wide = slab.astype(jnp.float32)
    logits = (
        sharpness / embedding * jnp.dot(unit, slab_wide.T, precision=lax.Precision.HIGHEST)
    )
    exponent = jnp.where(candidate > 0, jnp.exp(logits), 0.0)
    probs = exponent / jnp.sum(exponent, axis=-1, keepdims=True)
    logit_grad = probs - positive
    unit_grad = (
        sharpness / embedding * jnp.dot(logit_grad, slab_wide, precision=lax.Precision.HIGHEST)
    )
    inner = jnp.sum(whole * unit_grad, axis=-1, keepdims=True)
    pooled_grad = scale * unit_grad - whole * (scale * scale * scale) * inner / embedding
    pooled_grad = lax.dynamic_slice(pooled_grad, (0, core * half), (seqs, half))
    delta = (pooled_grad / counts[:, None])[:, None, :] * slope.reshape(seqs, length, half)
    delta = delta.astype(jnp.bfloat16).reshape(seqs * length, half)
    delta, weights = lax.optimization_barrier((delta, weights))
    copied = lax.ppermute(weights.astype(jnp.bfloat16), "grp", [(0, 1)])

    def term(offset, part, delta):
        return lax.dot_general(
            columns(offset, part),
            delta,
            (((0,), (0,)), ((), ())),
            preferred_element_type=jnp.float32,
        )

    if chips <= longest_ring:
        arrived = {}
        late = delta
        for step in range(chips // 2, 0, -1):
            for i, by in ((0, 1), (1, -1), (1, 1), (0, -1)):
                if step == chips // 2 and (i, by) not in ((0, 1), (1, -1)):
                    continue
                total = term(by * step, parts[i], delta)
                if (i, by) in arrived:
                    total = total + arrived[i, by].astype(jnp.float32)
                if step == 1 and i == 0:
                    total = after(copied, total)
                arrived[i, by] = along_ring(total.astype(jnp.bfloat16), by)
            if step == chips // 2:
                late = after(arrived[0, 1], delta)
        mine, other = [
            term(0, parts[i], late)
            + arrived[i, 1].astype(jnp.float32)
            + arrived[i, -1].astype(jnp.float32)
            for i in range(2)
        ]
    else:
        grad = lax.dot_general(
            normed, delta, (((0,), (0,)), ((), ())), preferred_element_type=jnp.float32
        )
        reduced = lax.psum_scatter(grad, "chip", scatter_dimension=0, tiled=True)
        mine, other = [lax.dynamic_slice(reduced, (i * rows, 0), (rows, half)) for i in parts]
    other = from_sibling(other)
    shard = in_core_order(mine, other, core, axis=1)
    row_square = jnp.mean(shard * shard, axis=1, keepdims=True)
    normalized = shard * lax.rsqrt(row_square + 1e-06)
    result = jnp.where(trainer, normalized, copied.astype(jnp.float32))
    return result[None]


def solution(mesh):
    groups, devices_fsdp = mesh.devices.shape
    finer = Mesh(
        mesh.devices.reshape(groups, devices_fsdp // cores, cores), ("grp", "chip", "core")
    )
    fsdp = ("chip", "core")
    placed = (
        P("grp", fsdp, None, None),
        P("grp", fsdp, None),
        P("grp", fsdp, None),
        P(),
        P(fsdp, None),
        P(),
    )
    return jax.shard_map(
        shards, mesh=finer, in_specs=placed, out_specs=P("grp", fsdp, None), check_vma=False
    )
```

```python
import functools

import jax
import jax.numpy as jnp
from jax import lax
from jax.experimental import pallas as pl
from jax.experimental.pallas import tpu as pltpu
from jax.sharding import Mesh, PartitionSpec as P

sharpness = 20.0
cores = 2
longest_ring = 16
vmem_limit = 20 << 20


def ring_order(chips):
    return list(range(0, chips, 2)) + list(range(1, chips, 2))[::-1]


def ring_place(chip, chips):
    return jnp.where(chip % 2 == 0, chip // 2, chips - 1 - chip // 2)


def ring_chip(place, chips):
    place = lax.rem(place + 2 * chips, chips)
    return jnp.where(place < chips // 2, 2 * place, 2 * (chips - 1 - place) + 1)


def along_ring(block, by):
    order = ring_order(lax.axis_size("chip"))
    pairs = [(chip, order[(i + by) % len(order)]) for i, chip in enumerate(order)]
    return lax.ppermute(block, "chip", pairs)


def after(first, block):
    return lax.optimization_barrier((first, block))[1]


def from_sibling(block):
    return lax.ppermute(block, "core", [(0, 1), (1, 0)])


def slab_blocks(stored, chips, core):
    order = ring_order(chips)
    kept = []
    for j in range(chips // cores):
        pairs = []
        for i, chip in enumerate(order):
            for c in range(cores):
                source = order[(i + j + c * (chips // cores)) % chips]
                pairs.append(((chips + source) * cores + c, chip * cores + c))
        kept.append(lax.ppermute(stored, ("grp", "chip", "core"), pairs))
    kept = jnp.concatenate(kept)
    other = from_sibling(kept)
    return [jnp.where(core == 0, kept, other), jnp.where(core == 0, other, kept)]


def in_core_order(mine, other, core, axis=0):
    return jnp.where(
        core == 0,
        jnp.concatenate([mine, other], axis=axis),
        jnp.concatenate([other, mine], axis=axis),
    )


def normalize_kernel(chunk, split, *refs):
    states_refs, gain_ref, out_ref = refs[:split], refs[split], refs[-1]

    def run(states_ref):
        @pl.loop(0, states_ref.shape[1] // chunk)
        def _(i):
            at = pl.ds(pl.multiple_of(i * chunk, chunk), chunk)
            wide = states_ref[0, at, :].astype(jnp.float32)
            mean_square = jnp.mean(wide * wide, axis=-1, keepdims=True)
            wide = wide * lax.rsqrt(mean_square + 1e-05) * gain_ref[...]
            out_ref[at, :] = wide.astype(jnp.bfloat16)

    if split == 1:
        run(states_refs[0])
        return
    for part, states_ref in enumerate(states_refs):
        pl.when(pl.program_id(0) == part)(functools.partial(run, states_ref))


def normalize(parts, gain, place, filled=None):
    length, width = parts[0].shape[1:]
    split = len(parts)
    seqs = parts[0].shape[0] if split == 1 else split
    tokens = seqs * length
    block = (1, length, width)
    if split == 1:
        in_specs = [pl.BlockSpec(block, lambda i: (i, 0, 0))]
    else:
        in_specs = [pl.BlockSpec(block, lambda i: (0, 0, 0))] * split
    in_specs.append(pl.BlockSpec((1, width), lambda i: (0, 0)))
    operands = [*parts, gain[None]]
    if filled is not None:
        in_specs.append(pl.BlockSpec(memory_space=pl.ANY))
        operands.append(filled)
    return pl.pallas_call(
        functools.partial(normalize_kernel, 16, split),
        grid=(seqs,),
        in_specs=in_specs,
        out_specs=pl.BlockSpec((length, width), lambda i: (place * seqs + i, 0)),
        out_shape=jax.ShapeDtypeStruct((cores * tokens, width), jnp.bfloat16),
        input_output_aliases={} if filled is None else {len(operands) - 1: 0},
        compiler_params=pltpu.CompilerParams(vmem_limit_bytes=vmem_limit),
        cost_estimate=pl.CostEstimate(
            flops=6 * tokens * width, bytes_accessed=4 * tokens * width, transcendentals=tokens
        ),
    )(*operands)


def shards(token_states, token_ids, master, gain, cand_ids, slab_owner):
    trainer = lax.axis_index("grp") == 0
    chips = lax.axis_size("chip")
    chip = lax.axis_index("chip")
    core = lax.axis_index("core")
    place = ring_place(chip, chips)
    states = token_states[0]
    seq_dev, length, width = states.shape
    rows, embedding = master.shape[1:]
    half = embedding // cores
    seqs = cores * seq_dev

    weights = master[0]
    own = lax.dynamic_slice(weights, (0, core * half), (rows, half)).astype(jnp.bfloat16)
    given = lax.dynamic_slice(weights, (0, (1 - core) * half), (rows, half))
    given = given.astype(jnp.bfloat16)
    sibling = from_sibling(given)

    normed = normalize([states], gain, 0)
    other_states = [from_sibling(states[i : i + 1]) for i in range(seq_dev)]
    first_sent = along_ring(own, 1)
    ids, cand_ids = token_ids[0], after(first_sent, cand_ids)
    ids = jnp.concatenate([ids, cand_ids], axis=1)
    ids = jnp.concatenate([ids, from_sibling(ids)])
    lengths = jnp.sum((ids[:, :length] != 0).astype(jnp.int32), axis=1)
    counts = lengths.astype(jnp.float32)
    cands = ids[:, length:]

    def columns(offset, part):
        first = (ring_chip(place + offset, chips) * cores + part) * rows
        return lax.dynamic_slice(normed, (0, first), (seqs * length, rows))

    parts = (core, 1 - core)
    if chips <= longest_ring:
        moving = {(i, by): block for by in (1, -1) for i, block in enumerate((own, sibling))}
        total, first = None, None
        waiting = [(0, parts[0], own), (0, parts[1], sibling)]
        for step in range(1, chips // 2 + 1):
            last = step == chips // 2
            sent = [(0, 1), (0, -1), (1, 1), (1, -1)]
            for i, by in [(0, 1), (1, -1)] if last else sent:
                if (step, i, by) == (1, 0, 1):
                    moving[i, by] = first_sent
                else:
                    if last and step > 2:
                        moving[i, by] = after(normed if i == 0 else first, moving[i, by])
                    moving[i, by] = along_ring(moving[i, by], by)
                waiting.append((-by * step, parts[i], moving[i, by]))
            if step == min(2, chips // 2):
                for key in sent:
                    other_states[0] = after(moving[key], other_states[0])
                normed = normalize(other_states, gain, 1, normed)
            if step < min(2, chips // 2):
                continue
            for offset, part, block in waiting:
                term = jnp.dot(columns(offset, part), block, preferred_element_type=jnp.float32)
                total = term if total is None else total + term
                if first is None and abs(offset) == 1 and part is parts[1]:
                    first = total
            waiting = []
        active = jnp.tanh(total).reshape(seqs, length, half)
    else:
        normed = normalize(other_states, gain, 1, normed)
        both = in_core_order(own, sibling, core)
        gathered = lax.all_gather(both, "chip", axis=0, tiled=True)
        hidden = jnp.dot(normed, gathered, preferred_element_type=jnp.float32)
        active = jnp.tanh(hidden).reshape(seqs, length, half)

    there = jnp.arange(length)[None, :, None] < lengths[:, None, None]
    pooled = jnp.sum(jnp.where(there, active, 0.0), axis=1) / counts[:, None]
    pooled_other = from_sibling(pooled)
    pooled_other = jnp.concatenate([pooled_other[seq_dev:], pooled_other[:seq_dev]])
    whole = in_core_order(pooled, pooled_other, core, axis=1)
    pooled_square = jnp.mean(whole * whole, axis=-1, keepdims=True)
    scale = lax.rsqrt(pooled_square + 1e-06)
    unit = whole * scale
    stored = unit.astype(jnp.bfloat16)
    stored = in_core_order(stored[:seq_dev], stored[seq_dev:], core)

    cut = {}
    if chips <= longest_ring:
        steps = [(chips // 2, 0, 1), (chips // 2, 1, -1), (chips // 2 - 1, 1, 1)]
        steps += [(chips // 2 - 1, 0, -1)]
        cut = {(by * step, i): columns(by * step, parts[i]) for step, i, by in steps}
        stored, *cuts = lax.optimization_barrier([stored, *cut.values()])
        cut = dict(zip(cut, cuts))
    slab = jnp.concatenate(slab_blocks(stored, chips, core))
    slab_rows = slab.shape[0]
    earlier = jnp.arange(slab_rows)[:, None] < jnp.arange(slab_rows)[None, :]
    same = slab_owner[:, None] == slab_owner[None, :]
    ranks = jnp.sum((earlier & same).astype(jnp.int32), axis=0)
    owner_place = ring_place(slab_owner // cores, chips)
    seen = lax.rem(owner_place - place + chips, chips)
    slots = seen * seqs + lax.rem(slab_owner, cores) * seq_dev + ranks
    positive, candidate = [
        jnp.sum(
            (slots[picked][:, :, None] == jnp.arange(slab_rows)).astype(jnp.float32), axis=1
        )
        for picked in (cands[:, :1], cands)
    ]

    slab_wide = slab.astype(jnp.float32)
    logits = (
        sharpness / embedding * jnp.dot(unit, slab_wide.T, precision=lax.Precision.HIGHEST)
    )
    exponent = jnp.where(candidate > 0, jnp.exp(logits), 0.0)
    probs = exponent / jnp.sum(exponent, axis=-1, keepdims=True)
    logit_grad = probs - positive
    unit_grad = (
        sharpness / embedding * jnp.dot(logit_grad, slab_wide, precision=lax.Precision.HIGHEST)
    )
    inner = jnp.sum(whole * unit_grad, axis=-1, keepdims=True)
    pooled_grad = scale * unit_grad - whole * (scale * scale * scale) * inner / embedding
    pooled_grad = lax.dynamic_slice(pooled_grad, (0, core * half), (seqs, half))
    slope = jnp.where(there, 1.0 - active * active, 0.0)
    delta = (pooled_grad / counts[:, None])[:, None, :] * slope
    delta = delta.astype(jnp.bfloat16).reshape(seqs * length, half)
    delta, weights = lax.optimization_barrier((delta, weights))
    copied = lax.ppermute(weights.astype(jnp.bfloat16), "grp", [(0, 1)])

    def term(offset, i, delta):
        return lax.dot_general(
            cut[offset, i] if (offset, i) in cut else columns(offset, parts[i]),
            delta,
            (((0,), (0,)), ((), ())),
            preferred_element_type=jnp.float32,
        )

    if chips <= longest_ring:
        arrived = {}
        late = delta
        for step in range(chips // 2, 0, -1):
            for i, by in ((0, 1), (1, -1), (1, 1), (0, -1)):
                if step == chips // 2 and (i, by) not in ((0, 1), (1, -1)):
                    continue
                total = term(by * step, i, delta)
                if (i, by) in arrived:
                    total = total + arrived[i, by].astype(jnp.float32)
                if step == 1 and i == 0:
                    total = after(copied, total)
                arrived[i, by] = along_ring(total.astype(jnp.bfloat16), by)
            if step == chips // 2:
                late = after(arrived[0, 1], delta)
        mine, other = [
            term(0, i, late)
            + arrived[i, 1].astype(jnp.float32)
            + arrived[i, -1].astype(jnp.float32)
            for i in range(2)
        ]
    else:
        grad = lax.dot_general(
            normed, delta, (((0,), (0,)), ((), ())), preferred_element_type=jnp.float32
        )
        reduced = lax.psum_scatter(grad, "chip", scatter_dimension=0, tiled=True)
        mine, other = [lax.dynamic_slice(reduced, (i * rows, 0), (rows, half)) for i in parts]
    other = from_sibling(other)
    shard = in_core_order(mine, other, core, axis=1)
    row_square = jnp.mean(shard * shard, axis=1, keepdims=True)
    normalized = shard * lax.rsqrt(row_square + 1e-06)
    result = jnp.where(trainer, normalized, copied.astype(jnp.float32))
    return result[None]


def solution(mesh):
    groups, devices_fsdp = mesh.devices.shape
    finer = Mesh(
        mesh.devices.reshape(groups, devices_fsdp // cores, cores), ("grp", "chip", "core")
    )
    fsdp = ("chip", "core")
    placed = (
        P("grp", fsdp, None, None),
        P("grp", fsdp, None),
        P("grp", fsdp, None),
        P(),
        P(fsdp, None),
        P(),
    )
    return jax.shard_map(
        shards, mesh=finer, in_specs=placed, out_specs=P("grp", fsdp, None), check_vma=False
    )
```

```python
import functools

import jax
import jax.numpy as jnp
from jax import lax
from jax.experimental import pallas as pl
from jax.experimental.pallas import tpu as pltpu
from jax.sharding import Mesh, PartitionSpec as P

sharpness = 20.0
cores = 2
longest_ring = 16
vmem_limit = 20 << 20


def ring_order(chips):
    return list(range(0, chips, 2)) + list(range(1, chips, 2))[::-1]


def ring_place(chip, chips):
    return jnp.where(chip % 2 == 0, chip // 2, chips - 1 - chip // 2)


def ring_chip(place, chips):
    place = lax.rem(place + 2 * chips, chips)
    return jnp.where(place < chips // 2, 2 * place, 2 * (chips - 1 - place) + 1)


def along_ring(block, by):
    order = ring_order(lax.axis_size("chip"))
    pairs = [(chip, order[(i + by) % len(order)]) for i, chip in enumerate(order)]
    return lax.ppermute(block, "chip", pairs)


def after(first, block):
    return lax.optimization_barrier((first, block))[1]


def from_sibling(block):
    return lax.ppermute(block, "core", [(0, 1), (1, 0)])


def slab_blocks(stored, chips, core):
    order = ring_order(chips)
    kept = []
    for j in range(chips // cores):
        pairs = []
        for i, chip in enumerate(order):
            for c in range(cores):
                source = order[(i + j + c * (chips // cores)) % chips]
                pairs.append(((chips + source) * cores + c, chip * cores + c))
        kept.append(lax.ppermute(stored, ("grp", "chip", "core"), pairs))
    kept = jnp.concatenate(kept)
    other = from_sibling(kept)
    return [jnp.where(core == 0, kept, other), jnp.where(core == 0, other, kept)]


def in_core_order(mine, other, core, axis=0):
    return jnp.where(
        core == 0,
        jnp.concatenate([mine, other], axis=axis),
        jnp.concatenate([other, mine], axis=axis),
    )


def normalize_kernel(chunk, states_ref, gain_ref, *out_refs):
    def run(out_ref):
        @pl.loop(0, states_ref.shape[1] // chunk)
        def _(i):
            at = pl.ds(pl.multiple_of(i * chunk, chunk), chunk)
            wide = states_ref[0, at, :].astype(jnp.float32)
            mean_square = jnp.mean(wide * wide, axis=-1, keepdims=True)
            wide = wide * lax.rsqrt(mean_square + 1e-05) * gain_ref[...]
            out_ref[at, :] = wide.astype(jnp.bfloat16)

    for part, out_ref in enumerate(out_refs):
        pl.when(pl.program_id(0) == part)(functools.partial(run, out_ref))


def normalize(states, gain):
    seqs, length, width = states.shape
    tokens = seqs * length
    return pl.pallas_call(
        functools.partial(normalize_kernel, 16),
        grid=(seqs,),
        in_specs=[
            pl.BlockSpec((1, length, width), lambda i: (i, 0, 0)),
            pl.BlockSpec((1, width), lambda i: (0, 0)),
        ],
        out_specs=[pl.BlockSpec((length, width), lambda i: (0, 0))] * seqs,
        out_shape=[jax.ShapeDtypeStruct((length, width), jnp.bfloat16)] * seqs,
        compiler_params=pltpu.CompilerParams(vmem_limit_bytes=vmem_limit),
        cost_estimate=pl.CostEstimate(
            flops=6 * tokens * width, bytes_accessed=4 * tokens * width, transcendentals=tokens
        ),
    )(states, gain[None])


def shards(token_states, token_ids, master, gain, cand_ids, slab_owner):
    trainer = lax.axis_index("grp") == 0
    chips = lax.axis_size("chip")
    chip = lax.axis_index("chip")
    core = lax.axis_index("core")
    place = ring_place(chip, chips)
    states = token_states[0]
    seq_dev, length, width = states.shape
    rows, embedding = master.shape[1:]
    half = embedding // cores
    seqs = cores * seq_dev

    weights = master[0]
    own = lax.dynamic_slice(weights, (0, core * half), (rows, half)).astype(jnp.bfloat16)
    given = lax.dynamic_slice(weights, (0, (1 - core) * half), (rows, half))
    given = given.astype(jnp.bfloat16)
    sibling = from_sibling(given)

    normed = list(normalize(after(sibling, states), gain))
    normed = jnp.concatenate(normed + [from_sibling(part) for part in normed])
    first_sent = along_ring(own, 1)
    ids, cand_ids = token_ids[0], after(first_sent, cand_ids)
    ids = jnp.concatenate([ids, cand_ids], axis=1)
    ids = jnp.concatenate([ids, from_sibling(ids)])
    lengths = jnp.sum((ids[:, :length] != 0).astype(jnp.int32), axis=1)
    counts = lengths.astype(jnp.float32)
    cands = ids[:, length:]

    def columns(offset, part):
        first = (ring_chip(place + offset, chips) * cores + part) * rows
        return lax.dynamic_slice(normed, (0, first), (seqs * length, rows))

    def product(offset, part, block):
        return jnp.dot(columns(offset, part), block, preferred_element_type=jnp.float32)

    parts = (core, 1 - core)
    if chips <= longest_ring:
        moving = {(i, by): block for by in (1, -1) for i, block in enumerate((own, sibling))}
        total = product(0, parts[0], own) + product(0, parts[1], sibling)
        first = None
        for step in range(1, chips // 2 + 1):
            last = step == chips // 2
            sent = [(0, 1), (0, -1), (1, 1), (1, -1)]
            for i, by in [(0, 1), (1, -1)] if last else sent:
                if (step, i, by) == (1, 0, 1):
                    moving[i, by] = first_sent
                else:
                    if last and i == 1 and first is not None:
                        moving[i, by] = after(first, moving[i, by])
                    moving[i, by] = along_ring(moving[i, by], by)
                total = total + product(-by * step, parts[i], moving[i, by])
            first = total if first is None else first
        active = jnp.tanh(total).reshape(seqs, length, half)
    else:
        both = in_core_order(own, sibling, core)
        gathered = lax.all_gather(both, "chip", axis=0, tiled=True)
        hidden = jnp.dot(normed, gathered, preferred_element_type=jnp.float32)
        active = jnp.tanh(hidden).reshape(seqs, length, half)

    there = jnp.arange(length)[None, :, None] < lengths[:, None, None]
    pooled = jnp.sum(jnp.where(there, active, 0.0), axis=1) / counts[:, None]
    pooled_other = from_sibling(pooled)
    pooled_other = jnp.concatenate([pooled_other[seq_dev:], pooled_other[:seq_dev]])
    whole = in_core_order(pooled, pooled_other, core, axis=1)
    pooled_square = jnp.mean(whole * whole, axis=-1, keepdims=True)
    scale = lax.rsqrt(pooled_square + 1e-06)
    unit = whole * scale
    stored = unit.astype(jnp.bfloat16)
    stored = in_core_order(stored[:seq_dev], stored[seq_dev:], core)

    cut = {}
    if chips <= longest_ring:
        steps = [(chips // 2, 0, 1), (chips // 2, 1, -1), (chips // 2 - 1, 1, 1)]
        steps += [(chips // 2 - 1, 0, -1)]
        cut = {(by * step, i): columns(by * step, parts[i]) for step, i, by in steps}
        stored, *cuts = lax.optimization_barrier([stored, *cut.values()])
        cut = dict(zip(cut, cuts))
    slab = jnp.concatenate(slab_blocks(stored, chips, core))
    slab_rows = slab.shape[0]
    earlier = jnp.arange(slab_rows)[:, None] < jnp.arange(slab_rows)[None, :]
    same = slab_owner[:, None] == slab_owner[None, :]
    ranks = jnp.sum((earlier & same).astype(jnp.int32), axis=0)
    owner_place = ring_place(slab_owner // cores, chips)
    seen = lax.rem(owner_place - place + chips, chips)
    slots = seen * seqs + lax.rem(slab_owner, cores) * seq_dev + ranks
    positive, candidate = [
        jnp.sum(
            (slots[picked][:, :, None] == jnp.arange(slab_rows)).astype(jnp.float32), axis=1
        )
        for picked in (cands[:, :1], cands)
    ]

    slab_wide = slab.astype(jnp.float32)
    logits = (
        sharpness / embedding * jnp.dot(unit, slab_wide.T, precision=lax.Precision.HIGHEST)
    )
    exponent = jnp.where(candidate > 0, jnp.exp(logits), 0.0)
    probs = exponent / jnp.sum(exponent, axis=-1, keepdims=True)
    logit_grad = probs - positive
    unit_grad = (
        sharpness / embedding * jnp.dot(logit_grad, slab_wide, precision=lax.Precision.HIGHEST)
    )
    inner = jnp.sum(whole * unit_grad, axis=-1, keepdims=True)
    pooled_grad = scale * unit_grad - whole * (scale * scale * scale) * inner / embedding
    pooled_grad = lax.dynamic_slice(pooled_grad, (0, core * half), (seqs, half))
    slope = jnp.where(there, 1.0 - active * active, 0.0)
    delta = (pooled_grad / counts[:, None])[:, None, :] * slope
    delta = delta.astype(jnp.bfloat16).reshape(seqs * length, half)
    delta, weights = lax.optimization_barrier((delta, weights))
    copied = lax.ppermute(weights.astype(jnp.bfloat16), "grp", [(0, 1)])

    def term(offset, i, delta):
        return lax.dot_general(
            cut[offset, i] if (offset, i) in cut else columns(offset, parts[i]),
            delta,
            (((0,), (0,)), ((), ())),
            preferred_element_type=jnp.float32,
        )

    if chips <= longest_ring:
        arrived = {}
        late = delta
        for step in range(chips // 2, 0, -1):
            for i, by in ((0, 1), (1, -1), (1, 1), (0, -1)):
                if step == chips // 2 and (i, by) not in ((0, 1), (1, -1)):
                    continue
                total = term(by * step, i, delta)
                if (i, by) in arrived:
                    total = total + arrived[i, by].astype(jnp.float32)
                if step == 1 and i == 0:
                    total = after(copied, total)
                arrived[i, by] = along_ring(total.astype(jnp.bfloat16), by)
            if step == chips // 2:
                late = after(arrived[0, 1], delta)
        mine, other = [
            term(0, i, late)
            + arrived[i, 1].astype(jnp.float32)
            + arrived[i, -1].astype(jnp.float32)
            for i in range(2)
        ]
    else:
        grad = lax.dot_general(
            normed, delta, (((0,), (0,)), ((), ())), preferred_element_type=jnp.float32
        )
        reduced = lax.psum_scatter(grad, "chip", scatter_dimension=0, tiled=True)
        mine, other = [lax.dynamic_slice(reduced, (i * rows, 0), (rows, half)) for i in parts]
    other = from_sibling(other)
    shard = in_core_order(mine, other, core, axis=1)
    row_square = jnp.mean(shard * shard, axis=1, keepdims=True)
    normalized = shard * lax.rsqrt(row_square + 1e-06)
    result = jnp.where(trainer, normalized, copied.astype(jnp.float32))
    return result[None]


def solution(mesh):
    groups, devices_fsdp = mesh.devices.shape
    finer = Mesh(
        mesh.devices.reshape(groups, devices_fsdp // cores, cores), ("grp", "chip", "core")
    )
    fsdp = ("chip", "core")
    placed = (
        P("grp", fsdp, None, None),
        P("grp", fsdp, None),
        P("grp", fsdp, None),
        P(),
        P(fsdp, None),
        P(),
    )
    return jax.shard_map(
        shards, mesh=finer, in_specs=placed, out_specs=P("grp", fsdp, None), check_vma=False
    )
```

```python
import functools

import jax
import jax.numpy as jnp
from jax import lax
from jax.experimental import pallas as pl
from jax.experimental.pallas import tpu as pltpu
from jax.sharding import Mesh, PartitionSpec as P

sharpness = 20.0
cores = 2
longest_ring = 16
vmem_limit = 20 << 20


def ring_order(chips):
    return list(range(0, chips, 2)) + list(range(1, chips, 2))[::-1]


def ring_place(chip, chips):
    return jnp.where(chip % 2 == 0, chip // 2, chips - 1 - chip // 2)


def ring_chip(place, chips):
    place = lax.rem(place + 2 * chips, chips)
    return jnp.where(place < chips // 2, 2 * place, 2 * (chips - 1 - place) + 1)


def along_ring(block, by):
    order = ring_order(lax.axis_size("chip"))
    pairs = [(chip, order[(i + by) % len(order)]) for i, chip in enumerate(order)]
    return lax.ppermute(block, "chip", pairs)


def after(first, block):
    return lax.optimization_barrier((first, block))[1]


def from_sibling(block):
    return lax.ppermute(block, "core", [(0, 1), (1, 0)])


def slab_blocks(stored, chips, core):
    order = ring_order(chips)
    kept = []
    for j in range(chips // cores):
        pairs = []
        for i, chip in enumerate(order):
            for c in range(cores):
                source = order[(i + j + c * (chips // cores)) % chips]
                pairs.append(((chips + source) * cores + c, chip * cores + c))
        kept.append(lax.ppermute(stored, ("grp", "chip", "core"), pairs))
    kept = jnp.concatenate(kept)
    other = from_sibling(kept)
    return [jnp.where(core == 0, kept, other), jnp.where(core == 0, other, kept)]


def in_core_order(mine, other, core, axis=0):
    return jnp.where(
        core == 0,
        jnp.concatenate([mine, other], axis=axis),
        jnp.concatenate([other, mine], axis=axis),
    )


def normalize_kernel(chunk, states_ref, gain_ref, out_ref):
    @pl.loop(0, states_ref.shape[1] // chunk)
    def _(i):
        at = pl.ds(pl.multiple_of(i * chunk, chunk), chunk)
        wide = states_ref[0, at, :].astype(jnp.float32)
        mean_square = jnp.mean(wide * wide, axis=-1, keepdims=True)
        wide = wide * lax.rsqrt(mean_square + 1e-05) * gain_ref[...]
        out_ref[at, :] = wide.astype(jnp.bfloat16)


def normalize(states, gain):
    seqs, length, width = states.shape
    tokens = seqs * length
    return pl.pallas_call(
        functools.partial(normalize_kernel, 16),
        grid=(seqs,),
        in_specs=[
            pl.BlockSpec((1, length, width), lambda i: (i, 0, 0)),
            pl.BlockSpec((1, width), lambda i: (0, 0)),
        ],
        out_specs=pl.BlockSpec((length, width), lambda i: (i, 0)),
        out_shape=jax.ShapeDtypeStruct((tokens, width), jnp.bfloat16),
        compiler_params=pltpu.CompilerParams(vmem_limit_bytes=vmem_limit),
        cost_estimate=pl.CostEstimate(
            flops=6 * tokens * width, bytes_accessed=4 * tokens * width, transcendentals=tokens
        ),
    )(states, gain[None])


def shards(token_states, token_ids, master, gain, cand_ids, slab_owner):
    trainer = lax.axis_index("grp") == 0
    chips = lax.axis_size("chip")
    chip = lax.axis_index("chip")
    core = lax.axis_index("core")
    place = ring_place(chip, chips)
    states = token_states[0]
    seq_dev, length, width = states.shape
    rows, embedding = master.shape[1:]
    half = embedding // cores
    seqs = cores * seq_dev

    weights = master[0]
    own = lax.dynamic_slice(weights, (0, core * half), (rows, half)).astype(jnp.bfloat16)
    given = lax.dynamic_slice(weights, (0, (1 - core) * half), (rows, half))
    given = given.astype(jnp.bfloat16)
    sibling = from_sibling(given)

    normed = normalize(after(sibling, states), gain)
    normed = [normed, from_sibling(normed)]
    first_sent = along_ring(own, 1)
    ids, cand_ids = token_ids[0], after(first_sent, cand_ids)
    ids = jnp.concatenate([ids, cand_ids], axis=1)
    ids = jnp.concatenate([ids, from_sibling(ids)])
    lengths = jnp.sum((ids[:, :length] != 0).astype(jnp.int32), axis=1)
    counts = lengths.astype(jnp.float32)
    cands = ids[:, length:]

    def columns(offset, part, whose):
        first = (ring_chip(place + offset, chips) * cores + part) * rows
        return lax.dynamic_slice(normed[whose], (0, first), (seq_dev * length, rows))

    def added(totals, whose, blocks):
        for offset, part, block in blocks:
            term = jnp.dot(
                columns(offset, part, whose), block, preferred_element_type=jnp.float32
            )
            totals[whose] = term if totals[whose] is None else totals[whose] + term

    parts = (core, 1 - core)
    if chips <= longest_ring:
        moving = {(i, by): block for by in (1, -1) for i, block in enumerate((own, sibling))}
        totals, sums = [None, None], {}
        waiting = [(0, parts[0], own), (0, parts[1], sibling)]
        for step in range(1, chips // 2 + 1):
            last = step == chips // 2
            sent = [(0, 1), (0, -1), (1, 1), (1, -1)]
            for i, by in [(0, 1), (1, -1)] if last else sent:
                if (step, i, by) == (1, 0, 1):
                    moving[i, by] = first_sent
                else:
                    if last and step > 2:
                        moving[i, by] = after(sums[step - 2 + i][1], moving[i, by])
                    elif step > 2:
                        moving[i, by] = after(sums[step - 2][0], moving[i, by])
                    moving[i, by] = along_ring(moving[i, by], by)
                waiting.append((-by * step, parts[i], moving[i, by]))
            for whose in range(2):
                added(totals, whose, waiting)
            sums[step] = list(totals)
            waiting = []
    else:
        both = in_core_order(own, sibling, core)
        gathered = lax.all_gather(both, "chip", axis=0, tiled=True)
        totals = [jnp.dot(n, gathered, preferred_element_type=jnp.float32) for n in normed]

    there = jnp.arange(length)[None, :, None] < lengths[:, None, None]
    there = [there[:seq_dev], there[seq_dev:]]
    active = [jnp.tanh(total).reshape(seq_dev, length, half) for total in totals]
    pooled = [jnp.sum(jnp.where(there[w], active[w], 0.0), axis=1) for w in range(2)]
    pooled = jnp.concatenate(pooled) / counts[:, None]
    pooled_other = from_sibling(pooled)
    pooled_other = jnp.concatenate([pooled_other[seq_dev:], pooled_other[:seq_dev]])
    whole = in_core_order(pooled, pooled_other, core, axis=1)
    pooled_square = jnp.mean(whole * whole, axis=-1, keepdims=True)
    scale = lax.rsqrt(pooled_square + 1e-06)
    unit = whole * scale
    stored = unit.astype(jnp.bfloat16)
    stored = in_core_order(stored[:seq_dev], stored[seq_dev:], core)

    cut = {}
    if chips <= longest_ring:
        steps = [(chips // 2, 0, 1), (chips // 2, 1, -1), (chips // 2 - 1, 1, 1)]
        steps += [(chips // 2 - 1, 0, -1)]
        cut = {
            (by * step, i, w): columns(by * step, parts[i], w)
            for step, i, by in steps
            for w in range(2)
        }
        stored, *cuts = lax.optimization_barrier([stored, *cut.values()])
        cut = dict(zip(cut, cuts))
    slab = jnp.concatenate(slab_blocks(stored, chips, core))
    slab_rows = slab.shape[0]
    earlier = jnp.arange(slab_rows)[:, None] < jnp.arange(slab_rows)[None, :]
    same = slab_owner[:, None] == slab_owner[None, :]
    ranks = jnp.sum((earlier & same).astype(jnp.int32), axis=0)
    owner_place = ring_place(slab_owner // cores, chips)
    seen = lax.rem(owner_place - place + chips, chips)
    slots = seen * seqs + lax.rem(slab_owner, cores) * seq_dev + ranks
    positive, candidate = [
        jnp.sum(
            (slots[picked][:, :, None] == jnp.arange(slab_rows)).astype(jnp.float32), axis=1
        )
        for picked in (cands[:, :1], cands)
    ]

    slab_wide = slab.astype(jnp.float32)
    logits = (
        sharpness / embedding * jnp.dot(unit, slab_wide.T, precision=lax.Precision.HIGHEST)
    )
    exponent = jnp.where(candidate > 0, jnp.exp(logits), 0.0)
    probs = exponent / jnp.sum(exponent, axis=-1, keepdims=True)
    logit_grad = probs - positive
    unit_grad = (
        sharpness / embedding * jnp.dot(logit_grad, slab_wide, precision=lax.Precision.HIGHEST)
    )
    inner = jnp.sum(whole * unit_grad, axis=-1, keepdims=True)
    pooled_grad = scale * unit_grad - whole * (scale * scale * scale) * inner / embedding
    pooled_grad = lax.dynamic_slice(pooled_grad, (0, core * half), (seqs, half))
    weighted = pooled_grad / counts[:, None]
    weighted = [weighted[:seq_dev], weighted[seq_dev:]]
    delta = [
        jnp.where(there[w], weighted[w][:, None, :] * (1.0 - active[w] * active[w]), 0.0)
        .astype(jnp.bfloat16)
        .reshape(seq_dev * length, half)
        for w in range(2)
    ]
    *delta, weights = lax.optimization_barrier((*delta, weights))
    copied = lax.ppermute(weights.astype(jnp.bfloat16), "grp", [(0, 1)])

    def term(offset, i, delta):
        total = None
        for w in range(2):
            key = (offset, i, w)
            term = lax.dot_general(
                cut[key] if key in cut else columns(offset, parts[i], w),
                delta[w],
                (((0,), (0,)), ((), ())),
                preferred_element_type=jnp.float32,
            )
            total = term if total is None else total + term
        return total

    if chips <= longest_ring:
        arrived = {}
        late = delta
        for step in range(chips // 2, 0, -1):
            for i, by in ((0, 1), (1, -1), (1, 1), (0, -1)):
                if step == chips // 2 and (i, by) not in ((0, 1), (1, -1)):
                    continue
                total = term(by * step, i, delta if step > chips // 2 - 2 else late)
                if (i, by) in arrived:
                    total = total + arrived[i, by].astype(jnp.float32)
                if step == 1 and i == 0:
                    total = after(copied, total)
                arrived[i, by] = along_ring(total.astype(jnp.bfloat16), by)
            if step == chips // 2:
                late = [after(arrived[0, 1], part) for part in delta]
        mine, other = [
            term(0, i, late)
            + arrived[i, 1].astype(jnp.float32)
            + arrived[i, -1].astype(jnp.float32)
            for i in range(2)
        ]
    else:
        grad = sum(
            lax.dot_general(
                n, d, (((0,), (0,)), ((), ())), preferred_element_type=jnp.float32
            )
            for n, d in zip(normed, delta)
        )
        reduced = lax.psum_scatter(grad, "chip", scatter_dimension=0, tiled=True)
        mine, other = [lax.dynamic_slice(reduced, (i * rows, 0), (rows, half)) for i in parts]
    other = from_sibling(other)
    shard = in_core_order(mine, other, core, axis=1)
    row_square = jnp.mean(shard * shard, axis=1, keepdims=True)
    normalized = shard * lax.rsqrt(row_square + 1e-06)
    result = jnp.where(trainer, normalized, copied.astype(jnp.float32))
    return result[None]


def solution(mesh):
    groups, devices_fsdp = mesh.devices.shape
    finer = Mesh(
        mesh.devices.reshape(groups, devices_fsdp // cores, cores), ("grp", "chip", "core")
    )
    fsdp = ("chip", "core")
    placed = (
        P("grp", fsdp, None, None),
        P("grp", fsdp, None),
        P("grp", fsdp, None),
        P(),
        P(fsdp, None),
        P(),
    )
    return jax.shard_map(
        shards, mesh=finer, in_specs=placed, out_specs=P("grp", fsdp, None), check_vma=False
    )
```

```python
import jax
import jax.numpy as jnp
from jax import lax
from jax.sharding import Mesh, PartitionSpec as P

sharpness = 20.0
cores = 2
longest_ring = 16


def ring_order(chips):
    return list(range(0, chips, 2)) + list(range(1, chips, 2))[::-1]


def ring_place(chip, chips):
    return jnp.where(chip % 2 == 0, chip // 2, chips - 1 - chip // 2)


def ring_chip(place, chips):
    place = lax.rem(place + 2 * chips, chips)
    return jnp.where(place < chips // 2, 2 * place, 2 * (chips - 1 - place) + 1)


def along_ring(block, by):
    order = ring_order(lax.axis_size("chip"))
    pairs = [(chip, order[(i + by) % len(order)]) for i, chip in enumerate(order)]
    return lax.ppermute(block, "chip", pairs)


def after(first, block):
    return lax.optimization_barrier((first, block))[1]


def from_sibling(block):
    return lax.ppermute(block, "core", [(0, 1), (1, 0)])


def slab_blocks(stored, chips):
    order = ring_order(chips)
    kept = []
    for j in range(chips // cores):
        pairs = []
        for i, chip in enumerate(order):
            for c in range(cores):
                source = order[(i + j + c * (chips // cores)) % chips]
                pairs.append(((chips + source) * cores + c, chip * cores + c))
        kept.append(lax.ppermute(stored, ("grp", "chip", "core"), pairs))
    return kept


def in_core_order(mine, other, core, axis=0):
    return jnp.where(
        core == 0,
        jnp.concatenate([mine, other], axis=axis),
        jnp.concatenate([other, mine], axis=axis),
    )


def normalize(states, gain):
    states_wide = states.astype(jnp.float32)
    mean_square = jnp.mean(states_wide * states_wide, axis=-1, keepdims=True)
    return (states_wide * lax.rsqrt(mean_square + 1e-05) * gain).astype(jnp.bfloat16)


def shards(token_states, token_ids, master, gain, cand_ids, slab_owner):
    trainer = lax.axis_index("grp") == 0
    chips = lax.axis_size("chip")
    chip = lax.axis_index("chip")
    core = lax.axis_index("core")
    place = ring_place(chip, chips)
    states = token_states[0]
    seq_dev, length, width = states.shape
    rows, embedding = master.shape[1:]
    half = embedding // cores
    seqs = cores * seq_dev

    weights = master[0]
    own = lax.dynamic_slice(weights, (0, core * half), (rows, half)).astype(jnp.bfloat16)
    given = lax.dynamic_slice(weights, (0, (1 - core) * half), (rows, half))
    given = given.astype(jnp.bfloat16)
    sibling = from_sibling(given)

    first_sent = along_ring(own, 1)
    other_states = from_sibling(states)
    states = after(first_sent, states)
    ids, cand_ids = token_ids[0], after(first_sent, cand_ids)
    slab_owner = after(first_sent, slab_owner)
    normed = jnp.concatenate([normalize(states, gain), normalize(other_states, gain)])
    normed = normed.reshape(seqs * length, width)
    ids = jnp.concatenate([ids, cand_ids], axis=1)
    ids = jnp.concatenate([ids, from_sibling(ids)])
    lengths = jnp.sum((ids[:, :length] != 0).astype(jnp.int32), axis=1)
    counts = lengths.astype(jnp.float32)
    cands = ids[:, length:]

    def columns(offset, part):
        first = (ring_chip(place + offset, chips) * cores + part) * rows
        return lax.dynamic_slice(normed, (0, first), (seqs * length, rows))

    def product(offset, part, block):
        return jnp.dot(columns(offset, part), block, preferred_element_type=jnp.float32)

    parts = (core, 1 - core)
    if chips <= longest_ring:
        moving = {(i, by): block for by in (1, -1) for i, block in enumerate((own, sibling))}
        total = product(0, parts[0], own) + product(0, parts[1], sibling)
        sums = {}
        for step in range(1, chips // 2 + 1):
            last = step == chips // 2
            sent = [(0, 1), (0, -1), (1, 1), (1, -1)]
            for i, by in [(0, 1), (1, -1)] if last else sent:
                if (step, i, by) == (1, 0, 1):
                    moving[i, by] = first_sent
                else:
                    if last and i == 1 and step > 2:
                        moving[i, by] = after(sums[1], moving[i, by])
                    moving[i, by] = along_ring(moving[i, by], by)
                total = total + product(-by * step, parts[i], moving[i, by])
            sums[step] = total
            if step == 1:
                weights = after(moving[1, 1], weights)
    else:
        both = in_core_order(own, sibling, core)
        gathered = lax.all_gather(both, "chip", axis=0, tiled=True)
        total = jnp.dot(normed, gathered, preferred_element_type=jnp.float32)

    copied = lax.ppermute(weights.astype(jnp.bfloat16), "grp", [(0, 1)])
    active = jnp.tanh(total).reshape(seqs, length, half)
    there = jnp.arange(length)[None, :, None] < lengths[:, None, None]
    pooled = jnp.sum(jnp.where(there, active, 0.0), axis=1) / counts[:, None]
    pooled, copied = lax.optimization_barrier((pooled, copied))
    pooled_other = from_sibling(pooled)
    pooled_other = jnp.concatenate([pooled_other[seq_dev:], pooled_other[:seq_dev]])
    whole = in_core_order(pooled, pooled_other, core, axis=1)
    pooled_square = jnp.mean(whole * whole, axis=-1, keepdims=True)
    scale = lax.rsqrt(pooled_square + 1e-06)
    unit = whole * scale
    stored = unit.astype(jnp.bfloat16)
    stored = in_core_order(stored[:seq_dev], stored[seq_dev:], core)

    kept = slab_blocks(stored, chips)
    kept = jnp.concatenate(kept)
    slab = in_core_order(kept, from_sibling(kept), core)
    slab_rows = slab.shape[0]
    earlier = jnp.arange(slab_rows)[:, None] < jnp.arange(slab_rows)[None, :]
    same = slab_owner[:, None] == slab_owner[None, :]
    ranks = jnp.sum((earlier & same).astype(jnp.int32), axis=0)
    owner_place = ring_place(slab_owner // cores, chips)
    seen = lax.rem(owner_place - place + chips, chips)
    slots = seen * seqs + lax.rem(slab_owner, cores) * seq_dev + ranks
    positive, candidate = [
        jnp.sum(
            (slots[picked][:, :, None] == jnp.arange(slab_rows)).astype(jnp.float32), axis=1
        )
        for picked in (cands[:, :1], cands)
    ]

    slab_wide = slab.astype(jnp.float32)
    logits = (
        sharpness / embedding * jnp.dot(unit, slab_wide.T, precision=lax.Precision.HIGHEST)
    )
    exponent = jnp.where(candidate > 0, jnp.exp(logits), 0.0)
    probs = exponent / jnp.sum(exponent, axis=-1, keepdims=True)
    logit_grad = probs - positive
    unit_grad = (
        sharpness / embedding * jnp.dot(logit_grad, slab_wide, precision=lax.Precision.HIGHEST)
    )
    inner = jnp.sum(whole * unit_grad, axis=-1, keepdims=True)
    pooled_grad = scale * unit_grad - whole * (scale * scale * scale) * inner / embedding
    pooled_grad = lax.dynamic_slice(pooled_grad, (0, core * half), (seqs, half))
    delta = (pooled_grad / counts[:, None])[:, None, :] * (1.0 - active * active)
    delta = jnp.where(there, delta, 0.0)
    delta = delta.astype(jnp.bfloat16).reshape(seqs * length, half)

    def term(offset, part, delta):
        return lax.dot_general(
            columns(offset, part),
            delta,
            (((0,), (0,)), ((), ())),
            preferred_element_type=jnp.float32,
        )

    if chips <= longest_ring:
        arrived = {}
        late = delta
        for step in range(chips // 2, 0, -1):
            for i, by in ((0, 1), (1, -1), (1, 1), (0, -1)):
                if step == chips // 2 and (i, by) not in ((0, 1), (1, -1)):
                    continue
                total = term(by * step, parts[i], delta)
                if (i, by) in arrived:
                    total = total + arrived[i, by].astype(jnp.float32)
                if step == 1 and i == 0:
                    total = after(copied, total)
                arrived[i, by] = along_ring(total.astype(jnp.bfloat16), by)
            if step == chips // 2:
                late = after(arrived[0, 1], delta)
        owns = [term(0, parts[i], late) for i in range(2)]
        arrived[1, 1] = after(owns, arrived[1, 1])
        arrived[0, -1] = after(owns, arrived[0, -1])
        mine, other = [
            owns[i] + arrived[i, 1].astype(jnp.float32) + arrived[i, -1].astype(jnp.float32)
            for i in range(2)
        ]
    else:
        grad = lax.dot_general(
            normed, delta, (((0,), (0,)), ((), ())), preferred_element_type=jnp.float32
        )
        reduced = lax.psum_scatter(grad, "chip", scatter_dimension=0, tiled=True)
        mine, other = [lax.dynamic_slice(reduced, (i * rows, 0), (rows, half)) for i in parts]
    other = from_sibling(other)
    shard = in_core_order(mine, other, core, axis=1)
    row_square = jnp.mean(shard * shard, axis=1, keepdims=True)
    normalized = shard * lax.rsqrt(row_square + 1e-06)
    result = jnp.where(trainer, normalized, copied.astype(jnp.float32))
    return result[None]


def solution(mesh):
    groups, devices_fsdp = mesh.devices.shape
    finer = Mesh(
        mesh.devices.reshape(groups, devices_fsdp // cores, cores), ("grp", "chip", "core")
    )
    fsdp = ("chip", "core")
    placed = (
        P("grp", fsdp, None, None),
        P("grp", fsdp, None),
        P("grp", fsdp, None),
        P(),
        P(fsdp, None),
        P(),
    )
    return jax.shard_map(
        shards, mesh=finer, in_specs=placed, out_specs=P("grp", fsdp, None), check_vma=False
    )
```

```python
import jax
import jax.numpy as jnp
from jax import lax
from jax.sharding import Mesh, PartitionSpec as P

sharpness = 20.0
cores = 2
longest_ring = 16


def ring_order(chips):
    return list(range(0, chips, 2)) + list(range(1, chips, 2))[::-1]


def ring_place(chip, chips):
    return jnp.where(chip % 2 == 0, chip // 2, chips - 1 - chip // 2)


def ring_chip(place, chips):
    place = lax.rem(place + 2 * chips, chips)
    return jnp.where(place < chips // 2, 2 * place, 2 * (chips - 1 - place) + 1)


def along_ring(block, by):
    order = ring_order(lax.axis_size("chip"))
    pairs = [(chip, order[(i + by) % len(order)]) for i, chip in enumerate(order)]
    return lax.ppermute(block, "chip", pairs)


def after(first, block):
    return lax.optimization_barrier((first, block))[1]


def passed_on(weights):
    return lax.ppermute(weights.astype(jnp.bfloat16), "grp", [(0, 1)])


def from_sibling(block):
    return lax.ppermute(block, "core", [(0, 1), (1, 0)])


def slab_blocks(stored, chips):
    order = ring_order(chips)
    kept = []
    for j in range(chips // cores):
        pairs = []
        for i, chip in enumerate(order):
            for c in range(cores):
                source = order[(i + j + c * (chips // cores)) % chips]
                pairs.append(((chips + source) * cores + c, chip * cores + c))
        kept.append(lax.ppermute(stored, ("grp", "chip", "core"), pairs))
    return kept


def in_core_order(mine, other, core, axis=0):
    return jnp.where(
        core == 0,
        jnp.concatenate([mine, other], axis=axis),
        jnp.concatenate([other, mine], axis=axis),
    )


def normalize(states, gain):
    states_wide = states.astype(jnp.float32)
    mean_square = jnp.mean(states_wide * states_wide, axis=-1, keepdims=True)
    return (states_wide * lax.rsqrt(mean_square + 1e-05) * gain).astype(jnp.bfloat16)


def shards(token_states, token_ids, master, gain, cand_ids, slab_owner):
    trainer = lax.axis_index("grp") == 0
    chips = lax.axis_size("chip")
    chip = lax.axis_index("chip")
    core = lax.axis_index("core")
    place = ring_place(chip, chips)
    states = token_states[0]
    seq_dev, length, width = states.shape
    rows, embedding = master.shape[1:]
    half = embedding // cores
    seqs = cores * seq_dev

    weights = master[0]
    own = lax.dynamic_slice(weights, (0, core * half), (rows, half)).astype(jnp.bfloat16)
    given = lax.dynamic_slice(weights, (0, (1 - core) * half), (rows, half))
    given = given.astype(jnp.bfloat16)
    sibling = from_sibling(given)

    first_sent = along_ring(own, 1)
    other_states = from_sibling(states)
    normed_own = normalize(after(first_sent, states), gain)
    normed_other = normalize(after(normed_own, other_states), gain)
    ids, cand_ids = token_ids[0], after(first_sent, cand_ids)
    slab_owner = after(first_sent, slab_owner)
    normed = jnp.concatenate([normed_own, normed_other])
    normed = normed.reshape(seqs * length, width)
    ids = jnp.concatenate([ids, cand_ids], axis=1)
    ids = jnp.concatenate([ids, from_sibling(ids)])
    lengths = jnp.sum((ids[:, :length] != 0).astype(jnp.int32), axis=1)
    counts = lengths.astype(jnp.float32)
    cands = ids[:, length:]

    def columns(offset, part):
        first = (ring_chip(place + offset, chips) * cores + part) * rows
        return lax.dynamic_slice(normed, (0, first), (seqs * length, rows))

    def product(offset, part, block):
        return jnp.dot(columns(offset, part), block, preferred_element_type=jnp.float32)

    parts = (core, 1 - core)
    if chips <= longest_ring:
        moving = {(i, by): block for by in (1, -1) for i, block in enumerate((own, sibling))}
        total = product(0, parts[0], own) + product(0, parts[1], sibling)
        sums = {}
        for step in range(1, chips // 2 + 1):
            last = step == chips // 2
            sent = [(0, 1), (0, -1), (1, 1), (1, -1)]
            for i, by in [(0, 1), (1, -1)] if last else sent:
                if (step, i, by) == (1, 0, 1):
                    moving[i, by] = first_sent
                else:
                    if last and step > 2:
                        moving[i, by] = after(sums[1 + i], moving[i, by])
                    elif step in (2, 3) and i == 1:
                        norms = normed_own if step == 2 else normed_other
                        moving[i, by] = after(norms, moving[i, by])
                    moving[i, by] = along_ring(moving[i, by], by)
                total = total + product(-by * step, parts[i], moving[i, by])
            sums[step] = total
    else:
        both = in_core_order(own, sibling, core)
        gathered = lax.all_gather(both, "chip", axis=0, tiled=True)
        total = jnp.dot(normed, gathered, preferred_element_type=jnp.float32)

    active = jnp.tanh(total).reshape(seqs, length, half)
    there = jnp.arange(length)[None, :, None] < lengths[:, None, None]
    pooled = jnp.sum(jnp.where(there, active, 0.0), axis=1) / counts[:, None]
    pooled_other = from_sibling(pooled)
    pooled_other = jnp.concatenate([pooled_other[seq_dev:], pooled_other[:seq_dev]])
    whole = in_core_order(pooled, pooled_other, core, axis=1)
    pooled_square = jnp.mean(whole * whole, axis=-1, keepdims=True)
    scale = lax.rsqrt(pooled_square + 1e-06)
    unit = whole * scale
    stored = unit.astype(jnp.bfloat16)
    stored = in_core_order(stored[:seq_dev], stored[seq_dev:], core)

    kept = slab_blocks(stored, chips)
    kept = jnp.concatenate(kept)
    slab = [kept, from_sibling(kept)]
    slab_rows = slab_owner.shape[0]
    earlier = jnp.arange(slab_rows)[:, None] < jnp.arange(slab_rows)[None, :]
    same = slab_owner[:, None] == slab_owner[None, :]
    ranks = jnp.sum((earlier & same).astype(jnp.int32), axis=0)
    owner_place = ring_place(slab_owner // cores, chips)
    seen = lax.rem(owner_place - place - core * (chips // cores) + 2 * chips, chips)
    slots = seen * seqs + lax.rem(slab_owner, cores) * seq_dev + ranks
    moved = (slots[:, None] == jnp.arange(slab_rows)[None, :]).astype(jnp.float32)
    picked = (cands[:, :, None] == jnp.arange(slab_rows)).astype(jnp.float32)
    positive = jnp.dot(picked[:, 0], moved)
    candidate = jnp.dot(jnp.sum(picked, axis=1), moved)
    piece = slab_rows // cores
    pieces = [slice(i * piece, (i + 1) * piece) for i in range(cores)]

    slab_wide = [rows_in.astype(jnp.float32) for rows_in in slab]
    exponent = []
    for rows_in, at in zip(slab_wide, pieces):
        logits = (
            sharpness / embedding * jnp.dot(unit, rows_in.T, precision=lax.Precision.HIGHEST)
        )
        exponent.append(jnp.where(candidate[:, at] > 0.5, jnp.exp(logits), 0.0))
    denominator = sum(jnp.sum(part, axis=-1, keepdims=True) for part in exponent)
    unit_grad = (
        sharpness
        / embedding
        * sum(
            jnp.dot(
                part / denominator - positive[:, at], rows_in, precision=lax.Precision.HIGHEST
            )
            for part, rows_in, at in zip(exponent, slab_wide, pieces)
        )
    )
    inner = jnp.sum(whole * unit_grad, axis=-1, keepdims=True)
    pooled_grad = scale * unit_grad - whole * (scale * scale * scale) * inner / embedding
    pooled_grad = lax.dynamic_slice(pooled_grad, (0, core * half), (seqs, half))
    delta = (pooled_grad / counts[:, None])[:, None, :] * (1.0 - active * active)
    delta = jnp.where(there, delta, 0.0)
    delta = delta.astype(jnp.bfloat16).reshape(seqs * length, half)

    def term(offset, part, delta):
        return lax.dot_general(
            columns(offset, part),
            delta,
            (((0,), (0,)), ((), ())),
            preferred_element_type=jnp.float32,
        )

    if chips <= longest_ring:
        arrived = {}
        late = delta
        for step in range(chips // 2, 0, -1):
            for i, by in ((0, 1), (1, -1), (1, 1), (0, -1)):
                if step == chips // 2 and (i, by) not in ((0, 1), (1, -1)):
                    continue
                total = term(by * step, parts[i], delta)
                if (i, by) in arrived:
                    total = total + arrived[i, by].astype(jnp.float32)
                if step == 1 and i == 0:
                    total = after(copied, total)
                arrived[i, by] = along_ring(total.astype(jnp.bfloat16), by)
            if step == chips // 2:
                late, weights = after(arrived[0, 1], (delta, weights))
                copied = passed_on(weights)
        owns = [term(0, parts[i], late) for i in range(2)]
        arrived[1, 1] = after(owns, arrived[1, 1])
        arrived[0, -1] = after(owns, arrived[0, -1])
        mine, other = [
            owns[i] + arrived[i, 1].astype(jnp.float32) + arrived[i, -1].astype(jnp.float32)
            for i in range(2)
        ]
    else:
        grad = lax.dot_general(
            normed, delta, (((0,), (0,)), ((), ())), preferred_element_type=jnp.float32
        )
        copied = passed_on(weights)
        reduced = lax.psum_scatter(grad, "chip", scatter_dimension=0, tiled=True)
        mine, other = [lax.dynamic_slice(reduced, (i * rows, 0), (rows, half)) for i in parts]
    other = from_sibling(other)
    shard = in_core_order(mine, other, core, axis=1)
    row_square = jnp.mean(shard * shard, axis=1, keepdims=True)
    normalized = shard * lax.rsqrt(row_square + 1e-06)
    result = jnp.where(trainer, normalized, copied.astype(jnp.float32))
    return result[None]


def solution(mesh):
    groups, devices_fsdp = mesh.devices.shape
    finer = Mesh(
        mesh.devices.reshape(groups, devices_fsdp // cores, cores), ("grp", "chip", "core")
    )
    fsdp = ("chip", "core")
    placed = (
        P("grp", fsdp, None, None),
        P("grp", fsdp, None),
        P("grp", fsdp, None),
        P(),
        P(fsdp, None),
        P(),
    )
    return jax.shard_map(
        shards, mesh=finer, in_specs=placed, out_specs=P("grp", fsdp, None), check_vma=False
    )
```

```python
import functools

import jax
import jax.numpy as jnp
from jax import lax
from jax.experimental import pallas as pl
from jax.experimental.pallas import tpu as pltpu
from jax.sharding import Mesh, PartitionSpec as P

sharpness = 20.0
cores = 2
longest_ring = 16
vmem_limit = 16 << 20


def ring_order(chips):
    return list(range(0, chips, 2)) + list(range(1, chips, 2))[::-1]


def ring_place(chip, chips):
    return jnp.where(chip % 2 == 0, chip // 2, chips - 1 - chip // 2)


def ring_chip(place, chips):
    place = lax.rem(place + 2 * chips, chips)
    return jnp.where(place < chips // 2, 2 * place, 2 * (chips - 1 - place) + 1)


def along_ring(block, by):
    order = ring_order(lax.axis_size("chip"))
    pairs = [(chip, order[(i + by) % len(order)]) for i, chip in enumerate(order)]
    return lax.ppermute(block, "chip", pairs)


def after(first, block):
    return lax.optimization_barrier((first, block))[1]


def passed_on(weights):
    return lax.ppermute(weights.astype(jnp.bfloat16), "grp", [(0, 1)])


def from_sibling(block):
    return lax.ppermute(block, "core", [(0, 1), (1, 0)])


def slab_blocks(stored, chips):
    order = ring_order(chips)
    kept = []
    for j in range(chips // cores):
        pairs = []
        for i, chip in enumerate(order):
            for c in range(cores):
                source = order[(i + j + c * (chips // cores)) % chips]
                pairs.append(((chips + source) * cores + c, chip * cores + c))
        kept.append(lax.ppermute(stored, ("grp", "chip", "core"), pairs))
    return kept


def in_core_order(mine, other, core, axis=0):
    return jnp.where(
        core == 0,
        jnp.concatenate([mine, other], axis=axis),
        jnp.concatenate([other, mine], axis=axis),
    )


def normalize_kernel(seqs, chunk, mine_ref, other_ref, gain_ref, out_ref):
    length = mine_ref.shape[1]

    def run(ref):
        @pl.loop(0, length // chunk)
        def _(i):
            at = pl.ds(pl.multiple_of(i * chunk, chunk), chunk)
            wide = ref[0, at, :].astype(jnp.float32)
            mean_square = jnp.mean(wide * wide, axis=-1, keepdims=True)
            wide = wide * lax.rsqrt(mean_square + 1e-05) * gain_ref[...]
            out_ref[at, :] = wide.astype(jnp.bfloat16)

    @pl.when(pl.program_id(0) < seqs)
    def _():
        run(mine_ref)

    @pl.when(pl.program_id(0) >= seqs)
    def _():
        run(other_ref)


def normalize_both(mine, other, gain):
    seqs, length, width = mine.shape
    tokens = 2 * seqs * length
    return pl.pallas_call(
        functools.partial(normalize_kernel, seqs, 16),
        grid=(2 * seqs,),
        in_specs=[
            pl.BlockSpec((1, length, width), lambda i: (jnp.minimum(i, seqs - 1), 0, 0)),
            pl.BlockSpec((1, length, width), lambda i: (jnp.maximum(i - seqs, 0), 0, 0)),
            pl.BlockSpec((1, width), lambda i: (0, 0)),
        ],
        out_specs=pl.BlockSpec((length, width), lambda i: (i, 0)),
        out_shape=jax.ShapeDtypeStruct((tokens, width), jnp.bfloat16),
        compiler_params=pltpu.CompilerParams(vmem_limit_bytes=vmem_limit),
        cost_estimate=pl.CostEstimate(
            flops=6 * tokens * width, bytes_accessed=4 * tokens * width, transcendentals=tokens
        ),
    )(mine, other, gain[None])


def shards(token_states, token_ids, master, gain, cand_ids, slab_owner):
    trainer = lax.axis_index("grp") == 0
    chips = lax.axis_size("chip")
    chip = lax.axis_index("chip")
    core = lax.axis_index("core")
    place = ring_place(chip, chips)
    states = token_states[0]
    seq_dev, length, width = states.shape
    rows, embedding = master.shape[1:]
    half = embedding // cores
    seqs = cores * seq_dev

    weights = master[0]
    own = lax.dynamic_slice(weights, (0, core * half), (rows, half)).astype(jnp.bfloat16)
    given = lax.dynamic_slice(weights, (0, (1 - core) * half), (rows, half))
    given = given.astype(jnp.bfloat16)
    sibling = from_sibling(given)

    other_states = from_sibling(states)
    parts = (core, 1 - core)
    sent = [(0, 1), (0, -1), (1, 1), (1, -1)]
    ids = token_ids[0]
    if chips <= longest_ring:
        moving = {(i, by): along_ring((own, sibling)[i], by) for i, by in sent}
        states, cand_ids, slab_owner = after(moving[1, 1], (states, cand_ids, slab_owner))
    normed = normalize_both(states, other_states, gain)
    ids = jnp.concatenate([ids, cand_ids], axis=1)
    ids = jnp.concatenate([ids, from_sibling(ids)])
    lengths = jnp.sum((ids[:, :length] != 0).astype(jnp.int32), axis=1)
    counts = lengths.astype(jnp.float32)
    cands = ids[:, length:]

    def columns(offset, part):
        first = (ring_chip(place + offset, chips) * cores + part) * rows
        return lax.dynamic_slice(normed, (0, first), (seqs * length, rows))

    def product(offset, part, block):
        return jnp.dot(columns(offset, part), block, preferred_element_type=jnp.float32)

    if chips <= longest_ring:
        total = product(0, parts[0], own) + product(0, parts[1], sibling)
        sums = {}
        for step in range(1, chips // 2 + 1):
            last = step == chips // 2
            for i, by in [(0, 1), (1, -1)] if last else sent:
                if step > 1:
                    if last and step > 2:
                        moving[i, by] = after(sums[1 + i], moving[i, by])
                    elif step == 3 and i == 1:
                        moving[i, by] = after(normed, moving[i, by])
                    moving[i, by] = along_ring(moving[i, by], by)
                total = total + product(-by * step, parts[i], moving[i, by])
            sums[step] = total
    else:
        both = in_core_order(own, sibling, core)
        gathered = lax.all_gather(both, "chip", axis=0, tiled=True)
        total = jnp.dot(normed, gathered, preferred_element_type=jnp.float32)

    active = jnp.tanh(total).reshape(seqs, length, half)
    there = jnp.arange(length)[None, :, None] < lengths[:, None, None]
    pooled = jnp.sum(jnp.where(there, active, 0.0), axis=1) / counts[:, None]
    pooled_other = from_sibling(pooled)
    pooled_other = jnp.concatenate([pooled_other[seq_dev:], pooled_other[:seq_dev]])
    whole = in_core_order(pooled, pooled_other, core, axis=1)
    pooled_square = jnp.mean(whole * whole, axis=-1, keepdims=True)
    scale = lax.rsqrt(pooled_square + 1e-06)
    unit = whole * scale
    stored = unit.astype(jnp.bfloat16)
    stored = in_core_order(stored[:seq_dev], stored[seq_dev:], core)

    kept = slab_blocks(stored, chips)
    kept = jnp.concatenate(kept)
    slab = [kept, from_sibling(kept)]
    slab_rows = slab_owner.shape[0]
    earlier = jnp.arange(slab_rows)[:, None] < jnp.arange(slab_rows)[None, :]
    same = slab_owner[:, None] == slab_owner[None, :]
    ranks = jnp.sum((earlier & same).astype(jnp.int32), axis=0)
    owner_place = ring_place(slab_owner // cores, chips)
    seen = lax.rem(owner_place - place - core * (chips // cores) + 2 * chips, chips)
    slots = seen * seqs + lax.rem(slab_owner, cores) * seq_dev + ranks
    moved = (slots[:, None] == jnp.arange(slab_rows)[None, :]).astype(jnp.float32)
    picked = (cands[:, :, None] == jnp.arange(slab_rows)).astype(jnp.float32)
    positive = jnp.dot(picked[:, 0], moved)
    candidate = jnp.dot(jnp.sum(picked, axis=1), moved)
    piece = slab_rows // cores
    pieces = [slice(i * piece, (i + 1) * piece) for i in range(cores)]

    slab_wide = [rows_in.astype(jnp.float32) for rows_in in slab]
    exponent = []
    for rows_in, at in zip(slab_wide, pieces):
        logits = (
            sharpness / embedding * jnp.dot(unit, rows_in.T, precision=lax.Precision.HIGHEST)
        )
        exponent.append(jnp.where(candidate[:, at] > 0.5, jnp.exp(logits), 0.0))
    denominator = sum(jnp.sum(part, axis=-1, keepdims=True) for part in exponent)
    unit_grad = (
        sharpness
        / embedding
        * sum(
            jnp.dot(
                part / denominator - positive[:, at], rows_in, precision=lax.Precision.HIGHEST
            )
            for part, rows_in, at in zip(exponent, slab_wide, pieces)
        )
    )
    inner = jnp.sum(whole * unit_grad, axis=-1, keepdims=True)
    pooled_grad = scale * unit_grad - whole * (scale * scale * scale) * inner / embedding
    pooled_grad = lax.dynamic_slice(pooled_grad, (0, core * half), (seqs, half))
    delta = (pooled_grad / counts[:, None])[:, None, :] * (1.0 - active * active)
    delta = jnp.where(there, delta, 0.0)
    delta = delta.astype(jnp.bfloat16).reshape(seqs * length, half)

    def term(offset, part, delta):
        return lax.dot_general(
            columns(offset, part),
            delta,
            (((0,), (0,)), ((), ())),
            preferred_element_type=jnp.float32,
        )

    if chips <= longest_ring:
        arrived = {}
        late = delta
        for step in range(chips // 2, 0, -1):
            for i, by in ((0, 1), (1, -1), (1, 1), (0, -1)):
                if step == chips // 2 and (i, by) not in ((0, 1), (1, -1)):
                    continue
                total = term(by * step, parts[i], delta)
                if (i, by) in arrived:
                    total = total + arrived[i, by].astype(jnp.float32)
                if step == 1 and i == 0:
                    total = after(copied, total)
                arrived[i, by] = along_ring(total.astype(jnp.bfloat16), by)
            if step == chips // 2:
                late, weights = after(arrived[0, 1], (delta, weights))
                copied = passed_on(weights)
        owns = [term(0, parts[i], late) for i in range(2)]
        arrived[1, 1] = after(owns, arrived[1, 1])
        arrived[0, -1] = after(owns, arrived[0, -1])
        mine, other = [
            owns[i] + arrived[i, 1].astype(jnp.float32) + arrived[i, -1].astype(jnp.float32)
            for i in range(2)
        ]
    else:
        grad = lax.dot_general(
            normed, delta, (((0,), (0,)), ((), ())), preferred_element_type=jnp.float32
        )
        copied = passed_on(weights)
        reduced = lax.psum_scatter(grad, "chip", scatter_dimension=0, tiled=True)
        mine, other = [lax.dynamic_slice(reduced, (i * rows, 0), (rows, half)) for i in parts]
    other = from_sibling(other)
    shard = in_core_order(mine, other, core, axis=1)
    row_square = jnp.mean(shard * shard, axis=1, keepdims=True)
    normalized = shard * lax.rsqrt(row_square + 1e-06)
    result = jnp.where(trainer, normalized, copied.astype(jnp.float32))
    return result[None]


def solution(mesh):
    groups, devices_fsdp = mesh.devices.shape
    finer = Mesh(
        mesh.devices.reshape(groups, devices_fsdp // cores, cores), ("grp", "chip", "core")
    )
    fsdp = ("chip", "core")
    placed = (
        P("grp", fsdp, None, None),
        P("grp", fsdp, None),
        P("grp", fsdp, None),
        P(),
        P(fsdp, None),
        P(),
    )
    return jax.shard_map(
        shards, mesh=finer, in_specs=placed, out_specs=P("grp", fsdp, None), check_vma=False
    )
```

```python
import functools

import jax
import jax.numpy as jnp
from jax import lax
from jax.experimental import pallas as pl
from jax.experimental.pallas import tpu as pltpu
from jax.sharding import Mesh, PartitionSpec as P

sharpness = 20.0
cores = 2
longest_ring = 16
vmem_limit = 16 << 20


def ring_order(chips):
    return list(range(0, chips, 2)) + list(range(1, chips, 2))[::-1]


def ring_place(chip, chips):
    return jnp.where(chip % 2 == 0, chip // 2, chips - 1 - chip // 2)


def ring_chip(place, chips):
    place = lax.rem(place + 2 * chips, chips)
    return jnp.where(place < chips // 2, 2 * place, 2 * (chips - 1 - place) + 1)


def along_ring(block, by):
    order = ring_order(lax.axis_size("chip"))
    pairs = [(chip, order[(i + by) % len(order)]) for i, chip in enumerate(order)]
    return lax.ppermute(block, "chip", pairs)


def after(first, block):
    return lax.optimization_barrier((first, block))[1]


def passed_on(weights):
    return lax.ppermute(weights.astype(jnp.bfloat16), "grp", [(0, 1)])


def cut(array, axis, start, size):
    starts = [0] * array.ndim
    starts[axis] = start
    sizes = list(array.shape)
    sizes[axis] = size
    return lax.dynamic_slice(array, starts, sizes, allow_negative_indices=False)


def from_sibling(block):
    return lax.ppermute(block, "core", [(0, 1), (1, 0)])


def slab_blocks(stored, chips):
    order = ring_order(chips)
    kept = []
    for j in range(chips // cores):
        pairs = []
        for i, chip in enumerate(order):
            for c in range(cores):
                source = order[(i + j + c * (chips // cores)) % chips]
                pairs.append(((chips + source) * cores + c, chip * cores + c))
        kept.append(lax.ppermute(stored, ("grp", "chip", "core"), pairs))
    return kept


def in_core_order(mine, other, first_core, axis=0):
    return jnp.where(
        first_core,
        jnp.concatenate([mine, other], axis=axis),
        jnp.concatenate([other, mine], axis=axis),
    )


def normalize_kernel(seqs, chunk, mine_ref, other_ref, gain_ref, out_ref):
    length = mine_ref.shape[1]

    def run(ref):
        @pl.loop(0, length // chunk)
        def _(i):
            at = pl.ds(pl.multiple_of(i * chunk, chunk), chunk)
            wide = ref[0, at, :].astype(jnp.float32)
            mean_square = jnp.mean(wide * wide, axis=-1, keepdims=True)
            wide = wide * lax.rsqrt(mean_square + 1e-05) * gain_ref[...]
            out_ref[at, :] = wide.astype(jnp.bfloat16)

    @pl.when(pl.program_id(0) < seqs)
    def _():
        run(mine_ref)

    @pl.when(pl.program_id(0) >= seqs)
    def _():
        run(other_ref)


def normalize_both(mine, other, gain):
    seqs, length, width = mine.shape
    tokens = 2 * seqs * length
    return pl.pallas_call(
        functools.partial(normalize_kernel, seqs, 16),
        grid=(2 * seqs,),
        in_specs=[
            pl.BlockSpec((1, length, width), lambda i: (jnp.minimum(i, seqs - 1), 0, 0)),
            pl.BlockSpec((1, length, width), lambda i: (jnp.maximum(i - seqs, 0), 0, 0)),
            pl.BlockSpec((1, width), lambda i: (0, 0)),
        ],
        out_specs=pl.BlockSpec((length, width), lambda i: (i, 0)),
        out_shape=jax.ShapeDtypeStruct((tokens, width), jnp.bfloat16),
        compiler_params=pltpu.CompilerParams(vmem_limit_bytes=vmem_limit),
        cost_estimate=pl.CostEstimate(
            flops=6 * tokens * width, bytes_accessed=4 * tokens * width, transcendentals=tokens
        ),
    )(mine, other, gain[None])


def shards(token_states, token_ids, master, gain, cand_ids, slab_owner):
    trainer = lax.axis_index("grp") == 0
    chips = lax.axis_size("chip")
    chip = lax.axis_index("chip")
    core = lax.axis_index("core")
    place = ring_place(chip, chips)
    states = token_states[0]
    seq_dev, length, width = states.shape
    rows, embedding = master.shape[1:]
    half = embedding // cores
    seqs = cores * seq_dev

    first_core = core == 0
    shift = place + core * (chips // cores)
    own_columns, given_columns = core * half, (1 - core) * half
    parts = (core, 1 - core)
    span = chips // 2 if chips <= longest_ring else 0
    starts = {
        (offset, i): (ring_chip(place + offset, chips) * cores + parts[i]) * rows
        for offset in range(-span, span + 1)
        for i in range(2)
    }
    scalars = [first_core, shift, own_columns, given_columns, trainer, *starts.values()]
    weights, *scalars = lax.optimization_barrier([master[0], *scalars])
    first_core, shift, own_columns, given_columns, trainer, *firsts = scalars
    starts = dict(zip(starts, firsts))
    own = cut(weights, 1, own_columns, half).astype(jnp.bfloat16)
    given = cut(weights, 1, given_columns, half).astype(jnp.bfloat16)
    sibling = from_sibling(given)

    other_states = from_sibling(states)
    sent = [(0, 1), (0, -1), (1, 1), (1, -1)]
    ids = token_ids[0]
    if chips <= longest_ring:
        moving = {(i, by): along_ring((own, sibling)[i], by) for i, by in sent}
        cand_ids, slab_owner = after(moving[1, 1], (cand_ids, slab_owner))
    normed = normalize_both(states, other_states, gain)
    slab_rows = slab_owner.shape[0]
    slab_ids = jnp.arange(slab_rows, dtype=jnp.int32)[None, :]
    picked = [
        (cand_ids[:, j : j + 1] == slab_ids).astype(jnp.int32) for j in range(cand_ids.shape[1])
    ]
    ids = jnp.concatenate([ids, sum(picked), picked[0]], axis=1)
    ids = jnp.concatenate([ids, from_sibling(ids)])
    lengths = jnp.sum((ids[:, :length] != 0).astype(jnp.int32), axis=1)
    counts = lengths.astype(jnp.float32)
    masks = ids[:, length:].astype(jnp.float32)

    def columns(offset, i):
        return cut(normed, 1, starts[offset, i], rows)

    def product(offset, i, block):
        return jnp.dot(columns(offset, i), block, preferred_element_type=jnp.float32)

    if chips <= longest_ring:
        total = product(0, 0, own) + product(0, 1, sibling)
        sums = {}
        for step in range(1, chips // 2 + 1):
            last = step == chips // 2
            for i, by in [(0, 1), (1, -1)] if last else sent:
                if step > 1:
                    if last and step > 2:
                        moving[i, by] = after(sums[1 + i], moving[i, by])
                    elif step == 3 and i == 1:
                        moving[i, by] = after(normed, moving[i, by])
                    moving[i, by] = along_ring(moving[i, by], by)
                total = total + product(-by * step, i, moving[i, by])
            sums[step] = total
    else:
        both = in_core_order(own, sibling, first_core)
        gathered = lax.all_gather(both, "chip", axis=0, tiled=True)
        total = jnp.dot(normed, gathered, preferred_element_type=jnp.float32)

    active = jnp.tanh(total).reshape(seqs, length, half)
    there = jnp.arange(length)[None, :, None] < lengths[:, None, None]
    pooled = jnp.sum(jnp.where(there, active, 0.0), axis=1) / counts[:, None]
    pooled_other = from_sibling(pooled)
    pooled_other = jnp.concatenate([pooled_other[seq_dev:], pooled_other[:seq_dev]])
    whole = in_core_order(pooled, pooled_other, first_core, axis=1)
    pooled_square = jnp.mean(whole * whole, axis=-1, keepdims=True)
    scale = lax.rsqrt(pooled_square + 1e-06)
    unit = whole * scale
    stored = unit.astype(jnp.bfloat16)
    stored = in_core_order(stored[:seq_dev], stored[seq_dev:], first_core)

    kept = slab_blocks(stored, chips)
    kept = jnp.concatenate(kept)
    slab = [kept, from_sibling(kept)]
    earlier = jnp.arange(slab_rows)[:, None] < jnp.arange(slab_rows)[None, :]
    same = slab_owner[:, None] == slab_owner[None, :]
    ranks = jnp.sum((earlier & same).astype(jnp.int32), axis=0)
    owner_place = ring_place(slab_owner // cores, chips)
    seen = lax.rem(owner_place - shift + 2 * chips, chips)
    slots = seen * seqs + lax.rem(slab_owner, cores) * seq_dev + ranks
    moved = (slots[:, None] == jnp.arange(slab_rows)[None, :]).astype(jnp.float32)
    candidate = jnp.dot(masks[:, :slab_rows], moved)
    positive = jnp.dot(masks[:, slab_rows:], moved)
    piece = slab_rows // cores
    pieces = [slice(i * piece, (i + 1) * piece) for i in range(cores)]

    slab_wide = [rows_in.astype(jnp.float32) for rows_in in slab]
    exponent = []
    for rows_in, at in zip(slab_wide, pieces):
        logits = (
            sharpness / embedding * jnp.dot(unit, rows_in.T, precision=lax.Precision.HIGHEST)
        )
        exponent.append(jnp.where(candidate[:, at] > 0.5, jnp.exp(logits), 0.0))
    denominator = sum(jnp.sum(part, axis=-1, keepdims=True) for part in exponent)
    unit_grad = (
        sharpness
        / embedding
        * sum(
            jnp.dot(
                part / denominator - positive[:, at], rows_in, precision=lax.Precision.HIGHEST
            )
            for part, rows_in, at in zip(exponent, slab_wide, pieces)
        )
    )
    inner = jnp.sum(whole * unit_grad, axis=-1, keepdims=True)
    pooled_grad = scale * unit_grad - whole * (scale * scale * scale) * inner / embedding
    pooled_grad = cut(pooled_grad, 1, own_columns, half)
    delta = (pooled_grad / counts[:, None])[:, None, :] * (1.0 - active * active)
    delta = jnp.where(there, delta, 0.0)
    delta = delta.astype(jnp.bfloat16).reshape(seqs * length, half)

    def term(offset, i, delta):
        return lax.dot_general(
            columns(offset, i),
            delta,
            (((0,), (0,)), ((), ())),
            preferred_element_type=jnp.float32,
        )

    if chips <= longest_ring:
        arrived = {}
        late = delta
        for step in range(chips // 2, 0, -1):
            for i, by in ((0, 1), (1, -1), (1, 1), (0, -1)):
                if step == chips // 2 and (i, by) not in ((0, 1), (1, -1)):
                    continue
                total = term(by * step, i, delta)
                if (i, by) in arrived:
                    total = total + arrived[i, by].astype(jnp.float32)
                if step == 1 and i == 0:
                    total = after(copied, total)
                arrived[i, by] = along_ring(total.astype(jnp.bfloat16), by)
            if step == chips // 2:
                late, weights = after(arrived[0, 1], (delta, weights))
                copied = passed_on(weights)
        owns = [term(0, i, late) for i in range(2)]
        arrived[1, 1] = after(owns, arrived[1, 1])
        arrived[0, -1] = after(owns, arrived[0, -1])
        mine, other = [
            owns[i] + arrived[i, 1].astype(jnp.float32) + arrived[i, -1].astype(jnp.float32)
            for i in range(2)
        ]
    else:
        grad = lax.dot_general(
            normed, delta, (((0,), (0,)), ((), ())), preferred_element_type=jnp.float32
        )
        copied = passed_on(weights)
        reduced = lax.psum_scatter(grad, "chip", scatter_dimension=0, tiled=True)
        mine, other = [cut(reduced, 0, part * rows, rows) for part in parts]
    other = from_sibling(other)
    shard = in_core_order(mine, other, first_core, axis=1)
    row_square = jnp.mean(shard * shard, axis=1, keepdims=True)
    normalized = shard * lax.rsqrt(row_square + 1e-06)
    result = jnp.where(trainer, normalized, copied.astype(jnp.float32))
    return result[None]


def solution(mesh):
    groups, devices_fsdp = mesh.devices.shape
    finer = Mesh(
        mesh.devices.reshape(groups, devices_fsdp // cores, cores), ("grp", "chip", "core")
    )
    fsdp = ("chip", "core")
    placed = (
        P("grp", fsdp, None, None),
        P("grp", fsdp, None),
        P("grp", fsdp, None),
        P(),
        P(fsdp, None),
        P(),
    )
    return jax.shard_map(
        shards, mesh=finer, in_specs=placed, out_specs=P("grp", fsdp, None), check_vma=False
    )
```

```python
import functools

import jax
import jax.numpy as jnp
from jax import lax
from jax.experimental import pallas as pl
from jax.experimental.pallas import tpu as pltpu
from jax.sharding import Mesh, PartitionSpec as P

sharpness = 20.0
cores = 2
longest_ring = 16
vmem_limit = 12 << 20


def ring_order(chips):
    return list(range(0, chips, 2)) + list(range(1, chips, 2))[::-1]


def ring_place(chip, chips):
    return jnp.where(chip % 2 == 0, chip // 2, chips - 1 - chip // 2)


def ring_chip(place, chips):
    place = lax.rem(place + 2 * chips, chips)
    return jnp.where(place < chips // 2, 2 * place, 2 * (chips - 1 - place) + 1)


def along_ring(block, by):
    order = ring_order(lax.axis_size("chip"))
    pairs = [(chip, order[(i + by) % len(order)]) for i, chip in enumerate(order)]
    return lax.ppermute(block, "chip", pairs)


def after(first, block):
    return lax.optimization_barrier((first, block))[1]


def passed_on(weights):
    return lax.ppermute(weights.astype(jnp.bfloat16), "grp", [(0, 1)])


def cut(array, axis, start, size):
    starts = [0] * array.ndim
    starts[axis] = start
    sizes = list(array.shape)
    sizes[axis] = size
    return lax.dynamic_slice(array, starts, sizes, allow_negative_indices=False)


def from_sibling(block):
    return lax.ppermute(block, "core", [(0, 1), (1, 0)])


def slab_blocks(stored, chips):
    order = ring_order(chips)
    kept = []
    for j in range(chips // cores):
        pairs = []
        for i, chip in enumerate(order):
            for c in range(cores):
                source = order[(i + j + c * (chips // cores)) % chips]
                pairs.append(((chips + source) * cores + c, chip * cores + c))
        kept.append(lax.ppermute(stored, ("grp", "chip", "core"), pairs))
    return kept


def in_core_order(mine, other, first_core, axis=0):
    return jnp.where(
        first_core,
        jnp.concatenate([mine, other], axis=axis),
        jnp.concatenate([other, mine], axis=axis),
    )


def normalize_kernel(chunk, states_ref, gain_ref, *refs):
    out_ref = refs[-1]

    @pl.loop(0, states_ref.shape[1] // chunk)
    def _(i):
        at = pl.ds(pl.multiple_of(i * chunk, chunk), chunk)
        wide = states_ref[0, at, :].astype(jnp.float32)
        mean_square = jnp.mean(wide * wide, axis=-1, keepdims=True)
        wide = wide * lax.rsqrt(mean_square + 1e-05) * gain_ref[...]
        out_ref[at, :] = wide.astype(jnp.bfloat16)


def normalize(states, gain, part, filled=None):
    seqs, length, width = states.shape
    tokens = seqs * length
    in_specs = [
        pl.BlockSpec((1, length, width), lambda i: (i, 0, 0)),
        pl.BlockSpec((1, width), lambda i: (0, 0)),
    ]
    operands = [states, gain[None]]
    if filled is not None:
        in_specs.append(pl.BlockSpec(memory_space=pl.ANY))
        operands.append(filled)
    return pl.pallas_call(
        functools.partial(normalize_kernel, 16),
        grid=(seqs,),
        in_specs=in_specs,
        out_specs=pl.BlockSpec((length, width), lambda i: (part * seqs + i, 0)),
        out_shape=jax.ShapeDtypeStruct((cores * tokens, width), jnp.bfloat16),
        input_output_aliases={} if filled is None else {2: 0},
        compiler_params=pltpu.CompilerParams(vmem_limit_bytes=vmem_limit),
        cost_estimate=pl.CostEstimate(
            flops=6 * tokens * width, bytes_accessed=4 * tokens * width, transcendentals=tokens
        ),
    )(*operands)


def shards(token_states, token_ids, master, gain, cand_ids, slab_owner):
    trainer = lax.axis_index("grp") == 0
    chips = lax.axis_size("chip")
    chip = lax.axis_index("chip")
    core = lax.axis_index("core")
    place = ring_place(chip, chips)
    states = token_states[0]
    seq_dev, length, width = states.shape
    rows, embedding = master.shape[1:]
    half = embedding // cores
    seqs = cores * seq_dev

    first_core = core == 0
    shift = place + core * (chips // cores)
    own_columns, given_columns = core * half, (1 - core) * half
    parts = (core, 1 - core)
    span = chips // 2 if chips <= longest_ring else 0
    starts = {
        (offset, i): (ring_chip(place + offset, chips) * cores + parts[i]) * rows
        for offset in range(-span, span + 1)
        for i in range(2)
    }
    scalars = [first_core, shift, own_columns, given_columns, trainer, *starts.values()]
    weights, *scalars = lax.optimization_barrier([master[0], *scalars])
    first_core, shift, own_columns, given_columns, trainer, *firsts = scalars
    starts = dict(zip(starts, firsts))
    own = cut(weights, 1, own_columns, half).astype(jnp.bfloat16)
    given = cut(weights, 1, given_columns, half).astype(jnp.bfloat16)
    sibling = from_sibling(given)

    other_states = from_sibling(states)
    sent = [(0, 1), (0, -1), (1, 1), (1, -1)]
    normed_own = normalize(states, gain, 0)
    normed = normalize(other_states, gain, 1, normed_own)
    if chips <= longest_ring:
        moving = {(i, by): along_ring((own, sibling)[i], by) for i, by in sent}

    def columns(offset, i):
        return cut(normed, 1, starts[offset, i], rows)

    def product(offset, i, block):
        return jnp.dot(columns(offset, i), block, preferred_element_type=jnp.float32)

    if chips <= longest_ring:
        total = product(0, 0, own) + product(0, 1, sibling)
        sums = {}
        for step in range(1, chips // 2 + 1):
            last = step == chips // 2
            for i, by in [(0, 1), (1, -1)] if last else sent:
                if step > 1:
                    if last and step > 2:
                        moving[i, by] = after(sums[1 + i], moving[i, by])
                    elif step in (2, 3) and i == 1:
                        moving[i, by] = after((normed_own, normed)[step - 2], moving[i, by])
                    moving[i, by] = along_ring(moving[i, by], by)
                total = total + product(-by * step, i, moving[i, by])
            sums[step] = total
            if step == chips // 2 - 1:
                cand_ids, slab_owner = after(sums[1], (cand_ids, slab_owner))
    else:
        both = in_core_order(own, sibling, first_core)
        gathered = lax.all_gather(both, "chip", axis=0, tiled=True)
        total = jnp.dot(normed, gathered, preferred_element_type=jnp.float32)

    slab_rows = slab_owner.shape[0]
    slab_ids = jnp.arange(slab_rows, dtype=jnp.int32)[None, :]
    picked = [
        (cand_ids[:, j : j + 1] == slab_ids).astype(jnp.int32) for j in range(cand_ids.shape[1])
    ]
    ids = jnp.concatenate([token_ids[0], sum(picked), picked[0]], axis=1)
    ids = jnp.concatenate([ids, from_sibling(ids)])
    lengths = jnp.sum((ids[:, :length] != 0).astype(jnp.int32), axis=1)
    counts = lengths.astype(jnp.float32)
    masks = ids[:, length:].astype(jnp.float32)

    active = jnp.tanh(total).reshape(seqs, length, half)
    there = jnp.arange(length)[None, :, None] < lengths[:, None, None]
    pooled = jnp.sum(jnp.where(there, active, 0.0), axis=1) / counts[:, None]
    pooled_other = from_sibling(pooled)
    pooled_other = jnp.concatenate([pooled_other[seq_dev:], pooled_other[:seq_dev]])
    whole = in_core_order(pooled, pooled_other, first_core, axis=1)
    pooled_square = jnp.mean(whole * whole, axis=-1, keepdims=True)
    scale = lax.rsqrt(pooled_square + 1e-06)
    unit = whole * scale
    stored = unit.astype(jnp.bfloat16)
    stored = in_core_order(stored[:seq_dev], stored[seq_dev:], first_core)

    kept = slab_blocks(stored, chips)
    kept = jnp.concatenate(kept)
    slab = [kept, from_sibling(kept)]
    earlier = jnp.arange(slab_rows)[:, None] < jnp.arange(slab_rows)[None, :]
    same = slab_owner[:, None] == slab_owner[None, :]
    ranks = jnp.sum((earlier & same).astype(jnp.int32), axis=0)
    owner_place = ring_place(slab_owner // cores, chips)
    seen = lax.rem(owner_place - shift + 2 * chips, chips)
    slots = seen * seqs + lax.rem(slab_owner, cores) * seq_dev + ranks
    moved = (slots[:, None] == jnp.arange(slab_rows)[None, :]).astype(jnp.float32)
    candidate = jnp.dot(masks[:, :slab_rows], moved)
    positive = jnp.dot(masks[:, slab_rows:], moved)
    piece = slab_rows // cores
    pieces = [slice(i * piece, (i + 1) * piece) for i in range(cores)]

    slab_wide = [rows_in.astype(jnp.float32) for rows_in in slab]
    exponent = []
    for rows_in, at in zip(slab_wide, pieces):
        logits = (
            sharpness / embedding * jnp.dot(unit, rows_in.T, precision=lax.Precision.HIGHEST)
        )
        exponent.append(jnp.where(candidate[:, at] > 0.5, jnp.exp(logits), 0.0))
    denominator = sum(jnp.sum(part, axis=-1, keepdims=True) for part in exponent)
    unit_grad = (
        sharpness
        / embedding
        * sum(
            jnp.dot(
                part / denominator - positive[:, at], rows_in, precision=lax.Precision.HIGHEST
            )
            for part, rows_in, at in zip(exponent, slab_wide, pieces)
        )
    )
    inner = jnp.sum(whole * unit_grad, axis=-1, keepdims=True)
    pooled_grad = scale * unit_grad - whole * (scale * scale * scale) * inner / embedding
    pooled_grad = cut(pooled_grad, 1, own_columns, half)
    delta = (pooled_grad / counts[:, None])[:, None, :] * (1.0 - active * active)
    delta = jnp.where(there, delta, 0.0)
    delta = delta.astype(jnp.bfloat16).reshape(seqs * length, half)

    def term(offset, i, delta):
        return lax.dot_general(
            columns(offset, i),
            delta,
            (((0,), (0,)), ((), ())),
            preferred_element_type=jnp.float32,
        )

    if chips <= longest_ring:
        arrived = {}
        late = delta
        early = delta
        for step in range(chips // 2, 0, -1):
            for i, by in ((0, 1), (1, -1), (1, 1), (0, -1)):
                if step == chips // 2 and (i, by) not in ((0, 1), (1, -1)):
                    continue
                total = term(by * step, i, delta)
                if (i, by) in arrived:
                    total = total + arrived[i, by].astype(jnp.float32)
                if step == 1 and i == 0:
                    total = after(copied, total)
                total = total.astype(jnp.bfloat16)
                if step == chips // 2:
                    early = after(total, early)
                arrived[i, by] = along_ring(total, by)
            if step == chips // 2:
                late, weights = after(arrived[0, 1], (delta, weights))
                copied = passed_on(weights)
        owns = [term(0, i, late) for i in range(2)]
        arrived[1, 1] = after(owns, arrived[1, 1])
        arrived[0, -1] = after(owns, arrived[0, -1])
        mine, other = [
            owns[i] + arrived[i, 1].astype(jnp.float32) + arrived[i, -1].astype(jnp.float32)
            for i in range(2)
        ]
    else:
        grad = lax.dot_general(
            normed, delta, (((0,), (0,)), ((), ())), preferred_element_type=jnp.float32
        )
        copied = passed_on(weights)
        reduced = lax.psum_scatter(grad, "chip", scatter_dimension=0, tiled=True)
        mine, other = [cut(reduced, 0, part * rows, rows) for part in parts]
    other = from_sibling(other)
    shard = in_core_order(mine, other, first_core, axis=1)
    row_square = jnp.mean(shard * shard, axis=1, keepdims=True)
    normalized = shard * lax.rsqrt(row_square + 1e-06)
    result = jnp.where(trainer, normalized, copied.astype(jnp.float32))
    return result[None]


def solution(mesh):
    groups, devices_fsdp = mesh.devices.shape
    finer = Mesh(
        mesh.devices.reshape(groups, devices_fsdp // cores, cores), ("grp", "chip", "core")
    )
    fsdp = ("chip", "core")
    placed = (
        P("grp", fsdp, None, None),
        P("grp", fsdp, None),
        P("grp", fsdp, None),
        P(),
        P(fsdp, None),
        P(),
    )
    return jax.shard_map(
        shards, mesh=finer, in_specs=placed, out_specs=P("grp", fsdp, None), check_vma=False
    )
```

```python
import functools

import jax
import jax.numpy as jnp
from jax import lax
from jax.experimental import pallas as pl
from jax.experimental.pallas import tpu as pltpu
from jax.sharding import Mesh, PartitionSpec as P

sharpness = 20.0
cores = 2
longest_ring = 16
vmem_limit = 12 << 20


def ring_order(chips):
    return list(range(0, chips, 2)) + list(range(1, chips, 2))[::-1]


def ring_place(chip, chips):
    return jnp.where(chip % 2 == 0, chip // 2, chips - 1 - chip // 2)


def ring_chip(place, chips):
    place = lax.rem(place + 2 * chips, chips)
    return jnp.where(place < chips // 2, 2 * place, 2 * (chips - 1 - place) + 1)


def along_ring(block, by):
    order = ring_order(lax.axis_size("chip"))
    pairs = [(chip, order[(i + by) % len(order)]) for i, chip in enumerate(order)]
    return lax.ppermute(block, "chip", pairs)


def after(first, block):
    return lax.optimization_barrier((first, block))[1]


def to_refresher(block):
    return lax.ppermute(block, "grp", [(0, 1)])


def passed_on(weights):
    return to_refresher(weights.astype(jnp.bfloat16))


def odd_columns_kernel(rows, normed_ref, out_ref, sems):
    tokens = out_ref.shape[0]
    copies = []
    for i in range(out_ref.shape[1] // rows):
        source = normed_ref.at[pl.ds(0, tokens), pl.ds((cores * i + 1) * rows, rows)]
        target = out_ref.at[:, pl.ds(i * rows, rows)]
        copies.append(pltpu.make_async_copy(source, target, sems.at[i]))
    for copy in copies:
        copy.start()
    for copy in copies:
        copy.wait()


def odd_columns(normed, rows):
    tokens, width = normed.shape[0] // cores, normed.shape[1]
    return pl.pallas_call(
        functools.partial(odd_columns_kernel, rows),
        in_specs=[pl.BlockSpec(memory_space=pl.ANY)],
        out_specs=pl.BlockSpec(memory_space=pl.ANY),
        out_shape=jax.ShapeDtypeStruct((tokens, width // cores), jnp.bfloat16),
        scratch_shapes=[pltpu.SemaphoreType.DMA((width // (cores * rows),))],
        compiler_params=pltpu.CompilerParams(vmem_limit_bytes=vmem_limit),
        cost_estimate=pl.CostEstimate(
            flops=0, bytes_accessed=2 * tokens * width, transcendentals=0
        ),
    )(normed)


def shares_kernel(rows, flag_ref, normed_ref, own_ref, other_ref, out_ref, sems):
    tokens = own_ref.shape[0]
    copies = []
    for i in range(out_ref.shape[1] // rows):
        source = normed_ref.at[:, pl.ds(cores * i * rows, rows)]
        target = out_ref.at[:, pl.ds(i * rows, rows)]
        copies.append(pltpu.make_async_copy(source, target, sems.at[i]))
    received = [
        pltpu.make_async_copy(ref, out_ref.at[pl.ds(i * tokens, tokens), :], sems.at[i])
        for i, ref in enumerate((own_ref, other_ref))
    ]

    def run(group):
        for copy in group:
            copy.start()
        for copy in group:
            copy.wait()

    pl.when(flag_ref[0] == 1)(functools.partial(run, copies))
    pl.when(flag_ref[0] != 1)(functools.partial(run, received))


def shares(normed, own, other, flag, rows):
    tokens, width = normed.shape
    anywhere = pl.BlockSpec(memory_space=pl.ANY)
    return pl.pallas_call(
        functools.partial(shares_kernel, rows),
        in_specs=[pl.BlockSpec(memory_space=pltpu.SMEM)] + [anywhere] * 3,
        out_specs=anywhere,
        out_shape=jax.ShapeDtypeStruct((tokens, width // cores), jnp.bfloat16),
        scratch_shapes=[pltpu.SemaphoreType.DMA((width // (cores * rows),))],
        compiler_params=pltpu.CompilerParams(vmem_limit_bytes=vmem_limit),
        cost_estimate=pl.CostEstimate(
            flops=0, bytes_accessed=2 * tokens * width, transcendentals=0
        ),
    )(flag, normed, own, other)


def cut(array, axis, start, size):
    starts = [0] * array.ndim
    starts[axis] = start
    sizes = list(array.shape)
    sizes[axis] = size
    return lax.dynamic_slice(array, starts, sizes, allow_negative_indices=False)


def from_sibling(block):
    return lax.ppermute(block, "core", [(0, 1), (1, 0)])


def slab_blocks(stored, chips):
    order = ring_order(chips)
    kept = []
    for j in range(chips // cores):
        pairs = []
        for i, chip in enumerate(order):
            for c in range(cores):
                source = order[(i + j + c * (chips // cores)) % chips]
                pairs.append(((chips + source) * cores + c, chip * cores + c))
        kept.append(lax.ppermute(stored, ("grp", "chip", "core"), pairs))
    return kept


def in_core_order(mine, other, first_core, axis=0):
    return jnp.where(
        first_core,
        jnp.concatenate([mine, other], axis=axis),
        jnp.concatenate([other, mine], axis=axis),
    )


def normalize_kernel(chunk, states_ref, gain_ref, *refs):
    out_ref = refs[-1]

    @pl.loop(0, states_ref.shape[1] // chunk)
    def _(i):
        at = pl.ds(pl.multiple_of(i * chunk, chunk), chunk)
        wide = states_ref[0, at, :].astype(jnp.float32)
        mean_square = jnp.mean(wide * wide, axis=-1, keepdims=True)
        wide = wide * lax.rsqrt(mean_square + 1e-05) * gain_ref[...]
        out_ref[at, :] = wide.astype(jnp.bfloat16)


def normalize(states, gain, part, filled=None):
    seqs, length, width = states.shape
    tokens = seqs * length
    in_specs = [
        pl.BlockSpec((1, length, width), lambda i: (i, 0, 0)),
        pl.BlockSpec((1, width), lambda i: (0, 0)),
    ]
    operands = [states, gain[None]]
    if filled is not None:
        in_specs.append(pl.BlockSpec(memory_space=pl.ANY))
        operands.append(filled)
    return pl.pallas_call(
        functools.partial(normalize_kernel, 16),
        grid=(seqs,),
        in_specs=in_specs,
        out_specs=pl.BlockSpec((length, width), lambda i: (part * seqs + i, 0)),
        out_shape=jax.ShapeDtypeStruct((cores * tokens, width), jnp.bfloat16),
        input_output_aliases={} if filled is None else {2: 0},
        compiler_params=pltpu.CompilerParams(vmem_limit_bytes=vmem_limit),
        cost_estimate=pl.CostEstimate(
            flops=6 * tokens * width, bytes_accessed=4 * tokens * width, transcendentals=tokens
        ),
    )(*operands)


def shards(token_states, token_ids, master, gain, cand_ids, slab_owner):
    trainer = lax.axis_index("grp") == 0
    chips = lax.axis_size("chip")
    chip = lax.axis_index("chip")
    core = lax.axis_index("core")
    place = ring_place(chip, chips)
    states = token_states[0]
    seq_dev, length, width = states.shape
    rows, embedding = master.shape[1:]
    half = embedding // cores
    seqs = cores * seq_dev

    first_core = core == 0
    shift = place + core * (chips // cores)
    own_columns, given_columns = core * half, (1 - core) * half
    parts = (core, 1 - core)
    span = chips // 2 if chips <= longest_ring else 0
    starts = {
        (offset, i): (ring_chip(place + offset, chips) * cores + parts[i]) * rows
        for offset in range(-span, span + 1)
        for i in range(2)
    }
    share_starts = {
        offset: ring_chip(place + offset, chips) * rows for offset in range(-span, span + 1)
    }
    flag = trainer.astype(jnp.int32)[None]
    scalars = [first_core, shift, own_columns, given_columns, trainer, flag]
    tables = [list(starts.values()), list(share_starts.values())]
    weights, scalars, tables = lax.optimization_barrier((master[0], scalars, tables))
    first_core, shift, own_columns, given_columns, trainer, flag = scalars
    starts = dict(zip(starts, tables[0]))
    share_starts = dict(zip(share_starts, tables[1]))
    own = cut(weights, 1, own_columns, half).astype(jnp.bfloat16)
    given = cut(weights, 1, given_columns, half).astype(jnp.bfloat16)
    sibling = from_sibling(given)

    other_states = from_sibling(states)
    sent = [(0, 1), (0, -1), (1, 1), (1, -1)]
    normed_own = normalize(states, gain, 0)
    odd = odd_columns(normed_own, rows)
    normed = normalize(other_states, gain, 1, filled=after(odd, normed_own))
    odd = to_refresher(odd)
    if chips <= longest_ring:
        moving = {(i, by): along_ring((own, sibling)[i], by) for i, by in sent}

    def columns(offset, i):
        return cut(normed, 1, starts[offset, i], rows)

    def product(offset, i, block):
        return jnp.dot(columns(offset, i), block, preferred_element_type=jnp.float32)

    if chips <= longest_ring:
        total = product(0, 0, own) + product(0, 1, sibling)
        sums = {}
        for step in range(1, chips // 2 + 1):
            last = step == chips // 2
            for i, by in [(0, 1), (1, -1)] if last else sent:
                if step > 1:
                    if last and step > 2:
                        moving[i, by] = after(sums[1 + i], moving[i, by])
                    elif step in (2, 3) and i == 1:
                        moving[i, by] = after((normed_own, normed)[step - 2], moving[i, by])
                    moving[i, by] = along_ring(moving[i, by], by)
                total = total + product(-by * step, i, moving[i, by])
            sums[step] = total
            if step == chips // 2 - 1:
                cand_ids, slab_owner = after(sums[1], (cand_ids, slab_owner))
    else:
        both = in_core_order(own, sibling, first_core)
        gathered = lax.all_gather(both, "chip", axis=0, tiled=True)
        total = jnp.dot(normed, gathered, preferred_element_type=jnp.float32)

    slab_rows = slab_owner.shape[0]
    slab_ids = jnp.arange(slab_rows, dtype=jnp.int32)[None, :]
    picked = [
        (cand_ids[:, j : j + 1] == slab_ids).astype(jnp.int32) for j in range(cand_ids.shape[1])
    ]
    ids = jnp.concatenate([token_ids[0], sum(picked), picked[0]], axis=1)
    ids = jnp.concatenate([ids, from_sibling(ids)])
    lengths = jnp.sum((ids[:, :length] != 0).astype(jnp.int32), axis=1)
    counts = lengths.astype(jnp.float32)
    masks = ids[:, length:].astype(jnp.float32)

    active = jnp.tanh(total).reshape(seqs, length, half)
    there = jnp.arange(length)[None, :, None] < lengths[:, None, None]
    pooled = jnp.sum(jnp.where(there, active, 0.0), axis=1) / counts[:, None]
    slope = jnp.where(there, 1.0 - active * active, 0.0).reshape(seqs * length, half)
    slope_sent = to_refresher(slope.astype(jnp.bfloat16))
    odd = after(pooled, odd)
    pooled_other = from_sibling(pooled)
    pooled_other = jnp.concatenate([pooled_other[seq_dev:], pooled_other[:seq_dev]])
    whole = in_core_order(pooled, pooled_other, first_core, axis=1)
    pooled_square = jnp.mean(whole * whole, axis=-1, keepdims=True)
    scale = lax.rsqrt(pooled_square + 1e-06)
    unit = whole * scale
    stored = unit.astype(jnp.bfloat16)
    stored = in_core_order(stored[:seq_dev], stored[seq_dev:], first_core)

    kept = slab_blocks(stored, chips)
    kept = jnp.concatenate(kept)
    slab = [kept, from_sibling(kept)]
    earlier = jnp.arange(slab_rows)[:, None] < jnp.arange(slab_rows)[None, :]
    same = slab_owner[:, None] == slab_owner[None, :]
    ranks = jnp.sum((earlier & same).astype(jnp.int32), axis=0)
    owner_place = ring_place(slab_owner // cores, chips)
    seen = lax.rem(owner_place - shift + 2 * chips, chips)
    slots = seen * seqs + lax.rem(slab_owner, cores) * seq_dev + ranks
    moved = (slots[:, None] == jnp.arange(slab_rows)[None, :]).astype(jnp.float32)
    candidate = jnp.dot(masks[:, :slab_rows], moved)
    positive = jnp.dot(masks[:, slab_rows:], moved)
    piece = slab_rows // cores
    pieces = [slice(i * piece, (i + 1) * piece) for i in range(cores)]

    slab_wide = [rows_in.astype(jnp.float32) for rows_in in slab]
    exponent = []
    for rows_in, at in zip(slab_wide, pieces):
        logits = (
            sharpness / embedding * jnp.dot(unit, rows_in.T, precision=lax.Precision.HIGHEST)
        )
        exponent.append(jnp.where(candidate[:, at] > 0.5, jnp.exp(logits), 0.0))
    denominator = sum(jnp.sum(part, axis=-1, keepdims=True) for part in exponent)
    unit_grad = (
        sharpness
        / embedding
        * sum(
            jnp.dot(
                part / denominator - positive[:, at], rows_in, precision=lax.Precision.HIGHEST
            )
            for part, rows_in, at in zip(exponent, slab_wide, pieces)
        )
    )
    inner = jnp.sum(whole * unit_grad, axis=-1, keepdims=True)
    pooled_grad = scale * unit_grad - whole * (scale * scale * scale) * inner / embedding
    pooled_grad = cut(pooled_grad, 1, own_columns, half)
    weighted = pooled_grad / counts[:, None]
    if chips <= longest_ring:
        share = shares(normed, odd, from_sibling(odd), flag, rows)
        weighted = jnp.where(trainer, weighted, to_refresher(weighted))
        slope = jnp.where(trainer, slope, slope_sent.astype(jnp.float32))
        delta = weighted[:, None, :] * slope.reshape(seqs, length, half)
        delta = delta.astype(jnp.bfloat16).reshape(seqs * length, half)
        sub = half // 2

        def term(offset, i, delta):
            return lax.dot_general(
                cut(share, 1, share_starts[offset], rows),
                delta[:, i * sub : (i + 1) * sub],
                (((0,), (0,)), ((), ())),
                preferred_element_type=jnp.float32,
            )

        arrived = {}
        early = late = delta
        for step in range(chips // 2, 0, -1):
            for i, by in ((0, 1), (1, -1), (1, 1), (0, -1)):
                if step == chips // 2 and (i, by) not in ((0, 1), (1, -1)):
                    continue
                total = term(by * step, i, early if step > chips // 2 - 2 else late)
                if (i, by) in arrived:
                    total = total + arrived[i, by].astype(jnp.float32)
                if step == 1 and i == 0:
                    total = after(copied, total)
                total = total.astype(jnp.bfloat16)
                if step == chips // 2:
                    early = after(total, early)
                arrived[i, by] = along_ring(total, by)
            if step == chips // 2:
                late, weights = after(arrived[0, 1], (delta, weights))
                copied = passed_on(weights)
        mine = jnp.concatenate(
            [
                term(0, i, late)
                + arrived[i, 1].astype(jnp.float32)
                + arrived[i, -1].astype(jnp.float32)
                for i in range(2)
            ],
            axis=1,
        )
        sent = mine.astype(jnp.bfloat16)
        to_first = [(2 * k + 1, 2 * k) for k in range(chips)]
        to_first += [(2 * (chips + k), 2 * k + 1) for k in range(chips)]
        to_second = [(2 * (chips + k) + 1, 2 * k + 1) for k in range(chips)]
        devices = ("grp", "chip", "core")
        one = lax.ppermute(sent, devices, to_first).astype(jnp.float32)
        two = lax.ppermute(sent, devices, to_second).astype(jnp.float32)
        shard = jnp.concatenate(
            [jnp.where(first_core, mine, one), jnp.where(first_core, one, two)], axis=1
        )
    else:
        delta = weighted[:, None, :] * slope.reshape(seqs, length, half)
        delta = delta.astype(jnp.bfloat16).reshape(seqs * length, half)
        grad = lax.dot_general(
            normed, delta, (((0,), (0,)), ((), ())), preferred_element_type=jnp.float32
        )
        copied = passed_on(weights)
        reduced = lax.psum_scatter(grad, "chip", scatter_dimension=0, tiled=True)
        mine, other = [cut(reduced, 0, part * rows, rows) for part in parts]
        shard = in_core_order(mine, from_sibling(other), first_core, axis=1)
    row_square = jnp.mean(shard * shard, axis=1, keepdims=True)
    normalized = shard * lax.rsqrt(row_square + 1e-06)
    result = jnp.where(trainer, normalized, copied.astype(jnp.float32))
    return result[None]


def solution(mesh):
    groups, devices_fsdp = mesh.devices.shape
    finer = Mesh(
        mesh.devices.reshape(groups, devices_fsdp // cores, cores), ("grp", "chip", "core")
    )
    fsdp = ("chip", "core")
    placed = (
        P("grp", fsdp, None, None),
        P("grp", fsdp, None),
        P("grp", fsdp, None),
        P(),
        P(fsdp, None),
        P(),
    )
    return jax.shard_map(
        shards, mesh=finer, in_specs=placed, out_specs=P("grp", fsdp, None), check_vma=False
    )
```

```python
import functools

import jax
import jax.numpy as jnp
from jax import lax
from jax.experimental import pallas as pl
from jax.experimental.pallas import tpu as pltpu
from jax.sharding import Mesh, PartitionSpec as P

sharpness = 20.0
cores = 2
longest_ring = 16
vmem_limit = 12 << 20


def ring_order(chips):
    return list(range(0, chips, 2)) + list(range(1, chips, 2))[::-1]


def ring_place(chip, chips):
    return jnp.where(chip % 2 == 0, chip // 2, chips - 1 - chip // 2)


def ring_chip(place, chips):
    place = lax.rem(place + 2 * chips, chips)
    return jnp.where(place < chips // 2, 2 * place, 2 * (chips - 1 - place) + 1)


def along_ring(block, by):
    order = ring_order(lax.axis_size("chip"))
    pairs = [(chip, order[(i + by) % len(order)]) for i, chip in enumerate(order)]
    return lax.ppermute(block, "chip", pairs)


def after(first, block):
    return lax.optimization_barrier((first, block))[1]


def passed_on(weights):
    return lax.ppermute(weights.astype(jnp.bfloat16), "grp", [(0, 1)])


def cut(array, axis, start, size):
    starts = [0] * array.ndim
    starts[axis] = start
    sizes = list(array.shape)
    sizes[axis] = size
    return lax.dynamic_slice(array, starts, sizes, allow_negative_indices=False)


def from_sibling(block):
    return lax.ppermute(block, "core", [(0, 1), (1, 0)])


def slab_blocks(stored, chips):
    quarter = chips // 4
    kept = []
    for j in range(quarter):
        pairs = []
        for chip in range(chips):
            for c in range(cores):
                source = 2 * ((chip // 2 + j + c * quarter) % (chips // 2)) + chip % 2
                pairs.append(((chips + source) * cores + c, chip * cores + c))
        kept.append(lax.ppermute(stored, ("grp", "chip", "core"), pairs))
    kept = jnp.concatenate(kept)
    paired = lax.ppermute(kept, "chip", [(chip, chip ^ 1) for chip in range(chips)])
    kept = jnp.concatenate([kept, paired])
    return [kept, from_sibling(kept)]


def in_core_order(mine, other, first_core, axis=0):
    return jnp.where(
        first_core,
        jnp.concatenate([mine, other], axis=axis),
        jnp.concatenate([other, mine], axis=axis),
    )


def normalize_kernel(chunk, states_ref, gain_ref, *refs):
    out_ref = refs[-1]

    @pl.loop(0, states_ref.shape[1] // chunk)
    def _(i):
        at = pl.ds(pl.multiple_of(i * chunk, chunk), chunk)
        wide = states_ref[0, at, :].astype(jnp.float32)
        mean_square = jnp.mean(wide * wide, axis=-1, keepdims=True)
        wide = wide * lax.rsqrt(mean_square + 1e-05) * gain_ref[...]
        out_ref[at, :] = wide.astype(jnp.bfloat16)


def normalize(states, gain, part, filled=None):
    seqs, length, width = states.shape
    tokens = seqs * length
    in_specs = [
        pl.BlockSpec((1, length, width), lambda i: (i, 0, 0)),
        pl.BlockSpec((1, width), lambda i: (0, 0)),
    ]
    operands = [states, gain[None]]
    if filled is not None:
        in_specs.append(pl.BlockSpec(memory_space=pl.ANY))
        operands.append(filled)
    return pl.pallas_call(
        functools.partial(normalize_kernel, 16),
        grid=(seqs,),
        in_specs=in_specs,
        out_specs=pl.BlockSpec((length, width), lambda i: (part * seqs + i, 0)),
        out_shape=jax.ShapeDtypeStruct((cores * tokens, width), jnp.bfloat16),
        input_output_aliases={} if filled is None else {2: 0},
        compiler_params=pltpu.CompilerParams(vmem_limit_bytes=vmem_limit),
        cost_estimate=pl.CostEstimate(
            flops=6 * tokens * width, bytes_accessed=4 * tokens * width, transcendentals=tokens
        ),
    )(*operands)


def shards(token_states, token_ids, master, gain, cand_ids, slab_owner):
    trainer = lax.axis_index("grp") == 0
    chips = lax.axis_size("chip")
    chip = lax.axis_index("chip")
    core = lax.axis_index("core")
    place = ring_place(chip, chips)
    states = token_states[0]
    seq_dev, length, width = states.shape
    rows, embedding = master.shape[1:]
    half = embedding // cores
    seqs = cores * seq_dev

    first_core = core == 0
    shift, parity = chip // 2 + core * (chips // 4), chip % 2
    own_columns, given_columns = core * half, (1 - core) * half
    parts = (core, 1 - core)
    span = chips // 2 if chips <= longest_ring else 0
    starts = {
        (offset, i): (ring_chip(place + offset, chips) * cores + parts[i]) * rows
        for offset in range(-span, span + 1)
        for i in range(2)
    }
    scalars = [first_core, shift, parity, own_columns, given_columns, trainer, *starts.values()]
    weights, *scalars = lax.optimization_barrier([master[0], *scalars])
    first_core, shift, parity, own_columns, given_columns, trainer, *firsts = scalars
    starts = dict(zip(starts, firsts))
    own = cut(weights, 1, own_columns, half).astype(jnp.bfloat16)
    given = cut(weights, 1, given_columns, half).astype(jnp.bfloat16)
    sibling = from_sibling(given)

    other_states = from_sibling(states)
    sent = [(0, 1), (0, -1), (1, 1), (1, -1)]
    if chips <= longest_ring:
        moving = {(i, by): along_ring((own, sibling)[i], by) for i, by in sent}
        states = after((moving[1, 1], moving[1, -1]), states)
    normed_own = normalize(states, gain, 0)

    def columns(offset, i):
        return cut(normed, 1, starts[offset, i], rows)

    def product(offset, i, block):
        return jnp.dot(columns(offset, i), block, preferred_element_type=jnp.float32)

    if chips <= longest_ring:
        total, sums = None, {}
        waiting = [(0, 0, own), (0, 1, sibling)]
        for step in range(1, chips // 2 + 1):
            last = step == chips // 2
            for i, by in [(0, 1), (1, -1)] if last else sent:
                if step > 1:
                    if last and step > 2:
                        tie = normed if i == 0 else sums[2]
                        moving[i, by] = after(tie, moving[i, by])
                    elif step == 3 and i == 0:
                        moving[i, by] = after(normed_own, moving[i, by])
                    moving[i, by] = along_ring(moving[i, by], by)
                waiting.append((-by * step, i, moving[i, by]))
            if step == 1 and not last:
                continue
            if step == min(2, chips // 2):
                other_states = after((moving[1, 1], moving[1, -1]), other_states)
                normed = normalize(other_states, gain, 1, normed_own)
            for offset, i, block in waiting:
                term = product(offset, i, block)
                total = term if total is None else total + term
            waiting = []
            sums[step] = total
            if step == chips // 2 - 1:
                cand_ids, slab_owner = after(sums[2], (cand_ids, slab_owner))
    else:
        normed = normalize(other_states, gain, 1, normed_own)
        both = in_core_order(own, sibling, first_core)
        gathered = lax.all_gather(both, "chip", axis=0, tiled=True)
        total = jnp.dot(normed, gathered, preferred_element_type=jnp.float32)

    slab_rows = slab_owner.shape[0]
    slab_ids = jnp.arange(slab_rows, dtype=jnp.int32)[None, :]
    picked = [
        (cand_ids[:, j : j + 1] == slab_ids).astype(jnp.int32) for j in range(cand_ids.shape[1])
    ]
    ids = jnp.concatenate([token_ids[0], sum(picked), picked[0]], axis=1)
    ids = jnp.concatenate([ids, from_sibling(ids)])
    lengths = jnp.sum((ids[:, :length] != 0).astype(jnp.int32), axis=1)
    counts = lengths.astype(jnp.float32)
    masks = ids[:, length:].astype(jnp.float32)

    active = jnp.tanh(total).reshape(seqs, length, half)
    there = jnp.arange(length)[None, :, None] < lengths[:, None, None]
    pooled = jnp.sum(jnp.where(there, active, 0.0), axis=1) / counts[:, None]
    pooled_other = from_sibling(pooled)
    pooled_other = jnp.concatenate([pooled_other[seq_dev:], pooled_other[:seq_dev]])
    whole = in_core_order(pooled, pooled_other, first_core, axis=1)
    pooled_square = jnp.mean(whole * whole, axis=-1, keepdims=True)
    scale = lax.rsqrt(pooled_square + 1e-06)
    unit = whole * scale
    stored = unit.astype(jnp.bfloat16)
    stored = in_core_order(stored[:seq_dev], stored[seq_dev:], first_core)

    slab = slab_blocks(stored, chips)
    earlier = jnp.arange(slab_rows)[:, None] < jnp.arange(slab_rows)[None, :]
    same = slab_owner[:, None] == slab_owner[None, :]
    ranks = jnp.sum((earlier & same).astype(jnp.int32), axis=0)
    quarter = chips // 4
    owner_chip = lax.div(slab_owner, cores)
    seen = lax.rem(lax.div(owner_chip, 2) - shift + chips, chips // 2)
    paired = (lax.rem(owner_chip, 2) != parity).astype(jnp.int32)
    block = lax.div(seen, quarter) * 2 * quarter + paired * quarter + lax.rem(seen, quarter)
    slots = block * seqs + lax.rem(slab_owner, cores) * seq_dev + ranks
    moved = (slots[:, None] == jnp.arange(slab_rows)[None, :]).astype(jnp.float32)
    candidate = jnp.dot(masks[:, :slab_rows], moved)
    positive = jnp.dot(masks[:, slab_rows:], moved)
    piece = slab_rows // cores
    pieces = [slice(i * piece, (i + 1) * piece) for i in range(cores)]

    slab_wide = [rows_in.astype(jnp.float32) for rows_in in slab]
    exponent = []
    for rows_in, at in zip(slab_wide, pieces):
        logits = (
            sharpness / embedding * jnp.dot(unit, rows_in.T, precision=lax.Precision.HIGHEST)
        )
        exponent.append(jnp.where(candidate[:, at] > 0.5, jnp.exp(logits), 0.0))
    denominator = sum(jnp.sum(part, axis=-1, keepdims=True) for part in exponent)
    unit_grad = (
        sharpness
        / embedding
        * sum(
            jnp.dot(
                part / denominator - positive[:, at], rows_in, precision=lax.Precision.HIGHEST
            )
            for part, rows_in, at in zip(exponent, slab_wide, pieces)
        )
    )
    inner = jnp.sum(whole * unit_grad, axis=-1, keepdims=True)
    pooled_grad = scale * unit_grad - whole * (scale * scale * scale) * inner / embedding
    pooled_grad = cut(pooled_grad, 1, own_columns, half)
    delta = (pooled_grad / counts[:, None])[:, None, :] * (1.0 - active * active)
    delta = jnp.where(there, delta, 0.0)
    delta = delta.astype(jnp.bfloat16).reshape(seqs * length, half)

    def term(offset, i, delta):
        return lax.dot_general(
            columns(offset, i),
            delta,
            (((0,), (0,)), ((), ())),
            preferred_element_type=jnp.float32,
        )

    if chips <= longest_ring:
        arrived = {}
        late = delta
        early = delta
        for step in range(chips // 2, 0, -1):
            for i, by in ((0, 1), (1, -1), (1, 1), (0, -1)):
                if step == chips // 2 and (i, by) not in ((0, 1), (1, -1)):
                    continue
                total = term(by * step, i, delta)
                if (i, by) in arrived:
                    total = total + arrived[i, by].astype(jnp.float32)
                if step == 1 and i == 0:
                    total = after(copied, total)
                total = total.astype(jnp.bfloat16)
                if step == chips // 2:
                    early = after(total, early)
                arrived[i, by] = along_ring(total, by)
            if step == chips // 2:
                late, weights = after(arrived[0, 1], (delta, weights))
                copied = passed_on(weights)
        owns = [term(0, i, late) for i in range(2)]
        arrived[1, 1] = after(owns, arrived[1, 1])
        arrived[0, -1] = after(owns, arrived[0, -1])
        mine, other = [
            owns[i] + arrived[i, 1].astype(jnp.float32) + arrived[i, -1].astype(jnp.float32)
            for i in range(2)
        ]
    else:
        grad = lax.dot_general(
            normed, delta, (((0,), (0,)), ((), ())), preferred_element_type=jnp.float32
        )
        copied = passed_on(weights)
        reduced = lax.psum_scatter(grad, "chip", scatter_dimension=0, tiled=True)
        mine, other = [cut(reduced, 0, part * rows, rows) for part in parts]
    other = from_sibling(other)
    shard = in_core_order(mine, other, first_core, axis=1)
    row_square = jnp.mean(shard * shard, axis=1, keepdims=True)
    normalized = shard * lax.rsqrt(row_square + 1e-06)
    result = jnp.where(trainer, normalized, copied.astype(jnp.float32))
    return result[None]


def solution(mesh):
    groups, devices_fsdp = mesh.devices.shape
    finer = Mesh(
        mesh.devices.reshape(groups, devices_fsdp // cores, cores), ("grp", "chip", "core")
    )
    fsdp = ("chip", "core")
    placed = (
        P("grp", fsdp, None, None),
        P("grp", fsdp, None),
        P("grp", fsdp, None),
        P(),
        P(fsdp, None),
        P(),
    )
    return jax.shard_map(
        shards, mesh=finer, in_specs=placed, out_specs=P("grp", fsdp, None), check_vma=False
    )
```

```python
import functools

import jax
import jax.numpy as jnp
from jax import lax
from jax.experimental import pallas as pl
from jax.experimental.pallas import tpu as pltpu
from jax.sharding import Mesh, PartitionSpec as P

sharpness = 20.0
cores = 2
longest_ring = 16
vmem_limit = 12 << 20


def ring_order(chips):
    return list(range(0, chips, 2)) + list(range(1, chips, 2))[::-1]


def ring_place(chip, chips):
    return jnp.where(chip % 2 == 0, chip // 2, chips - 1 - chip // 2)


def ring_chip(place, chips):
    place = lax.rem(place + 2 * chips, chips)
    return jnp.where(place < chips // 2, 2 * place, 2 * (chips - 1 - place) + 1)


def along_ring(block, by):
    order = ring_order(lax.axis_size("chip"))
    pairs = [(chip, order[(i + by) % len(order)]) for i, chip in enumerate(order)]
    return lax.ppermute(block, "chip", pairs)


def after(first, block):
    return lax.optimization_barrier((first, block))[1]


def passed_on(weights):
    return lax.ppermute(weights.astype(jnp.bfloat16), "grp", [(0, 1)])


def cut(array, axis, start, size):
    starts = [0] * array.ndim
    starts[axis] = start
    sizes = list(array.shape)
    sizes[axis] = size
    return lax.dynamic_slice(array, starts, sizes, allow_negative_indices=False)


def from_sibling(block):
    return lax.ppermute(block, "core", [(0, 1), (1, 0)])


def slab_blocks(stored, chips):
    order = ring_order(chips)
    kept = []
    for j in range(chips // cores):
        pairs = []
        for i, chip in enumerate(order):
            for c in range(cores):
                source = order[(i + j + c * (chips // cores)) % chips]
                pairs.append(((chips + source) * cores + c, chip * cores + c))
        kept.append(lax.ppermute(stored, ("grp", "chip", "core"), pairs))
    return kept


def in_core_order(mine, other, first_core, axis=0):
    return jnp.where(
        first_core,
        jnp.concatenate([mine, other], axis=axis),
        jnp.concatenate([other, mine], axis=axis),
    )


def normalize_kernel(chunk, states_ref, gain_ref, *refs):
    out_ref = refs[-1]

    @pl.loop(0, states_ref.shape[1] // chunk)
    def _(i):
        at = pl.ds(pl.multiple_of(i * chunk, chunk), chunk)
        wide = states_ref[0, at, :].astype(jnp.float32)
        mean_square = jnp.mean(wide * wide, axis=-1, keepdims=True)
        wide = wide * lax.rsqrt(mean_square + 1e-05) * gain_ref[...]
        out_ref[at, :] = wide.astype(jnp.bfloat16)


def normalize(states, gain, part, filled=None):
    seqs, length, width = states.shape
    tokens = seqs * length
    in_specs = [
        pl.BlockSpec((1, length, width), lambda i: (i, 0, 0)),
        pl.BlockSpec((1, width), lambda i: (0, 0)),
    ]
    operands = [states, gain[None]]
    if filled is not None:
        in_specs.append(pl.BlockSpec(memory_space=pl.ANY))
        operands.append(filled)
    return pl.pallas_call(
        functools.partial(normalize_kernel, 16),
        grid=(seqs,),
        in_specs=in_specs,
        out_specs=pl.BlockSpec((length, width), lambda i: (part * seqs + i, 0)),
        out_shape=jax.ShapeDtypeStruct((cores * tokens, width), jnp.bfloat16),
        input_output_aliases={} if filled is None else {2: 0},
        compiler_params=pltpu.CompilerParams(vmem_limit_bytes=vmem_limit),
        cost_estimate=pl.CostEstimate(
            flops=6 * tokens * width, bytes_accessed=4 * tokens * width, transcendentals=tokens
        ),
    )(*operands)


def shards(token_states, token_ids, master, gain, cand_ids, slab_owner):
    trainer = lax.axis_index("grp") == 0
    chips = lax.axis_size("chip")
    chip = lax.axis_index("chip")
    core = lax.axis_index("core")
    place = ring_place(chip, chips)
    states = token_states[0]
    seq_dev, length, width = states.shape
    rows, embedding = master.shape[1:]
    half = embedding // cores
    seqs = cores * seq_dev

    first_core = core == 0
    shift = place + core * (chips // cores)
    own_columns, given_columns = core * half, (1 - core) * half
    parts = (core, 1 - core)
    span = chips // 2 if chips <= longest_ring else 0
    starts = {
        (offset, i): (ring_chip(place + offset, chips) * cores + parts[i]) * rows
        for offset in range(-span, span + 1)
        for i in range(2)
    }
    scalars = [first_core, shift, own_columns, given_columns, trainer, *starts.values()]
    weights, *scalars = lax.optimization_barrier([master[0], *scalars])
    first_core, shift, own_columns, given_columns, trainer, *firsts = scalars
    starts = dict(zip(starts, firsts))
    own = cut(weights, 1, own_columns, half).astype(jnp.bfloat16)
    given = cut(weights, 1, given_columns, half).astype(jnp.bfloat16)
    sibling = from_sibling(given)

    other_states = from_sibling(states)
    sent = [(0, 1), (0, -1), (1, 1), (1, -1)]
    normed_own = normalize(states, gain, 0)
    normed = normalize(other_states, gain, 1, normed_own)
    if chips <= longest_ring:
        moving = {(i, by): along_ring((own, sibling)[i], by) for i, by in sent}

    def columns(offset, i):
        return cut(normed, 1, starts[offset, i], rows)

    def product(offset, i, block):
        return jnp.dot(columns(offset, i), block, preferred_element_type=jnp.float32)

    if chips <= longest_ring:
        total = product(0, 0, own) + product(0, 1, sibling)
        sums = {}
        for step in range(1, chips // 2 + 1):
            last = step == chips // 2
            for i, by in [(0, 1), (1, -1)] if last else sent:
                if step > 1:
                    if last and step > 2:
                        moving[i, by] = after(sums[1 + i], moving[i, by])
                    elif step in (2, 3) and i == 1:
                        moving[i, by] = after((normed_own, normed)[step - 2], moving[i, by])
                    moving[i, by] = along_ring(moving[i, by], by)
                total = total + product(-by * step, i, moving[i, by])
            sums[step] = total
            if step == chips // 2 - 1:
                cand_ids, slab_owner = after(sums[1], (cand_ids, slab_owner))
    else:
        both = in_core_order(own, sibling, first_core)
        gathered = lax.all_gather(both, "chip", axis=0, tiled=True)
        total = jnp.dot(normed, gathered, preferred_element_type=jnp.float32)

    slab_rows = slab_owner.shape[0]
    slab_ids = jnp.arange(slab_rows, dtype=jnp.int32)[None, :]
    picked = [
        (cand_ids[:, j : j + 1] == slab_ids).astype(jnp.int32) for j in range(cand_ids.shape[1])
    ]
    ids = jnp.concatenate([token_ids[0], sum(picked), picked[0]], axis=1)
    ids = jnp.concatenate([ids, from_sibling(ids)])
    lengths = jnp.sum((ids[:, :length] != 0).astype(jnp.int32), axis=1)
    counts = lengths.astype(jnp.float32)
    masks = ids[:, length:].astype(jnp.float32)

    active = jnp.tanh(total).reshape(seqs, length, half)
    there = jnp.arange(length)[None, :, None] < lengths[:, None, None]
    pooled = jnp.sum(jnp.where(there, active, 0.0), axis=1) / counts[:, None]
    pooled_other = from_sibling(pooled)
    pooled_other = jnp.concatenate([pooled_other[seq_dev:], pooled_other[:seq_dev]])
    whole = in_core_order(pooled, pooled_other, first_core, axis=1)
    pooled_square = jnp.mean(whole * whole, axis=-1, keepdims=True)
    scale = lax.rsqrt(pooled_square + 1e-06)
    unit = whole * scale
    stored = unit.astype(jnp.bfloat16)
    stored = in_core_order(stored[:seq_dev], stored[seq_dev:], first_core)

    kept = slab_blocks(stored, chips)
    kept = jnp.concatenate(kept)
    slab = [kept, from_sibling(kept)]
    earlier = jnp.arange(slab_rows)[:, None] < jnp.arange(slab_rows)[None, :]
    same = slab_owner[:, None] == slab_owner[None, :]
    ranks = jnp.sum((earlier & same).astype(jnp.int32), axis=0)
    owner_place = ring_place(slab_owner // cores, chips)
    seen = lax.rem(owner_place - shift + 2 * chips, chips)
    slots = seen * seqs + lax.rem(slab_owner, cores) * seq_dev + ranks
    moved = (slots[:, None] == jnp.arange(slab_rows)[None, :]).astype(jnp.float32)
    candidate = jnp.dot(masks[:, :slab_rows], moved)
    positive = jnp.dot(masks[:, slab_rows:], moved)
    piece = slab_rows // cores
    pieces = [slice(i * piece, (i + 1) * piece) for i in range(cores)]

    slab_wide = [rows_in.astype(jnp.float32) for rows_in in slab]
    exponent = []
    for rows_in, at in zip(slab_wide, pieces):
        logits = (
            sharpness / embedding * jnp.dot(unit, rows_in.T, precision=lax.Precision.HIGHEST)
        )
        exponent.append(jnp.where(candidate[:, at] > 0.5, jnp.exp(logits), 0.0))
    denominator = sum(jnp.sum(part, axis=-1, keepdims=True) for part in exponent)
    unit_grad = (
        sharpness
        / embedding
        * sum(
            jnp.dot(
                part / denominator - positive[:, at], rows_in, precision=lax.Precision.HIGHEST
            )
            for part, rows_in, at in zip(exponent, slab_wide, pieces)
        )
    )
    inner = jnp.sum(whole * unit_grad, axis=-1, keepdims=True)
    pooled_grad = scale * unit_grad - whole * (scale * scale * scale) * inner / embedding
    pooled_grad = cut(pooled_grad, 1, own_columns, half)
    delta = (pooled_grad / counts[:, None])[:, None, :] * (1.0 - active * active)
    delta = jnp.where(there, delta, 0.0)
    delta = delta.astype(jnp.bfloat16).reshape(seqs * length, half)

    def term(offset, i, delta):
        return lax.dot_general(
            columns(offset, i),
            delta,
            (((0,), (0,)), ((), ())),
            preferred_element_type=jnp.float32,
        )

    if chips <= longest_ring:
        four, three = [(0, 1), (1, -1)], [(1, 1), (0, -1)]
        hops = [(chips // 2, four)]
        for step in range(chips // 2 - 1, 0, -1):
            hops += [(step, three), (step, four)]
        arrived, gates = {}, [delta]
        for hop, (step, ways) in enumerate(hops):
            gate = after(gates[max(hop - 2, 0)] if hop > 2 else gates[-1], delta)
            totals = [term(by * step, i, gate) for i, by in ways]
            for at, (i, by) in enumerate(ways):
                if (i, by) in arrived:
                    totals[at], before = lax.optimization_barrier((totals[at], arrived[i, by]))
                    totals[at] = totals[at] + before.astype(jnp.float32)
            totals = [total.astype(jnp.bfloat16) for total in totals]
            if hop == len(hops) - 1:
                totals = after(copied, totals)
            for (i, by), total in zip(ways, totals):
                arrived[i, by] = along_ring(total, by)
            gates.append(totals if hop < 2 else [arrived[way] for way in ways])
            if hop == 0:
                first_hop = [arrived[way] for way in ways]
                weights = after(first_hop, weights)
                copied = passed_on(weights)
            if hop == 1:
                second_hop = [arrived[way] for way in ways]
            if hop == 2:
                gates[1:3] = [first_hop, second_hop]
        late = after(gates[-3], delta)
        owns = [term(0, i, late) for i in range(2)]
        arrived[1, 1] = after(owns, arrived[1, 1])
        arrived[0, -1] = after(owns, arrived[0, -1])
        mine, other = [
            owns[i] + arrived[i, 1].astype(jnp.float32) + arrived[i, -1].astype(jnp.float32)
            for i in range(2)
        ]
    else:
        grad = lax.dot_general(
            normed, delta, (((0,), (0,)), ((), ())), preferred_element_type=jnp.float32
        )
        copied = passed_on(weights)
        reduced = lax.psum_scatter(grad, "chip", scatter_dimension=0, tiled=True)
        mine, other = [cut(reduced, 0, part * rows, rows) for part in parts]
    other = from_sibling(other)
    shard = in_core_order(mine, other, first_core, axis=1)
    row_square = jnp.mean(shard * shard, axis=1, keepdims=True)
    normalized = shard * lax.rsqrt(row_square + 1e-06)
    result = jnp.where(trainer, normalized, copied.astype(jnp.float32))
    return result[None]


def solution(mesh):
    groups, devices_fsdp = mesh.devices.shape
    finer = Mesh(
        mesh.devices.reshape(groups, devices_fsdp // cores, cores), ("grp", "chip", "core")
    )
    fsdp = ("chip", "core")
    placed = (
        P("grp", fsdp, None, None),
        P("grp", fsdp, None),
        P("grp", fsdp, None),
        P(),
        P(fsdp, None),
        P(),
    )
    return jax.shard_map(
        shards, mesh=finer, in_specs=placed, out_specs=P("grp", fsdp, None), check_vma=False
    )
```

```python
import functools

import jax
import jax.numpy as jnp
from jax import lax
from jax.experimental import pallas as pl
from jax.experimental.pallas import tpu as pltpu
from jax.sharding import Mesh, PartitionSpec as P

sharpness = 20.0
cores = 2
longest_ring = 16
vmem_limit = 12 << 20


def ring_order(chips):
    return list(range(0, chips, 2)) + list(range(1, chips, 2))[::-1]


def ring_place(chip, chips):
    return jnp.where(chip % 2 == 0, chip // 2, chips - 1 - chip // 2)


def ring_chip(place, chips):
    place = lax.rem(place + 2 * chips, chips)
    return jnp.where(place < chips // 2, 2 * place, 2 * (chips - 1 - place) + 1)


def along_ring(block, by):
    order = ring_order(lax.axis_size("chip"))
    pairs = [(chip, order[(i + by) % len(order)]) for i, chip in enumerate(order)]
    return lax.ppermute(block, "chip", pairs)


def after(first, block):
    return lax.optimization_barrier((first, block))[1]


def passed_on(weights):
    return lax.ppermute(weights.astype(jnp.bfloat16), "grp", [(0, 1)])


def cut(array, axis, start, size):
    starts = [0] * array.ndim
    starts[axis] = start
    sizes = list(array.shape)
    sizes[axis] = size
    return lax.dynamic_slice(array, starts, sizes, allow_negative_indices=False)


def from_sibling(block):
    return lax.ppermute(block, "core", [(0, 1), (1, 0)])


def slab_blocks(stored, chips):
    order = ring_order(chips)
    kept = []
    for j in range(chips // cores):
        pairs = []
        for i, chip in enumerate(order):
            for c in range(cores):
                source = order[(i + j + c * (chips // cores)) % chips]
                pairs.append(((chips + source) * cores + c, chip * cores + c))
        kept.append(lax.ppermute(stored, ("grp", "chip", "core"), pairs))
    return kept


def in_core_order(mine, other, first_core, axis=0):
    return jnp.where(
        first_core,
        jnp.concatenate([mine, other], axis=axis),
        jnp.concatenate([other, mine], axis=axis),
    )


def normalize_kernel(chunk, states_ref, gain_ref, *refs):
    out_ref = refs[-1]

    @pl.loop(0, states_ref.shape[1] // chunk)
    def _(i):
        at = pl.ds(pl.multiple_of(i * chunk, chunk), chunk)
        wide = states_ref[0, at, :].astype(jnp.float32)
        mean_square = jnp.mean(wide * wide, axis=-1, keepdims=True)
        wide = wide * lax.rsqrt(mean_square + 1e-05) * gain_ref[...]
        out_ref[at, :] = wide.astype(jnp.bfloat16)


def normalize(states, gain, part, filled=None):
    seqs, length, width = states.shape
    tokens = seqs * length
    in_specs = [
        pl.BlockSpec((1, length, width), lambda i: (i, 0, 0)),
        pl.BlockSpec((1, width), lambda i: (0, 0)),
    ]
    operands = [states, gain[None]]
    if filled is not None:
        in_specs.append(pl.BlockSpec(memory_space=pl.ANY))
        operands.append(filled)
    return pl.pallas_call(
        functools.partial(normalize_kernel, 16),
        grid=(seqs,),
        in_specs=in_specs,
        out_specs=pl.BlockSpec((length, width), lambda i: (part * seqs + i, 0)),
        out_shape=jax.ShapeDtypeStruct((cores * tokens, width), jnp.bfloat16),
        input_output_aliases={} if filled is None else {2: 0},
        compiler_params=pltpu.CompilerParams(vmem_limit_bytes=vmem_limit),
        cost_estimate=pl.CostEstimate(
            flops=6 * tokens * width, bytes_accessed=4 * tokens * width, transcendentals=tokens
        ),
    )(*operands)


def shards(token_states, token_ids, master, gain, cand_ids, slab_owner):
    trainer = lax.axis_index("grp") == 0
    chips = lax.axis_size("chip")
    chip = lax.axis_index("chip")
    core = lax.axis_index("core")
    place = ring_place(chip, chips)
    states = token_states[0]
    seq_dev, length, width = states.shape
    rows, embedding = master.shape[1:]
    half = embedding // cores
    seqs = cores * seq_dev

    first_core = core == 0
    shift = place + core * (chips // cores)
    own_columns, given_columns = core * half, (1 - core) * half
    parts = (core, 1 - core)
    span = chips // 2 if chips <= longest_ring else 0
    starts = {
        (offset, i): (ring_chip(place + offset, chips) * cores + parts[i]) * rows
        for offset in range(-span, span + 1)
        for i in range(2)
    }
    scalars = [first_core, shift, own_columns, given_columns, trainer, *starts.values()]
    weights, *scalars = lax.optimization_barrier([master[0], *scalars])
    first_core, shift, own_columns, given_columns, trainer, *firsts = scalars
    starts = dict(zip(starts, firsts))
    own = cut(weights, 1, own_columns, half).astype(jnp.bfloat16)
    given = cut(weights, 1, given_columns, half).astype(jnp.bfloat16)
    sibling = from_sibling(given)

    other_states = from_sibling(states)
    sent = [(0, 1), (0, -1), (1, 1), (1, -1)]
    normed_own = normalize(states, gain, 0)
    normed = normalize(other_states, gain, 1, normed_own)
    if chips <= longest_ring:
        moving = {(i, by): along_ring((own, sibling)[i], by) for i, by in sent}

    def columns(offset, i):
        return cut(normed, 1, starts[offset, i], rows)

    def product(offset, i, block):
        return jnp.dot(columns(offset, i), block, preferred_element_type=jnp.float32)

    if chips <= longest_ring:
        total = product(0, 0, own) + product(0, 1, sibling)
        sums = {}
        for step in range(1, chips // 2 + 1):
            last = step == chips // 2
            for i, by in [(0, 1), (1, -1)] if last else sent:
                if step > 1:
                    if last and step > 2:
                        moving[i, by] = after(sums[1 + i], moving[i, by])
                    elif step in (2, 3) and i == 1:
                        moving[i, by] = after((normed_own, normed)[step - 2], moving[i, by])
                    moving[i, by] = along_ring(moving[i, by], by)
                total = total + product(-by * step, i, moving[i, by])
            sums[step] = total
            if step == chips // 2 - 1:
                cand_ids, slab_owner = after(sums[1], (cand_ids, slab_owner))
    else:
        both = in_core_order(own, sibling, first_core)
        gathered = lax.all_gather(both, "chip", axis=0, tiled=True)
        total = jnp.dot(normed, gathered, preferred_element_type=jnp.float32)

    slab_rows = slab_owner.shape[0]
    slab_ids = jnp.arange(slab_rows, dtype=jnp.int32)[None, :]
    picked = [
        (cand_ids[:, j : j + 1] == slab_ids).astype(jnp.int32) for j in range(cand_ids.shape[1])
    ]
    ids = jnp.concatenate([token_ids[0], sum(picked), picked[0]], axis=1)
    ids = jnp.concatenate([ids, from_sibling(ids)])
    lengths = jnp.sum((ids[:, :length] != 0).astype(jnp.int32), axis=1)
    counts = lengths.astype(jnp.float32)
    masks = ids[:, length:].astype(jnp.float32)

    active = jnp.tanh(total).reshape(seqs, length, half)
    there = jnp.arange(length)[None, :, None] < lengths[:, None, None]
    pooled = jnp.sum(jnp.where(there, active, 0.0), axis=1) / counts[:, None]
    pooled_other = from_sibling(pooled)
    pooled_other = jnp.concatenate([pooled_other[seq_dev:], pooled_other[:seq_dev]])
    whole = in_core_order(pooled, pooled_other, first_core, axis=1)
    pooled_square = jnp.mean(whole * whole, axis=-1, keepdims=True)
    scale = lax.rsqrt(pooled_square + 1e-06)
    unit = whole * scale
    stored = unit.astype(jnp.bfloat16)
    stored = in_core_order(stored[:seq_dev], stored[seq_dev:], first_core)

    kept = slab_blocks(stored, chips)
    kept = jnp.concatenate(kept)
    slab = [kept, from_sibling(kept)]
    earlier = jnp.arange(slab_rows)[:, None] < jnp.arange(slab_rows)[None, :]
    same = slab_owner[:, None] == slab_owner[None, :]
    ranks = jnp.sum((earlier & same).astype(jnp.int32), axis=0)
    owner_place = ring_place(slab_owner // cores, chips)
    seen = lax.rem(owner_place - shift + 2 * chips, chips)
    slots = seen * seqs + lax.rem(slab_owner, cores) * seq_dev + ranks
    moved = (slots[:, None] == jnp.arange(slab_rows)[None, :]).astype(jnp.float32)
    candidate = jnp.dot(masks[:, :slab_rows], moved)
    positive = jnp.dot(masks[:, slab_rows:], moved)
    piece = slab_rows // cores
    pieces = [slice(i * piece, (i + 1) * piece) for i in range(cores)]

    slab_wide = [rows_in.astype(jnp.float32) for rows_in in slab]
    exponent = []
    for rows_in, at in zip(slab_wide, pieces):
        logits = (
            sharpness / embedding * jnp.dot(unit, rows_in.T, precision=lax.Precision.HIGHEST)
        )
        exponent.append(jnp.where(candidate[:, at] > 0.5, jnp.exp(logits), 0.0))
    denominator = sum(jnp.sum(part, axis=-1, keepdims=True) for part in exponent)
    unit_grad = (
        sharpness
        / embedding
        * sum(
            jnp.dot(
                part / denominator - positive[:, at], rows_in, precision=lax.Precision.HIGHEST
            )
            for part, rows_in, at in zip(exponent, slab_wide, pieces)
        )
    )
    inner = jnp.sum(whole * unit_grad, axis=-1, keepdims=True)
    pooled_grad = scale * unit_grad - whole * (scale * scale * scale) * inner / embedding
    pooled_grad = cut(pooled_grad, 1, own_columns, half)
    delta = (pooled_grad / counts[:, None])[:, None, :] * (1.0 - active * active)
    delta = jnp.where(there, delta, 0.0)
    delta = delta.astype(jnp.bfloat16).reshape(seqs * length, half)

    def term(offset, i, delta):
        return lax.dot_general(
            columns(offset, i),
            delta,
            (((0,), (0,)), ((), ())),
            preferred_element_type=jnp.float32,
        )

    if chips <= longest_ring:
        four, three = [(0, 1), (1, -1)], [(1, 1), (0, -1)]
        hops = [(chips // 2, four)]
        for step in range(chips // 2 - 1, 0, -1):
            hops += [(step, three), (step, four)]
        arrived, previous, source = {}, delta, delta
        for hop, (step, ways) in enumerate(hops):
            totals = []
            for i, by in ways:
                total = term(by * step, i, source)
                if (i, by) in arrived:
                    before = after(previous, arrived[i, by])
                    total = total + before.astype(jnp.float32)
                totals.append(total.astype(jnp.bfloat16))
            if hop == len(hops) - 1:
                totals = after(copied, totals)
            for (i, by), total in zip(ways, totals):
                arrived[i, by] = along_ring(total, by)
            previous = totals
            if hop == 0:
                source = after(totals, delta)
                late, weights = after(arrived[0, 1], (delta, weights))
                copied = passed_on(weights)
            else:
                source = late
        owns = [term(0, i, late) for i in range(2)]
        arrived[1, 1] = after(owns, arrived[1, 1])
        arrived[0, -1] = after(owns, arrived[0, -1])
        mine, other = [
            owns[i] + arrived[i, 1].astype(jnp.float32) + arrived[i, -1].astype(jnp.float32)
            for i in range(2)
        ]
    else:
        grad = lax.dot_general(
            normed, delta, (((0,), (0,)), ((), ())), preferred_element_type=jnp.float32
        )
        copied = passed_on(weights)
        reduced = lax.psum_scatter(grad, "chip", scatter_dimension=0, tiled=True)
        mine, other = [cut(reduced, 0, part * rows, rows) for part in parts]
    other = from_sibling(other)
    shard = in_core_order(mine, other, first_core, axis=1)
    row_square = jnp.mean(shard * shard, axis=1, keepdims=True)
    normalized = shard * lax.rsqrt(row_square + 1e-06)
    result = jnp.where(trainer, normalized, copied.astype(jnp.float32))
    return result[None]


def solution(mesh):
    groups, devices_fsdp = mesh.devices.shape
    finer = Mesh(
        mesh.devices.reshape(groups, devices_fsdp // cores, cores), ("grp", "chip", "core")
    )
    fsdp = ("chip", "core")
    placed = (
        P("grp", fsdp, None, None),
        P("grp", fsdp, None),
        P("grp", fsdp, None),
        P(),
        P(fsdp, None),
        P(),
    )
    return jax.shard_map(
        shards, mesh=finer, in_specs=placed, out_specs=P("grp", fsdp, None), check_vma=False
    )
```

```python
import functools

import jax
import jax.numpy as jnp
from jax import lax
from jax.experimental import pallas as pl
from jax.experimental.pallas import tpu as pltpu
from jax.sharding import Mesh, PartitionSpec as P

sharpness = 20.0
cores = 2
longest_ring = 16
vmem_limit = 12 << 20


def ring_order(chips):
    return list(range(0, chips, 2)) + list(range(1, chips, 2))[::-1]


def ring_place(chip, chips):
    return jnp.where(chip % 2 == 0, chip // 2, chips - 1 - chip // 2)


def ring_chip(place, chips):
    place = lax.rem(place + 2 * chips, chips)
    return jnp.where(place < chips // 2, 2 * place, 2 * (chips - 1 - place) + 1)


def along_ring(block, by):
    order = ring_order(lax.axis_size("chip"))
    pairs = [(chip, order[(i + by) % len(order)]) for i, chip in enumerate(order)]
    return lax.ppermute(block, "chip", pairs)


def after(first, block):
    return lax.optimization_barrier((first, block))[1]


def passed_on(weights):
    return lax.ppermute(weights.astype(jnp.bfloat16), "grp", [(0, 1)])


def cut(array, axis, start, size):
    starts = [0] * array.ndim
    starts[axis] = start
    sizes = list(array.shape)
    sizes[axis] = size
    return lax.dynamic_slice(array, starts, sizes, allow_negative_indices=False)


def from_sibling(block):
    return lax.ppermute(block, "core", [(0, 1), (1, 0)])


def slab_blocks(stored, chips):
    order = ring_order(chips)
    kept = []
    for j in range(chips // cores):
        pairs = []
        for i, chip in enumerate(order):
            for c in range(cores):
                source = order[(i + j + c * (chips // cores)) % chips]
                pairs.append(((chips + source) * cores + c, chip * cores + c))
        kept.append(lax.ppermute(stored, ("grp", "chip", "core"), pairs))
    return kept


def in_core_order(mine, other, first_core, axis=0):
    return jnp.where(
        first_core,
        jnp.concatenate([mine, other], axis=axis),
        jnp.concatenate([other, mine], axis=axis),
    )


def normalize_kernel(chunk, states_ref, gain_ref, *refs):
    out_ref = refs[-1]

    @pl.loop(0, states_ref.shape[1] // chunk)
    def _(i):
        at = pl.ds(pl.multiple_of(i * chunk, chunk), chunk)
        wide = states_ref[0, at, :].astype(jnp.float32)
        mean_square = jnp.mean(wide * wide, axis=-1, keepdims=True)
        wide = wide * lax.rsqrt(mean_square + 1e-05) * gain_ref[...]
        out_ref[at, :] = wide.astype(jnp.bfloat16)


def normalize(states, gain, part, filled=None):
    seqs, length, width = states.shape
    tokens = seqs * length
    in_specs = [
        pl.BlockSpec((1, length, width), lambda i: (i, 0, 0)),
        pl.BlockSpec((1, width), lambda i: (0, 0)),
    ]
    operands = [states, gain[None]]
    if filled is not None:
        in_specs.append(pl.BlockSpec(memory_space=pl.ANY))
        operands.append(filled)
    return pl.pallas_call(
        functools.partial(normalize_kernel, 16),
        grid=(seqs,),
        in_specs=in_specs,
        out_specs=pl.BlockSpec((length, width), lambda i: (part * seqs + i, 0)),
        out_shape=jax.ShapeDtypeStruct((cores * tokens, width), jnp.bfloat16),
        input_output_aliases={} if filled is None else {2: 0},
        compiler_params=pltpu.CompilerParams(vmem_limit_bytes=vmem_limit),
        cost_estimate=pl.CostEstimate(
            flops=6 * tokens * width, bytes_accessed=4 * tokens * width, transcendentals=tokens
        ),
    )(*operands)


def shards(token_states, token_ids, master, gain, cand_ids, slab_owner):
    trainer = lax.axis_index("grp") == 0
    chips = lax.axis_size("chip")
    chip = lax.axis_index("chip")
    core = lax.axis_index("core")
    place = ring_place(chip, chips)
    states = token_states[0]
    seq_dev, length, width = states.shape
    rows, embedding = master.shape[1:]
    half = embedding // cores
    seqs = cores * seq_dev

    first_core = core == 0
    shift = place + core * (chips // cores)
    own_columns, given_columns = core * half, (1 - core) * half
    parts = (core, 1 - core)
    span = chips // 2 if chips <= longest_ring else 0
    starts = {
        (offset, i): (ring_chip(place + offset, chips) * cores + parts[i]) * rows
        for offset in range(-span, span + 1)
        for i in range(2)
    }
    scalars = [first_core, shift, own_columns, given_columns, trainer, *starts.values()]
    weights, *scalars = lax.optimization_barrier([master[0], *scalars])
    first_core, shift, own_columns, given_columns, trainer, *firsts = scalars
    starts = dict(zip(starts, firsts))
    own = cut(weights, 1, own_columns, half).astype(jnp.bfloat16)
    given = cut(weights, 1, given_columns, half).astype(jnp.bfloat16)
    sibling = from_sibling(given)

    other_states = from_sibling(states)
    four, three = [(0, 1), (1, -1)], [(1, 1), (0, -1)]
    normed_own = normalize(states, gain, 0)
    normed = normalize(other_states, gain, 1, normed_own)
    if chips <= longest_ring:
        held = [own, sibling, after(sibling, own)]
        moving = {(i, by): along_ring(held[i], by) for i, by in four}
        moving[1, 1] = along_ring(held[1], 1)
        moving[0, -1] = along_ring(held[2], -1)

    def columns(offset, i):
        return cut(normed, 1, starts[offset, i], rows)

    def product(offset, i, block):
        return jnp.dot(columns(offset, i), block, preferred_element_type=jnp.float32)

    if chips <= longest_ring:
        total = product(0, 0, own) + product(0, 1, sibling)
        sums = {}
        for step in range(1, chips // 2 + 1):
            last = step == chips // 2
            for i, by in four if last else four + three:
                if step > 1:
                    if last and step > 2:
                        moving[i, by] = after(sums[1], moving[i, by])
                    elif step in (2, 3) and (i, by) in three:
                        moving[i, by] = after((normed_own, normed)[step - 2], moving[i, by])
                    moving[i, by] = along_ring(moving[i, by], by)
                total = total + product(-by * step, i, moving[i, by])
            sums[step] = total
            if step == chips // 2 - 1:
                cand_ids, slab_owner = after(sums[1], (cand_ids, slab_owner))
    else:
        both = in_core_order(own, sibling, first_core)
        gathered = lax.all_gather(both, "chip", axis=0, tiled=True)
        total = jnp.dot(normed, gathered, preferred_element_type=jnp.float32)

    slab_rows = slab_owner.shape[0]
    slab_ids = jnp.arange(slab_rows, dtype=jnp.int32)[None, :]
    picked = [
        (cand_ids[:, j : j + 1] == slab_ids).astype(jnp.int32) for j in range(cand_ids.shape[1])
    ]
    ids = jnp.concatenate([token_ids[0], sum(picked), picked[0]], axis=1)
    ids = jnp.concatenate([ids, from_sibling(ids)])
    lengths = jnp.sum((ids[:, :length] != 0).astype(jnp.int32), axis=1)
    counts = lengths.astype(jnp.float32)
    masks = ids[:, length:].astype(jnp.float32)

    active = jnp.tanh(total).reshape(seqs, length, half)
    there = jnp.arange(length)[None, :, None] < lengths[:, None, None]
    pooled = jnp.sum(jnp.where(there, active, 0.0), axis=1) / counts[:, None]
    pooled_other = from_sibling(pooled)
    pooled_other = jnp.concatenate([pooled_other[seq_dev:], pooled_other[:seq_dev]])
    whole = in_core_order(pooled, pooled_other, first_core, axis=1)
    pooled_square = jnp.mean(whole * whole, axis=-1, keepdims=True)
    scale = lax.rsqrt(pooled_square + 1e-06)
    unit = whole * scale
    stored = unit.astype(jnp.bfloat16)
    stored = in_core_order(stored[:seq_dev], stored[seq_dev:], first_core)

    kept = slab_blocks(stored, chips)
    kept = jnp.concatenate(kept)
    slab = [kept, from_sibling(kept)]
    earlier = jnp.arange(slab_rows)[:, None] < jnp.arange(slab_rows)[None, :]
    same = slab_owner[:, None] == slab_owner[None, :]
    ranks = jnp.sum((earlier & same).astype(jnp.int32), axis=0)
    owner_place = ring_place(slab_owner // cores, chips)
    seen = lax.rem(owner_place - shift + 2 * chips, chips)
    slots = seen * seqs + lax.rem(slab_owner, cores) * seq_dev + ranks
    moved = (slots[:, None] == jnp.arange(slab_rows)[None, :]).astype(jnp.float32)
    candidate = jnp.dot(masks[:, :slab_rows], moved)
    positive = jnp.dot(masks[:, slab_rows:], moved)
    piece = slab_rows // cores
    pieces = [slice(i * piece, (i + 1) * piece) for i in range(cores)]

    slab_wide = [rows_in.astype(jnp.float32) for rows_in in slab]
    exponent = []
    for rows_in, at in zip(slab_wide, pieces):
        logits = (
            sharpness / embedding * jnp.dot(unit, rows_in.T, precision=lax.Precision.HIGHEST)
        )
        exponent.append(jnp.where(candidate[:, at] > 0.5, jnp.exp(logits), 0.0))
    denominator = sum(jnp.sum(part, axis=-1, keepdims=True) for part in exponent)
    unit_grad = (
        sharpness
        / embedding
        * sum(
            jnp.dot(
                part / denominator - positive[:, at], rows_in, precision=lax.Precision.HIGHEST
            )
            for part, rows_in, at in zip(exponent, slab_wide, pieces)
        )
    )
    inner = jnp.sum(whole * unit_grad, axis=-1, keepdims=True)
    pooled_grad = scale * unit_grad - whole * (scale * scale * scale) * inner / embedding
    pooled_grad = cut(pooled_grad, 1, own_columns, half)
    delta = (pooled_grad / counts[:, None])[:, None, :] * (1.0 - active * active)
    delta = jnp.where(there, delta, 0.0)
    delta = delta.astype(jnp.bfloat16).reshape(seqs * length, half)

    def term(offset, i, delta):
        return lax.dot_general(
            columns(offset, i),
            delta,
            (((0,), (0,)), ((), ())),
            preferred_element_type=jnp.float32,
        )

    if chips <= longest_ring:
        hops = [(chips // 2, four)]
        for step in range(chips // 2 - 1, 0, -1):
            hops += [(step, three), (step, four)]
        arrived, previous, source = {}, delta, delta
        for hop, (step, ways) in enumerate(hops):
            totals = []
            for i, by in ways:
                total = term(by * step, i, source)
                if (i, by) in arrived:
                    before = after(previous, arrived[i, by])
                    total = total + before.astype(jnp.float32)
                totals.append(total.astype(jnp.bfloat16))
            if hop == len(hops) - 1:
                totals = after(copied, totals)
            for (i, by), total in zip(ways, totals):
                arrived[i, by] = along_ring(total, by)
            previous = totals
            if hop == 0:
                source = after(totals, delta)
                late, weights = after(arrived[0, 1], (delta, weights))
                copied = passed_on(weights)
            else:
                source = late
        owns = [term(0, i, late) for i in range(2)]
        arrived[1, 1] = after(owns, arrived[1, 1])
        arrived[0, -1] = after(owns, arrived[0, -1])
        mine, other = [
            owns[i] + arrived[i, 1].astype(jnp.float32) + arrived[i, -1].astype(jnp.float32)
            for i in range(2)
        ]
    else:
        grad = lax.dot_general(
            normed, delta, (((0,), (0,)), ((), ())), preferred_element_type=jnp.float32
        )
        copied = passed_on(weights)
        reduced = lax.psum_scatter(grad, "chip", scatter_dimension=0, tiled=True)
        mine, other = [cut(reduced, 0, part * rows, rows) for part in parts]
    other = from_sibling(other)
    shard = in_core_order(mine, other, first_core, axis=1)
    row_square = jnp.mean(shard * shard, axis=1, keepdims=True)
    normalized = shard * lax.rsqrt(row_square + 1e-06)
    result = jnp.where(trainer, normalized, copied.astype(jnp.float32))
    return result[None]


def solution(mesh):
    groups, devices_fsdp = mesh.devices.shape
    finer = Mesh(
        mesh.devices.reshape(groups, devices_fsdp // cores, cores), ("grp", "chip", "core")
    )
    fsdp = ("chip", "core")
    placed = (
        P("grp", fsdp, None, None),
        P("grp", fsdp, None),
        P("grp", fsdp, None),
        P(),
        P(fsdp, None),
        P(),
    )
    return jax.shard_map(
        shards, mesh=finer, in_specs=placed, out_specs=P("grp", fsdp, None), check_vma=False
    )
```

```python
import functools

import jax
import jax.numpy as jnp
from jax import lax
from jax.experimental import pallas as pl
from jax.experimental.pallas import tpu as pltpu
from jax.sharding import Mesh, PartitionSpec as P

sharpness = 20.0
cores = 2
longest_ring = 16
vmem_limit = 12 << 20


def ring_order(chips):
    return list(range(0, chips, 2)) + list(range(1, chips, 2))[::-1]


def ring_place(chip, chips):
    return jnp.where(chip % 2 == 0, chip // 2, chips - 1 - chip // 2)


def ring_chip(place, chips):
    place = lax.rem(place + 2 * chips, chips)
    return jnp.where(place < chips // 2, 2 * place, 2 * (chips - 1 - place) + 1)


def along_ring(block, by):
    order = ring_order(lax.axis_size("chip"))
    pairs = [(chip, order[(i + by) % len(order)]) for i, chip in enumerate(order)]
    return lax.ppermute(block, "chip", pairs)


def after(first, block):
    return lax.optimization_barrier((first, block))[1]


def passed_on(weights):
    return lax.ppermute(weights.astype(jnp.bfloat16), "grp", [(0, 1)])


def cut(array, axis, start, size):
    starts = [0] * array.ndim
    starts[axis] = start
    sizes = list(array.shape)
    sizes[axis] = size
    return lax.dynamic_slice(array, starts, sizes, allow_negative_indices=False)


def from_sibling(block):
    return lax.ppermute(block, "core", [(0, 1), (1, 0)])


def slab_blocks(stored, chips):
    order = ring_order(chips)
    kept = []
    for j in range(chips // cores):
        pairs = []
        for i, chip in enumerate(order):
            for c in range(cores):
                source = order[(i + j + c * (chips // cores)) % chips]
                pairs.append(((chips + source) * cores + c, chip * cores + c))
        kept.append(lax.ppermute(stored, ("grp", "chip", "core"), pairs))
    return kept


def in_core_order(mine, other, first_core, axis=0):
    return jnp.where(
        first_core,
        jnp.concatenate([mine, other], axis=axis),
        jnp.concatenate([other, mine], axis=axis),
    )


def normalize_kernel(chunk, states_ref, gain_ref, *refs):
    out_ref = refs[-1]

    @pl.loop(0, states_ref.shape[1] // chunk)
    def _(i):
        at = pl.ds(pl.multiple_of(i * chunk, chunk), chunk)
        wide = states_ref[0, at, :].astype(jnp.float32)
        mean_square = jnp.mean(wide * wide, axis=-1, keepdims=True)
        wide = wide * lax.rsqrt(mean_square + 1e-05) * gain_ref[...]
        out_ref[at, :] = wide.astype(jnp.bfloat16)


def normalize(states, gain, part, filled=None):
    seqs, length, width = states.shape
    tokens = seqs * length
    in_specs = [
        pl.BlockSpec((1, length, width), lambda i: (i, 0, 0)),
        pl.BlockSpec((1, width), lambda i: (0, 0)),
    ]
    operands = [states, gain[None]]
    if filled is not None:
        in_specs.append(pl.BlockSpec(memory_space=pl.ANY))
        operands.append(filled)
    return pl.pallas_call(
        functools.partial(normalize_kernel, 16),
        grid=(seqs,),
        in_specs=in_specs,
        out_specs=pl.BlockSpec((length, width), lambda i: (part * seqs + i, 0)),
        out_shape=jax.ShapeDtypeStruct((cores * tokens, width), jnp.bfloat16),
        input_output_aliases={} if filled is None else {2: 0},
        compiler_params=pltpu.CompilerParams(vmem_limit_bytes=vmem_limit),
        cost_estimate=pl.CostEstimate(
            flops=6 * tokens * width, bytes_accessed=4 * tokens * width, transcendentals=tokens
        ),
    )(*operands)


def shards(token_states, token_ids, master, gain, cand_ids, slab_owner):
    trainer = lax.axis_index("grp") == 0
    chips = lax.axis_size("chip")
    chip = lax.axis_index("chip")
    core = lax.axis_index("core")
    place = ring_place(chip, chips)
    states = token_states[0]
    seq_dev, length, width = states.shape
    rows, embedding = master.shape[1:]
    half = embedding // cores
    seqs = cores * seq_dev

    first_core = core == 0
    shift = place + core * (chips // cores)
    own_columns, given_columns = core * half, (1 - core) * half
    parts = (core, 1 - core)
    span = chips // 2 if chips <= longest_ring else 0
    starts = {
        (offset, i): (ring_chip(place + offset, chips) * cores + parts[i]) * rows
        for offset in range(-span, span + 1)
        for i in range(2)
    }
    scalars = [first_core, shift, own_columns, given_columns, trainer, *starts.values()]
    weights = after(scalars, master[0])
    own = cut(weights, 1, own_columns, half).astype(jnp.bfloat16)
    given = cut(weights, 1, given_columns, half).astype(jnp.bfloat16)
    sibling = from_sibling(given)

    other_states = from_sibling(states)
    sent = [(0, 1), (0, -1), (1, 1), (1, -1)]
    normed_own = normalize(states, gain, 0)
    normed = normalize(other_states, gain, 1, normed_own)
    if chips <= longest_ring:
        moving = {(i, by): along_ring((own, sibling)[i], by) for i, by in sent}

    def columns(offset, i):
        return cut(normed, 1, starts[offset, i], rows)

    def product(offset, i, block):
        return jnp.dot(columns(offset, i), block, preferred_element_type=jnp.float32)

    if chips <= longest_ring:
        total = product(0, 0, own) + product(0, 1, sibling)
        sums = {}
        for step in range(1, chips // 2 + 1):
            last = step == chips // 2
            for i, by in [(0, 1), (1, -1)] if last else sent:
                if step > 1:
                    if last and step > 2:
                        moving[i, by] = after(sums[1 + i], moving[i, by])
                    elif step in (2, 3) and i == 1:
                        moving[i, by] = after((normed_own, normed)[step - 2], moving[i, by])
                    moving[i, by] = along_ring(moving[i, by], by)
                total = total + product(-by * step, i, moving[i, by])
            sums[step] = total
            if step == chips // 2 - 1:
                cand_ids, slab_owner = after(sums[1], (cand_ids, slab_owner))
    else:
        both = in_core_order(own, sibling, first_core)
        gathered = lax.all_gather(both, "chip", axis=0, tiled=True)
        total = jnp.dot(normed, gathered, preferred_element_type=jnp.float32)

    slab_rows = slab_owner.shape[0]
    slab_ids = jnp.arange(slab_rows, dtype=jnp.int32)[None, :]
    picked = [
        (cand_ids[:, j : j + 1] == slab_ids).astype(jnp.int32) for j in range(cand_ids.shape[1])
    ]
    ids = jnp.concatenate([token_ids[0], sum(picked), picked[0]], axis=1)
    ids = jnp.concatenate([ids, from_sibling(ids)])
    lengths = jnp.sum((ids[:, :length] != 0).astype(jnp.int32), axis=1)
    counts = lengths.astype(jnp.float32)
    masks = ids[:, length:].astype(jnp.float32)

    active = jnp.tanh(total).reshape(seqs, length, half)
    there = jnp.arange(length)[None, :, None] < lengths[:, None, None]
    pooled = jnp.sum(jnp.where(there, active, 0.0), axis=1) / counts[:, None]
    pooled_other = from_sibling(pooled)
    pooled_other = jnp.concatenate([pooled_other[seq_dev:], pooled_other[:seq_dev]])
    whole = in_core_order(pooled, pooled_other, first_core, axis=1)
    pooled_square = jnp.mean(whole * whole, axis=-1, keepdims=True)
    scale = lax.rsqrt(pooled_square + 1e-06)
    unit = whole * scale
    stored = unit.astype(jnp.bfloat16)
    stored = in_core_order(stored[:seq_dev], stored[seq_dev:], first_core)

    kept = slab_blocks(stored, chips)
    kept = jnp.concatenate(kept)
    slab = [kept, from_sibling(kept)]
    earlier = jnp.arange(slab_rows)[:, None] < jnp.arange(slab_rows)[None, :]
    same = slab_owner[:, None] == slab_owner[None, :]
    ranks = jnp.sum((earlier & same).astype(jnp.int32), axis=0)
    owner_place = ring_place(slab_owner // cores, chips)
    seen = lax.rem(owner_place - shift + 2 * chips, chips)
    slots = seen * seqs + lax.rem(slab_owner, cores) * seq_dev + ranks
    moved = (slots[:, None] == jnp.arange(slab_rows)[None, :]).astype(jnp.float32)
    candidate = jnp.dot(masks[:, :slab_rows], moved)
    positive = jnp.dot(masks[:, slab_rows:], moved)
    piece = slab_rows // cores
    pieces = [slice(i * piece, (i + 1) * piece) for i in range(cores)]

    slab_wide = [rows_in.astype(jnp.float32) for rows_in in slab]
    exponent = []
    for rows_in, at in zip(slab_wide, pieces):
        logits = (
            sharpness / embedding * jnp.dot(unit, rows_in.T, precision=lax.Precision.HIGHEST)
        )
        exponent.append(jnp.where(candidate[:, at] > 0.5, jnp.exp(logits), 0.0))
    denominator = sum(jnp.sum(part, axis=-1, keepdims=True) for part in exponent)
    unit_grad = (
        sharpness
        / embedding
        * sum(
            jnp.dot(
                part / denominator - positive[:, at], rows_in, precision=lax.Precision.HIGHEST
            )
            for part, rows_in, at in zip(exponent, slab_wide, pieces)
        )
    )
    inner = jnp.sum(whole * unit_grad, axis=-1, keepdims=True)
    pooled_grad = scale * unit_grad - whole * (scale * scale * scale) * inner / embedding
    pooled_grad = cut(pooled_grad, 1, own_columns, half)
    delta = (pooled_grad / counts[:, None])[:, None, :] * (1.0 - active * active)
    delta = jnp.where(there, delta, 0.0)
    delta = delta.astype(jnp.bfloat16).reshape(seqs * length, half)

    def term(offset, i, delta):
        return lax.dot_general(
            columns(offset, i),
            delta,
            (((0,), (0,)), ((), ())),
            preferred_element_type=jnp.float32,
        )

    if chips <= longest_ring:
        four, three = [(0, 1), (1, -1)], [(1, 1), (0, -1)]
        hops = [(chips // 2, four)]
        for step in range(chips // 2 - 1, 0, -1):
            hops += [(step, three), (step, four)]
        arrived, previous, source = {}, delta, delta
        for hop, (step, ways) in enumerate(hops):
            totals = []
            for i, by in ways:
                total = term(by * step, i, source)
                if (i, by) in arrived:
                    before = after(previous, arrived[i, by])
                    total = total + before.astype(jnp.float32)
                totals.append(total.astype(jnp.bfloat16))
            if hop == len(hops) - 1:
                totals = after(copied, totals)
            for (i, by), total in zip(ways, totals):
                arrived[i, by] = along_ring(total, by)
            previous = totals
            if hop == 0:
                source = after(totals, delta)
                late, weights = after(arrived[0, 1], (delta, weights))
                copied = passed_on(weights)
            else:
                source = late
        owns = [term(0, i, late) for i in range(2)]
        arrived[1, 1] = after(owns, arrived[1, 1])
        arrived[0, -1] = after(owns, arrived[0, -1])
        mine, other = [
            owns[i] + arrived[i, 1].astype(jnp.float32) + arrived[i, -1].astype(jnp.float32)
            for i in range(2)
        ]
    else:
        grad = lax.dot_general(
            normed, delta, (((0,), (0,)), ((), ())), preferred_element_type=jnp.float32
        )
        copied = passed_on(weights)
        reduced = lax.psum_scatter(grad, "chip", scatter_dimension=0, tiled=True)
        mine, other = [cut(reduced, 0, part * rows, rows) for part in parts]
    other = from_sibling(other)
    shard = in_core_order(mine, other, first_core, axis=1)
    row_square = jnp.mean(shard * shard, axis=1, keepdims=True)
    normalized = shard * lax.rsqrt(row_square + 1e-06)
    result = jnp.where(trainer, normalized, copied.astype(jnp.float32))
    return result[None]


def solution(mesh):
    groups, devices_fsdp = mesh.devices.shape
    finer = Mesh(
        mesh.devices.reshape(groups, devices_fsdp // cores, cores), ("grp", "chip", "core")
    )
    fsdp = ("chip", "core")
    placed = (
        P("grp", fsdp, None, None),
        P("grp", fsdp, None),
        P("grp", fsdp, None),
        P(),
        P(fsdp, None),
        P(),
    )
    return jax.shard_map(
        shards, mesh=finer, in_specs=placed, out_specs=P("grp", fsdp, None), check_vma=False
    )
```

```python
import functools

import jax
import jax.numpy as jnp
from jax import lax
from jax.experimental import pallas as pl
from jax.experimental.pallas import tpu as pltpu
from jax.sharding import Mesh, PartitionSpec as P

sharpness = 20.0
cores = 2
longest_ring = 16
vmem_limit = 12 << 20


def ring_order(chips):
    return list(range(0, chips, 2)) + list(range(1, chips, 2))[::-1]


def ring_place(chip, chips):
    return jnp.where(chip % 2 == 0, chip // 2, chips - 1 - chip // 2)


def ring_chip(place, chips):
    place = lax.rem(place + 2 * chips, chips)
    return jnp.where(place < chips // 2, 2 * place, 2 * (chips - 1 - place) + 1)


def along_ring(block, by):
    order = ring_order(lax.axis_size("chip"))
    pairs = [(chip, order[(i + by) % len(order)]) for i, chip in enumerate(order)]
    return lax.ppermute(block, "chip", pairs)


def after(first, block):
    return lax.optimization_barrier((first, block))[1]


def passed_on(weights):
    return lax.ppermute(weights.astype(jnp.bfloat16), "grp", [(0, 1)])


def cut(array, axis, start, size):
    starts = [0] * array.ndim
    starts[axis] = start
    sizes = list(array.shape)
    sizes[axis] = size
    return lax.dynamic_slice(array, starts, sizes, allow_negative_indices=False)


def from_sibling(block):
    return lax.ppermute(block, "core", [(0, 1), (1, 0)])


def slab_blocks(stored, chips):
    order = ring_order(chips)
    kept = []
    for j in range(chips // cores):
        pairs = []
        for i, chip in enumerate(order):
            for c in range(cores):
                source = order[(i + j + c * (chips // cores)) % chips]
                pairs.append(((chips + source) * cores + c, chip * cores + c))
        kept.append(lax.ppermute(stored, ("grp", "chip", "core"), pairs))
    return kept


def in_core_order(mine, other, first_core, axis=0):
    return jnp.where(
        first_core,
        jnp.concatenate([mine, other], axis=axis),
        jnp.concatenate([other, mine], axis=axis),
    )


def normalize_kernel(chunk, states_ref, gain_ref, *refs):
    out_ref = refs[-1]

    @pl.loop(0, states_ref.shape[1] // chunk)
    def _(i):
        at = pl.ds(pl.multiple_of(i * chunk, chunk), chunk)
        wide = states_ref[0, at, :].astype(jnp.float32)
        mean_square = jnp.mean(wide * wide, axis=-1, keepdims=True)
        wide = wide * lax.rsqrt(mean_square + 1e-05) * gain_ref[...]
        out_ref[at, :] = wide.astype(jnp.bfloat16)


def normalize(states, gain, part, filled=None):
    seqs, length, width = states.shape
    tokens = seqs * length
    in_specs = [
        pl.BlockSpec((1, length, width), lambda i: (i, 0, 0)),
        pl.BlockSpec((1, width), lambda i: (0, 0)),
    ]
    operands = [states, gain[None]]
    if filled is not None:
        in_specs.append(pl.BlockSpec(memory_space=pl.ANY))
        operands.append(filled)
    return pl.pallas_call(
        functools.partial(normalize_kernel, 16),
        grid=(seqs,),
        in_specs=in_specs,
        out_specs=pl.BlockSpec((length, width), lambda i: (part * seqs + i, 0)),
        out_shape=jax.ShapeDtypeStruct((cores * tokens, width), jnp.bfloat16),
        input_output_aliases={} if filled is None else {2: 0},
        compiler_params=pltpu.CompilerParams(vmem_limit_bytes=vmem_limit),
        cost_estimate=pl.CostEstimate(
            flops=6 * tokens * width, bytes_accessed=4 * tokens * width, transcendentals=tokens
        ),
    )(*operands)


def shards(token_states, token_ids, master, gain, cand_ids, slab_owner):
    trainer = lax.axis_index("grp") == 0
    chips = lax.axis_size("chip")
    chip = lax.axis_index("chip")
    core = lax.axis_index("core")
    place = ring_place(chip, chips)
    states = token_states[0]
    seq_dev, length, width = states.shape
    rows, embedding = master.shape[1:]
    half = embedding // cores
    seqs = cores * seq_dev

    first_core = core == 0
    shift = place + core * (chips // cores)
    own_columns, given_columns = core * half, (1 - core) * half
    parts = (core, 1 - core)
    span = chips // 2 if chips <= longest_ring else 0
    starts = {
        (offset, i): (ring_chip(place + offset, chips) * cores + parts[i]) * rows
        for offset in range(-span, span + 1)
        for i in range(2)
    }
    scalars = [first_core, shift, own_columns, given_columns, trainer, *starts.values()]
    weights = after(scalars, master[0])
    own = cut(weights, 1, own_columns, half).astype(jnp.bfloat16)
    given = cut(weights, 1, given_columns, half).astype(jnp.bfloat16)
    sibling = from_sibling(given)

    other_states = from_sibling(states)
    four, three = [(0, 1), (1, -1)], [(1, 1), (0, -1)]
    normed_own = normalize(states, gain, 0)
    normed = normalize(other_states, gain, 1, normed_own)
    if chips <= longest_ring:
        held = [own, sibling, after(sibling, own)]
        moving = {(i, by): along_ring(held[i], by) for i, by in four}
        moving[1, 1] = along_ring(held[1], 1)
        moving[0, -1] = along_ring(held[2], -1)

    def columns(offset, i):
        return cut(normed, 1, starts[offset, i], rows)

    def product(offset, i, block):
        return jnp.dot(columns(offset, i), block, preferred_element_type=jnp.float32)

    if chips <= longest_ring:
        total = product(0, 0, own) + product(0, 1, sibling)
        sums = {}
        for step in range(1, chips // 2 + 1):
            last = step == chips // 2
            for i, by in four if last else four + three:
                if step > 1:
                    if last and step > 2:
                        moving[i, by] = after(normed, moving[i, by])
                    elif step == 3 and (i, by) in four:
                        moving[i, by] = after(normed_own, moving[i, by])
                    moving[i, by] = along_ring(moving[i, by], by)
                total = total + product(-by * step, i, moving[i, by])
            sums[step] = total
            if step == chips // 2 - 1:
                cand_ids, slab_owner = after(sums[1], (cand_ids, slab_owner))
    else:
        both = in_core_order(own, sibling, first_core)
        gathered = lax.all_gather(both, "chip", axis=0, tiled=True)
        total = jnp.dot(normed, gathered, preferred_element_type=jnp.float32)

    slab_rows = slab_owner.shape[0]
    slab_ids = jnp.arange(slab_rows, dtype=jnp.int32)[None, :]
    picked = [
        (cand_ids[:, j : j + 1] == slab_ids).astype(jnp.int32) for j in range(cand_ids.shape[1])
    ]
    ids = jnp.concatenate([token_ids[0], sum(picked), picked[0]], axis=1)
    ids = jnp.concatenate([ids, from_sibling(ids)])
    lengths = jnp.sum((ids[:, :length] != 0).astype(jnp.int32), axis=1)
    counts = lengths.astype(jnp.float32)
    masks = ids[:, length:].astype(jnp.float32)

    active = jnp.tanh(total).reshape(seqs, length, half)
    there = jnp.arange(length)[None, :, None] < lengths[:, None, None]
    pooled = jnp.sum(jnp.where(there, active, 0.0), axis=1) / counts[:, None]
    pooled_other = from_sibling(pooled)
    pooled_other = jnp.concatenate([pooled_other[seq_dev:], pooled_other[:seq_dev]])
    whole = in_core_order(pooled, pooled_other, first_core, axis=1)
    pooled_square = jnp.mean(whole * whole, axis=-1, keepdims=True)
    scale = lax.rsqrt(pooled_square + 1e-06)
    unit = whole * scale
    stored = unit.astype(jnp.bfloat16)
    stored = in_core_order(stored[:seq_dev], stored[seq_dev:], first_core)

    kept = slab_blocks(stored, chips)
    kept = jnp.concatenate(kept)
    slab = [kept, from_sibling(kept)]
    earlier = jnp.arange(slab_rows)[:, None] < jnp.arange(slab_rows)[None, :]
    same = slab_owner[:, None] == slab_owner[None, :]
    ranks = jnp.sum((earlier & same).astype(jnp.int32), axis=0)
    owner_place = ring_place(slab_owner // cores, chips)
    seen = lax.rem(owner_place - shift + 2 * chips, chips)
    slots = seen * seqs + lax.rem(slab_owner, cores) * seq_dev + ranks
    moved = (slots[:, None] == jnp.arange(slab_rows)[None, :]).astype(jnp.float32)
    candidate = jnp.dot(masks[:, :slab_rows], moved)
    positive = jnp.dot(masks[:, slab_rows:], moved)
    piece = slab_rows // cores
    pieces = [slice(i * piece, (i + 1) * piece) for i in range(cores)]

    slab_wide = [rows_in.astype(jnp.float32) for rows_in in slab]
    exponent = []
    for rows_in, at in zip(slab_wide, pieces):
        logits = (
            sharpness / embedding * jnp.dot(unit, rows_in.T, precision=lax.Precision.HIGHEST)
        )
        exponent.append(jnp.where(candidate[:, at] > 0.5, jnp.exp(logits), 0.0))
    denominator = sum(jnp.sum(part, axis=-1, keepdims=True) for part in exponent)
    unit_grad = (
        sharpness
        / embedding
        * sum(
            jnp.dot(
                part / denominator - positive[:, at], rows_in, precision=lax.Precision.HIGHEST
            )
            for part, rows_in, at in zip(exponent, slab_wide, pieces)
        )
    )
    inner = jnp.sum(whole * unit_grad, axis=-1, keepdims=True)
    pooled_grad = scale * unit_grad - whole * (scale * scale * scale) * inner / embedding
    pooled_grad = cut(pooled_grad, 1, own_columns, half)
    delta = (pooled_grad / counts[:, None])[:, None, :] * (1.0 - active * active)
    delta = jnp.where(there, delta, 0.0)
    delta = delta.astype(jnp.bfloat16).reshape(seqs * length, half)

    def term(offset, i, delta):
        return lax.dot_general(
            columns(offset, i),
            delta,
            (((0,), (0,)), ((), ())),
            preferred_element_type=jnp.float32,
        )

    if chips <= longest_ring:
        hops = [(chips // 2, four)]
        for step in range(chips // 2 - 1, 0, -1):
            hops += [(step, three), (step, four)]
        arrived, previous, source = {}, delta, delta
        for hop, (step, ways) in enumerate(hops):
            totals = []
            for i, by in ways:
                total = term(by * step, i, source)
                if (i, by) in arrived:
                    before = after(previous, arrived[i, by])
                    total = total + before.astype(jnp.float32)
                totals.append(total.astype(jnp.bfloat16))
            if hop == len(hops) - 1:
                totals = after(copied, totals)
            for (i, by), total in zip(ways, totals):
                arrived[i, by] = along_ring(total, by)
            previous = totals
            if hop == 0:
                source = after(totals, delta)
                late, weights = after(arrived[0, 1], (delta, weights))
                copied = passed_on(weights)
            else:
                source = late
        late = after([arrived[way] for way in three], delta)
        owns = [term(0, i, late) for i in range(2)]
        arrived[1, 1] = after(owns, arrived[1, 1])
        arrived[0, -1] = after(owns, arrived[0, -1])
        mine, other = [
            owns[i] + arrived[i, 1].astype(jnp.float32) + arrived[i, -1].astype(jnp.float32)
            for i in range(2)
        ]
    else:
        grad = lax.dot_general(
            normed, delta, (((0,), (0,)), ((), ())), preferred_element_type=jnp.float32
        )
        copied = passed_on(weights)
        reduced = lax.psum_scatter(grad, "chip", scatter_dimension=0, tiled=True)
        mine, other = [cut(reduced, 0, part * rows, rows) for part in parts]
    other = from_sibling(other)
    shard = in_core_order(mine, other, first_core, axis=1)
    row_square = jnp.mean(shard * shard, axis=1, keepdims=True)
    normalized = shard * lax.rsqrt(row_square + 1e-06)
    result = jnp.where(trainer, normalized, copied.astype(jnp.float32))
    return result[None]


def solution(mesh):
    groups, devices_fsdp = mesh.devices.shape
    finer = Mesh(
        mesh.devices.reshape(groups, devices_fsdp // cores, cores), ("grp", "chip", "core")
    )
    fsdp = ("chip", "core")
    placed = (
        P("grp", fsdp, None, None),
        P("grp", fsdp, None),
        P("grp", fsdp, None),
        P(),
        P(fsdp, None),
        P(),
    )
    return jax.shard_map(
        shards, mesh=finer, in_specs=placed, out_specs=P("grp", fsdp, None), check_vma=False
    )
```

```python
import functools

import jax
import jax.numpy as jnp
from jax import lax
from jax.experimental import pallas as pl
from jax.experimental.pallas import tpu as pltpu
from jax.sharding import Mesh, PartitionSpec as P

sharpness = 20.0
cores = 2
longest_ring = 16
vmem_limit = 12 << 20


def ring_order(chips):
    return list(range(0, chips, 2)) + list(range(1, chips, 2))[::-1]


def ring_place(chip, chips):
    return jnp.where(chip % 2 == 0, chip // 2, chips - 1 - chip // 2)


def ring_chip(place, chips):
    place = lax.rem(place + 2 * chips, chips)
    return jnp.where(place < chips // 2, 2 * place, 2 * (chips - 1 - place) + 1)


def along_ring(block, by):
    order = ring_order(lax.axis_size("chip"))
    pairs = [(chip, order[(i + by) % len(order)]) for i, chip in enumerate(order)]
    return lax.ppermute(block, "chip", pairs)


def after(first, block):
    return lax.optimization_barrier((first, block))[1]


def passed_on(weights):
    return lax.ppermute(weights.astype(jnp.bfloat16), "grp", [(0, 1)])


def cut(array, axis, start, size):
    starts = [0] * array.ndim
    starts[axis] = start
    sizes = list(array.shape)
    sizes[axis] = size
    return lax.dynamic_slice(array, starts, sizes, allow_negative_indices=False)


def from_sibling(block):
    return lax.ppermute(block, "core", [(0, 1), (1, 0)])


def slab_blocks(stored, chips):
    order = ring_order(chips)
    kept = []
    for j in range(chips // cores):
        pairs = []
        for i, chip in enumerate(order):
            for c in range(cores):
                source = order[(i + j + c * (chips // cores)) % chips]
                pairs.append(((chips + source) * cores + c, chip * cores + c))
        kept.append(lax.ppermute(stored, ("grp", "chip", "core"), pairs))
    return kept


def in_core_order(mine, other, first_core, axis=0):
    return jnp.where(
        first_core,
        jnp.concatenate([mine, other], axis=axis),
        jnp.concatenate([other, mine], axis=axis),
    )


def normalize_kernel(chunk, states_ref, gain_ref, *refs):
    out_ref = refs[-1]

    @pl.loop(0, states_ref.shape[1] // chunk)
    def _(i):
        at = pl.ds(pl.multiple_of(i * chunk, chunk), chunk)
        wide = states_ref[0, at, :].astype(jnp.float32)
        mean_square = jnp.mean(wide * wide, axis=-1, keepdims=True)
        wide = wide * lax.rsqrt(mean_square + 1e-05) * gain_ref[...]
        out_ref[at, :] = wide.astype(jnp.bfloat16)


def normalize(states, gain, part, filled=None):
    seqs, length, width = states.shape
    tokens = seqs * length
    in_specs = [
        pl.BlockSpec((1, length, width), lambda i: (i, 0, 0)),
        pl.BlockSpec((1, width), lambda i: (0, 0)),
    ]
    operands = [states, gain[None]]
    if filled is not None:
        in_specs.append(pl.BlockSpec(memory_space=pl.ANY))
        operands.append(filled)
    return pl.pallas_call(
        functools.partial(normalize_kernel, 16),
        grid=(seqs,),
        in_specs=in_specs,
        out_specs=pl.BlockSpec((length, width), lambda i: (part * seqs + i, 0)),
        out_shape=jax.ShapeDtypeStruct((cores * tokens, width), jnp.bfloat16),
        input_output_aliases={} if filled is None else {2: 0},
        compiler_params=pltpu.CompilerParams(vmem_limit_bytes=vmem_limit),
        cost_estimate=pl.CostEstimate(
            flops=6 * tokens * width, bytes_accessed=4 * tokens * width, transcendentals=tokens
        ),
    )(*operands)


def shards(token_states, token_ids, master, gain, cand_ids, slab_owner):
    trainer = lax.axis_index("grp") == 0
    chips = lax.axis_size("chip")
    chip = lax.axis_index("chip")
    core = lax.axis_index("core")
    place = ring_place(chip, chips)
    states = token_states[0]
    seq_dev, length, width = states.shape
    rows, embedding = master.shape[1:]
    half = embedding // cores
    seqs = cores * seq_dev

    first_core = core == 0
    shift = place + core * (chips // cores)
    own_columns, given_columns = core * half, (1 - core) * half
    parts = (core, 1 - core)
    span = chips // 2 if chips <= longest_ring else 0
    starts = {
        (offset, i): (ring_chip(place + offset, chips) * cores + parts[i]) * rows
        for offset in range(-span, span + 1)
        for i in range(2)
    }
    scalars = [first_core, shift, own_columns, given_columns, trainer, *starts.values()]
    weights = after(scalars, master[0])
    own = cut(weights, 1, own_columns, half).astype(jnp.bfloat16)
    given = cut(weights, 1, given_columns, half).astype(jnp.bfloat16)
    sibling = from_sibling(given)

    other_states = from_sibling(states)
    sent = [(0, 1), (0, -1), (1, 1), (1, -1)]
    normed_own = normalize(states, gain, 0)
    normed = normalize(other_states, gain, 1, normed_own)
    if chips <= longest_ring:
        moving = {(i, by): along_ring((own, sibling)[i], by) for i, by in sent}

    def columns(offset, i):
        return cut(normed, 1, starts[offset, i], rows)

    def product(offset, i, block):
        return jnp.dot(columns(offset, i), block, preferred_element_type=jnp.float32)

    if chips <= longest_ring:
        total = product(0, 0, own) + product(0, 1, sibling)
        sums = {}
        for step in range(1, chips // 2 + 1):
            last = step == chips // 2
            for i, by in [(0, 1), (1, -1)] if last else sent:
                if step > 1:
                    if last and step > 2:
                        moving[i, by] = after(sums[1 + i], moving[i, by])
                    elif step in (2, 3) and i == 1:
                        moving[i, by] = after((normed_own, normed)[step - 2], moving[i, by])
                    moving[i, by] = along_ring(moving[i, by], by)
                total = total + product(-by * step, i, moving[i, by])
            sums[step] = total
            if step == chips // 2 - 1:
                cand_ids, slab_owner = after(sums[1], (cand_ids, slab_owner))
    else:
        both = in_core_order(own, sibling, first_core)
        gathered = lax.all_gather(both, "chip", axis=0, tiled=True)
        total = jnp.dot(normed, gathered, preferred_element_type=jnp.float32)

    slab_rows = slab_owner.shape[0]
    slab_ids = jnp.arange(slab_rows, dtype=jnp.int32)[None, :]
    picked = [
        (cand_ids[:, j : j + 1] == slab_ids).astype(jnp.int32) for j in range(cand_ids.shape[1])
    ]
    ids = jnp.concatenate([token_ids[0], sum(picked), picked[0]], axis=1)
    ids = jnp.concatenate([ids, from_sibling(ids)])
    lengths = jnp.sum((ids[:, :length] != 0).astype(jnp.int32), axis=1)
    counts = lengths.astype(jnp.float32)
    masks = ids[:, length:].astype(jnp.float32)

    active = jnp.tanh(total).reshape(seqs, length, half)
    there = jnp.arange(length)[None, :, None] < lengths[:, None, None]
    pooled = jnp.sum(jnp.where(there, active, 0.0), axis=1) / counts[:, None]
    pooled_other = from_sibling(pooled)
    pooled_other = jnp.concatenate([pooled_other[seq_dev:], pooled_other[:seq_dev]])
    whole = in_core_order(pooled, pooled_other, first_core, axis=1)
    pooled_square = jnp.mean(whole * whole, axis=-1, keepdims=True)
    scale = lax.rsqrt(pooled_square + 1e-06)
    unit = whole * scale
    stored = unit.astype(jnp.bfloat16)
    stored = in_core_order(stored[:seq_dev], stored[seq_dev:], first_core)

    kept = slab_blocks(stored, chips)
    kept = jnp.concatenate(kept)
    slab = [kept, from_sibling(kept)]
    earlier = jnp.arange(slab_rows)[:, None] < jnp.arange(slab_rows)[None, :]
    same = slab_owner[:, None] == slab_owner[None, :]
    ranks = jnp.sum((earlier & same).astype(jnp.int32), axis=0)
    owner_place = ring_place(slab_owner // cores, chips)
    seen = lax.rem(owner_place - shift + 2 * chips, chips)
    slots = seen * seqs + lax.rem(slab_owner, cores) * seq_dev + ranks
    moved = (slots[:, None] == jnp.arange(slab_rows)[None, :]).astype(jnp.float32)
    candidate = jnp.dot(masks[:, :slab_rows], moved)
    positive = jnp.dot(masks[:, slab_rows:], moved)
    piece = slab_rows // cores
    pieces = [slice(i * piece, (i + 1) * piece) for i in range(cores)]

    slab_wide = [rows_in.astype(jnp.float32) for rows_in in slab]
    exponent = []
    for rows_in, at in zip(slab_wide, pieces):
        logits = (
            sharpness / embedding * jnp.dot(unit, rows_in.T, precision=lax.Precision.HIGHEST)
        )
        exponent.append(jnp.where(candidate[:, at] > 0.5, jnp.exp(logits), 0.0))
    denominator = sum(jnp.sum(part, axis=-1, keepdims=True) for part in exponent)
    unit_grad = (
        sharpness
        / embedding
        * sum(
            jnp.dot(
                part / denominator - positive[:, at], rows_in, precision=lax.Precision.HIGHEST
            )
            for part, rows_in, at in zip(exponent, slab_wide, pieces)
        )
    )
    inner = jnp.sum(whole * unit_grad, axis=-1, keepdims=True)
    pooled_grad = scale * unit_grad - whole * (scale * scale * scale) * inner / embedding
    pooled_grad = cut(pooled_grad, 1, own_columns, half)
    delta = (pooled_grad / counts[:, None])[:, None, :] * (1.0 - active * active)
    delta = jnp.where(there, delta, 0.0)
    delta = delta.astype(jnp.bfloat16).reshape(seqs * length, half)

    def term(offset, i, delta):
        return lax.dot_general(
            columns(offset, i),
            delta,
            (((0,), (0,)), ((), ())),
            preferred_element_type=jnp.float32,
        )

    if chips <= longest_ring:
        four, three = [(0, 1), (1, -1)], [(1, 1), (0, -1)]
        hops = [(chips // 2, four)]
        for step in range(chips // 2 - 1, 0, -1):
            hops += [(step, three), (step, four)]
        arrived, previous, source = {}, {}, delta
        for hop, (step, ways) in enumerate(hops):
            totals = []
            for i, by in ways:
                total = term(by * step, i, source)
                if (i, by) in arrived:
                    before = after(previous[by], arrived[i, by])
                    total = total + before.astype(jnp.float32)
                totals.append(total.astype(jnp.bfloat16))
            if hop == len(hops) - 1:
                totals = after(copied, totals)
            for (i, by), total in zip(ways, totals):
                arrived[i, by] = along_ring(total, by)
            previous = {by: total for (i, by), total in zip(ways, totals)}
            if hop == 0:
                source = after(totals, delta)
                late, weights = after(arrived[0, 1], (delta, weights))
                copied = passed_on(weights)
            else:
                source = late
        owns = [term(0, i, late) for i in range(2)]
        arrived[1, 1] = after(owns, arrived[1, 1])
        arrived[0, -1] = after(owns, arrived[0, -1])
        mine, other = [
            owns[i] + arrived[i, 1].astype(jnp.float32) + arrived[i, -1].astype(jnp.float32)
            for i in range(2)
        ]
    else:
        grad = lax.dot_general(
            normed, delta, (((0,), (0,)), ((), ())), preferred_element_type=jnp.float32
        )
        copied = passed_on(weights)
        reduced = lax.psum_scatter(grad, "chip", scatter_dimension=0, tiled=True)
        mine, other = [cut(reduced, 0, part * rows, rows) for part in parts]
    other = from_sibling(other)
    shard = in_core_order(mine, other, first_core, axis=1)
    row_square = jnp.mean(shard * shard, axis=1, keepdims=True)
    normalized = shard * lax.rsqrt(row_square + 1e-06)
    result = jnp.where(trainer, normalized, copied.astype(jnp.float32))
    return result[None]


def solution(mesh):
    groups, devices_fsdp = mesh.devices.shape
    finer = Mesh(
        mesh.devices.reshape(groups, devices_fsdp // cores, cores), ("grp", "chip", "core")
    )
    fsdp = ("chip", "core")
    placed = (
        P("grp", fsdp, None, None),
        P("grp", fsdp, None),
        P("grp", fsdp, None),
        P(),
        P(fsdp, None),
        P(),
    )
    return jax.shard_map(
        shards, mesh=finer, in_specs=placed, out_specs=P("grp", fsdp, None), check_vma=False
    )
```

```python
import functools

import jax
import jax.numpy as jnp
from jax import lax
from jax.experimental import pallas as pl
from jax.experimental.pallas import tpu as pltpu
from jax.sharding import Mesh, PartitionSpec as P

sharpness = 20.0
cores = 2
longest_ring = 16
vmem_limit = 12 << 20


def ring_order(chips):
    return list(range(0, chips, 2)) + list(range(1, chips, 2))[::-1]


def ring_place(chip, chips):
    return jnp.where(chip % 2 == 0, chip // 2, chips - 1 - chip // 2)


def ring_chip(place, chips):
    place = lax.rem(place + 2 * chips, chips)
    return jnp.where(place < chips // 2, 2 * place, 2 * (chips - 1 - place) + 1)


def along_ring(block, by):
    order = ring_order(lax.axis_size("chip"))
    pairs = [(chip, order[(i + by) % len(order)]) for i, chip in enumerate(order)]
    return lax.ppermute(block, "chip", pairs)


def after(first, block):
    return lax.optimization_barrier((first, block))[1]


def passed_on(weights):
    return lax.ppermute(weights.astype(jnp.bfloat16), "grp", [(0, 1)])


def cut(array, axis, start, size):
    starts = [0] * array.ndim
    starts[axis] = start
    sizes = list(array.shape)
    sizes[axis] = size
    return lax.dynamic_slice(array, starts, sizes, allow_negative_indices=False)


def from_sibling(block):
    return lax.ppermute(block, "core", [(0, 1), (1, 0)])


def slab_blocks(stored, chips):
    order = ring_order(chips)
    kept = []
    for j in range(chips // cores):
        pairs = []
        for i, chip in enumerate(order):
            for c in range(cores):
                source = order[(i + j + c * (chips // cores)) % chips]
                pairs.append(((chips + source) * cores + c, chip * cores + c))
        kept.append(lax.ppermute(stored, ("grp", "chip", "core"), pairs))
    return kept


def in_core_order(mine, other, first_core, axis=0):
    return jnp.where(
        first_core,
        jnp.concatenate([mine, other], axis=axis),
        jnp.concatenate([other, mine], axis=axis),
    )


def normalize_kernel(chunk, states_ref, gain_ref, *refs):
    out_ref = refs[-1]

    @pl.loop(0, states_ref.shape[1] // chunk)
    def _(i):
        at = pl.ds(pl.multiple_of(i * chunk, chunk), chunk)
        wide = states_ref[0, at, :].astype(jnp.float32)
        mean_square = jnp.mean(wide * wide, axis=-1, keepdims=True)
        wide = wide * lax.rsqrt(mean_square + 1e-05) * gain_ref[...]
        out_ref[at, :] = wide.astype(jnp.bfloat16)


def normalize(states, gain, part, filled=None):
    seqs, length, width = states.shape
    tokens = seqs * length
    in_specs = [
        pl.BlockSpec((1, length, width), lambda i: (i, 0, 0)),
        pl.BlockSpec((1, width), lambda i: (0, 0)),
    ]
    operands = [states, gain[None]]
    if filled is not None:
        in_specs.append(pl.BlockSpec(memory_space=pl.ANY))
        operands.append(filled)
    return pl.pallas_call(
        functools.partial(normalize_kernel, 16),
        grid=(seqs,),
        in_specs=in_specs,
        out_specs=pl.BlockSpec((length, width), lambda i: (part * seqs + i, 0)),
        out_shape=jax.ShapeDtypeStruct((cores * tokens, width), jnp.bfloat16),
        input_output_aliases={} if filled is None else {2: 0},
        compiler_params=pltpu.CompilerParams(vmem_limit_bytes=vmem_limit),
        cost_estimate=pl.CostEstimate(
            flops=6 * tokens * width, bytes_accessed=4 * tokens * width, transcendentals=tokens
        ),
    )(*operands)


def shards(token_states, token_ids, master, gain, cand_ids, slab_owner):
    trainer = lax.axis_index("grp") == 0
    chips = lax.axis_size("chip")
    chip = lax.axis_index("chip")
    core = lax.axis_index("core")
    place = ring_place(chip, chips)
    states = token_states[0]
    seq_dev, length, width = states.shape
    rows, embedding = master.shape[1:]
    half = embedding // cores
    seqs = cores * seq_dev

    first_core = core == 0
    shift = place + core * (chips // cores)
    own_columns, given_columns = core * half, (1 - core) * half
    parts = (core, 1 - core)
    span = chips // 2 if chips <= longest_ring else 0
    starts = {
        (offset, i): (ring_chip(place + offset, chips) * cores + parts[i]) * rows
        for offset in range(-span, span + 1)
        for i in range(2)
    }
    scalars = [first_core, shift, own_columns, given_columns, trainer, *starts.values()]
    weights = after(scalars, master[0])
    own = cut(weights, 1, own_columns, half).astype(jnp.bfloat16)
    given = cut(weights, 1, given_columns, half).astype(jnp.bfloat16)
    sibling = from_sibling(given)

    other_states = from_sibling(states)
    sent = [(0, 1), (0, -1), (1, 1), (1, -1)]
    normed_own = normalize(states, gain, 0)
    normed = normalize(other_states, gain, 1, normed_own)
    if chips <= longest_ring:
        moving = {(i, by): along_ring((own, sibling)[i], by) for i, by in sent}

    def columns(offset, i):
        return cut(normed, 1, starts[offset, i], rows)

    def product(offset, i, block):
        return jnp.dot(columns(offset, i), block, preferred_element_type=jnp.float32)

    if chips <= longest_ring:
        total = product(0, 0, own) + product(0, 1, sibling)
        sums = {}
        for step in range(1, chips // 2 + 1):
            last = step == chips // 2
            for i, by in [(0, 1), (1, -1)] if last else sent:
                if step > 1:
                    if last and step > 2:
                        moving[i, by] = after(sums[1 + i], moving[i, by])
                    elif step in (2, 3) and i == 1:
                        moving[i, by] = after((normed_own, normed)[step - 2], moving[i, by])
                    moving[i, by] = along_ring(moving[i, by], by)
                total = total + product(-by * step, i, moving[i, by])
            sums[step] = total
            if step == chips // 2 - 1:
                cand_ids, slab_owner = after(sums[1], (cand_ids, slab_owner))
    else:
        both = in_core_order(own, sibling, first_core)
        gathered = lax.all_gather(both, "chip", axis=0, tiled=True)
        total = jnp.dot(normed, gathered, preferred_element_type=jnp.float32)

    slab_rows = slab_owner.shape[0]
    slab_ids = jnp.arange(slab_rows, dtype=jnp.int32)[None, :]
    picked = [
        (cand_ids[:, j : j + 1] == slab_ids).astype(jnp.int32) for j in range(cand_ids.shape[1])
    ]
    ids = jnp.concatenate([token_ids[0], sum(picked), picked[0]], axis=1)
    ids = jnp.concatenate([ids, from_sibling(ids)])
    lengths = jnp.sum((ids[:, :length] != 0).astype(jnp.int32), axis=1)
    counts = lengths.astype(jnp.float32)
    masks = ids[:, length:].astype(jnp.float32)

    active = jnp.tanh(total).reshape(seqs, length, half)
    there = jnp.arange(length)[None, :, None] < lengths[:, None, None]
    pooled = jnp.sum(jnp.where(there, active, 0.0), axis=1) / counts[:, None]
    pooled_other = from_sibling(pooled)
    pooled_other = jnp.concatenate([pooled_other[seq_dev:], pooled_other[:seq_dev]])
    whole = in_core_order(pooled, pooled_other, first_core, axis=1)
    pooled_square = jnp.mean(whole * whole, axis=-1, keepdims=True)
    scale = lax.rsqrt(pooled_square + 1e-06)
    unit = whole * scale
    stored = unit.astype(jnp.bfloat16)
    stored = in_core_order(stored[:seq_dev], stored[seq_dev:], first_core)

    kept = slab_blocks(stored, chips)
    kept = jnp.concatenate(kept)
    slab = [kept, from_sibling(kept)]
    earlier = jnp.arange(slab_rows)[:, None] < jnp.arange(slab_rows)[None, :]
    same = slab_owner[:, None] == slab_owner[None, :]
    ranks = jnp.sum((earlier & same).astype(jnp.int32), axis=0)
    owner_place = ring_place(slab_owner // cores, chips)
    seen = lax.rem(owner_place - shift + 2 * chips, chips)
    slots = seen * seqs + lax.rem(slab_owner, cores) * seq_dev + ranks
    moved = (slots[:, None] == jnp.arange(slab_rows)[None, :]).astype(jnp.float32)
    candidate = jnp.dot(masks[:, :slab_rows], moved)
    positive = jnp.dot(masks[:, slab_rows:], moved)
    piece = slab_rows // cores
    pieces = [slice(i * piece, (i + 1) * piece) for i in range(cores)]

    slab_wide = [rows_in.astype(jnp.float32) for rows_in in slab]
    exponent = []
    for rows_in, at in zip(slab_wide, pieces):
        logits = (
            sharpness / embedding * jnp.dot(unit, rows_in.T, precision=lax.Precision.HIGHEST)
        )
        exponent.append(jnp.where(candidate[:, at] > 0.5, jnp.exp(logits), 0.0))
    denominator = sum(jnp.sum(part, axis=-1, keepdims=True) for part in exponent)
    unit_grad = (
        sharpness
        / embedding
        * sum(
            jnp.dot(
                part / denominator - positive[:, at], rows_in, precision=lax.Precision.HIGHEST
            )
            for part, rows_in, at in zip(exponent, slab_wide, pieces)
        )
    )
    inner = jnp.sum(whole * unit_grad, axis=-1, keepdims=True)
    pooled_grad = scale * unit_grad - whole * (scale * scale * scale) * inner / embedding
    pooled_grad = cut(pooled_grad, 1, own_columns, half)
    delta = (pooled_grad / counts[:, None])[:, None, :] * (1.0 - active * active)
    delta = jnp.where(there, delta, 0.0)
    delta = delta.astype(jnp.bfloat16).reshape(seqs * length, half)

    def term(offset, i, delta):
        return lax.dot_general(
            columns(offset, i),
            delta,
            (((0,), (0,)), ((), ())),
            preferred_element_type=jnp.float32,
        )

    if chips <= longest_ring:
        four, three = [(0, 1), (1, -1)], [(1, 1), (0, -1)]
        hops = [(chips // 2, four)]
        for step in range(chips // 2 - 1, 0, -1):
            hops += [(step, three), (step, four)]
        arrived, previous, source = {}, delta, delta
        for hop, (step, ways) in enumerate(hops):
            if hop == max(len(hops) - 3, 1):
                owns = [term(0, i, late) for i in range(2)]
                previous = after(owns, previous)
            totals = []
            for i, by in ways:
                total = term(by * step, i, source)
                if (i, by) in arrived:
                    before = after(previous, arrived[i, by])
                    total = total + before.astype(jnp.float32)
                totals.append(total.astype(jnp.bfloat16))
            if hop == len(hops) - 1:
                totals = after(copied, totals)
            for (i, by), total in zip(ways, totals):
                arrived[i, by] = along_ring(total, by)
            previous = totals
            if hop == 0:
                source = after(totals, delta)
                late, weights = after(arrived[0, 1], (delta, weights))
                copied = passed_on(weights)
            else:
                source = late
        mine, other = [
            owns[i] + arrived[i, 1].astype(jnp.float32) + arrived[i, -1].astype(jnp.float32)
            for i in range(2)
        ]
    else:
        grad = lax.dot_general(
            normed, delta, (((0,), (0,)), ((), ())), preferred_element_type=jnp.float32
        )
        copied = passed_on(weights)
        reduced = lax.psum_scatter(grad, "chip", scatter_dimension=0, tiled=True)
        mine, other = [cut(reduced, 0, part * rows, rows) for part in parts]
    other = from_sibling(other)
    shard = in_core_order(mine, other, first_core, axis=1)
    row_square = jnp.mean(shard * shard, axis=1, keepdims=True)
    normalized = shard * lax.rsqrt(row_square + 1e-06)
    result = jnp.where(trainer, normalized, copied.astype(jnp.float32))
    return result[None]


def solution(mesh):
    groups, devices_fsdp = mesh.devices.shape
    finer = Mesh(
        mesh.devices.reshape(groups, devices_fsdp // cores, cores), ("grp", "chip", "core")
    )
    fsdp = ("chip", "core")
    placed = (
        P("grp", fsdp, None, None),
        P("grp", fsdp, None),
        P("grp", fsdp, None),
        P(),
        P(fsdp, None),
        P(),
    )
    return jax.shard_map(
        shards, mesh=finer, in_specs=placed, out_specs=P("grp", fsdp, None), check_vma=False
    )
```

```python
import functools

import jax
import jax.numpy as jnp
from jax import lax
from jax.experimental import pallas as pl
from jax.experimental.pallas import tpu as pltpu
from jax.sharding import Mesh, PartitionSpec as P

sharpness = 20.0
cores = 2
longest_ring = 16
vmem_limit = 12 << 20


def ring_order(chips):
    return list(range(0, chips, 2)) + list(range(1, chips, 2))[::-1]


def ring_place(chip, chips):
    return jnp.where(chip % 2 == 0, chip // 2, chips - 1 - chip // 2)


def ring_chip(place, chips):
    place = lax.rem(place + 2 * chips, chips)
    return jnp.where(place < chips // 2, 2 * place, 2 * (chips - 1 - place) + 1)


def along_ring(block, by):
    order = ring_order(lax.axis_size("chip"))
    pairs = [(chip, order[(i + by) % len(order)]) for i, chip in enumerate(order)]
    return lax.ppermute(block, "chip", pairs)


def after(first, block):
    return lax.optimization_barrier((first, block))[1]


def passed_on(weights):
    return lax.ppermute(weights.astype(jnp.bfloat16), "grp", [(0, 1)])


def cut(array, axis, start, size):
    starts = [0] * array.ndim
    starts[axis] = start
    sizes = list(array.shape)
    sizes[axis] = size
    return lax.dynamic_slice(array, starts, sizes, allow_negative_indices=False)


def from_sibling(block):
    return lax.ppermute(block, "core", [(0, 1), (1, 0)])


def slab_blocks(stored, chips):
    order = ring_order(chips)
    kept = []
    for j in range(chips // cores):
        pairs = []
        for i, chip in enumerate(order):
            for c in range(cores):
                source = order[(i + j + c * (chips // cores)) % chips]
                pairs.append(((chips + source) * cores + c, chip * cores + c))
        kept.append(lax.ppermute(stored, ("grp", "chip", "core"), pairs))
    return kept


def in_core_order(mine, other, first_core, axis=0):
    return jnp.where(
        first_core,
        jnp.concatenate([mine, other], axis=axis),
        jnp.concatenate([other, mine], axis=axis),
    )


def normalize_kernel(chunk, states_ref, gain_ref, *refs):
    out_ref = refs[-1]

    @pl.loop(0, states_ref.shape[1] // chunk)
    def _(i):
        at = pl.ds(pl.multiple_of(i * chunk, chunk), chunk)
        wide = states_ref[0, at, :].astype(jnp.float32)
        mean_square = jnp.mean(wide * wide, axis=-1, keepdims=True)
        wide = wide * lax.rsqrt(mean_square + 1e-05) * gain_ref[...]
        out_ref[at, :] = wide.astype(jnp.bfloat16)


def normalize(states, gain, part, filled=None):
    seqs, length, width = states.shape
    tokens = seqs * length
    in_specs = [
        pl.BlockSpec((1, length, width), lambda i: (i, 0, 0)),
        pl.BlockSpec((1, width), lambda i: (0, 0)),
    ]
    operands = [states, gain[None]]
    if filled is not None:
        in_specs.append(pl.BlockSpec(memory_space=pl.ANY))
        operands.append(filled)
    return pl.pallas_call(
        functools.partial(normalize_kernel, 16),
        grid=(seqs,),
        in_specs=in_specs,
        out_specs=pl.BlockSpec((length, width), lambda i: (part * seqs + i, 0)),
        out_shape=jax.ShapeDtypeStruct((cores * tokens, width), jnp.bfloat16),
        input_output_aliases={} if filled is None else {2: 0},
        compiler_params=pltpu.CompilerParams(vmem_limit_bytes=vmem_limit),
        cost_estimate=pl.CostEstimate(
            flops=6 * tokens * width, bytes_accessed=4 * tokens * width, transcendentals=tokens
        ),
    )(*operands)


def shards(token_states, token_ids, master, gain, cand_ids, slab_owner):
    trainer = lax.axis_index("grp") == 0
    chips = lax.axis_size("chip")
    chip = lax.axis_index("chip")
    core = lax.axis_index("core")
    place = ring_place(chip, chips)
    states = token_states[0]
    seq_dev, length, width = states.shape
    rows, embedding = master.shape[1:]
    half = embedding // cores
    seqs = cores * seq_dev

    first_core = core == 0
    shift = place + core * (chips // cores)
    own_columns, given_columns = core * half, (1 - core) * half
    parts = (core, 1 - core)
    span = chips // 2 if chips <= longest_ring else 0
    starts = {
        (offset, i): (ring_chip(place + offset, chips) * cores + parts[i]) * rows
        for offset in range(-span, span + 1)
        for i in range(2)
    }
    scalars = [first_core, shift, own_columns, given_columns, trainer, *starts.values()]
    weights = after(scalars, master[0])
    own = cut(weights, 1, own_columns, half).astype(jnp.bfloat16)
    given = cut(weights, 1, given_columns, half).astype(jnp.bfloat16)
    sibling = from_sibling(given)

    other_states = from_sibling(states)
    sent = [(0, 1), (0, -1), (1, 1), (1, -1)]
    normed_own = normalize(states, gain, 0)
    normed = normalize(other_states, gain, 1, normed_own)
    if chips <= longest_ring:
        moving = {(i, by): along_ring((own, sibling)[i], by) for i, by in sent}

    def columns(offset, i):
        return cut(normed, 1, starts[offset, i], rows)

    def product(offset, i, block):
        return jnp.dot(columns(offset, i), block, preferred_element_type=jnp.float32)

    if chips <= longest_ring:
        total = product(0, 0, own) + product(0, 1, sibling)
        sums = {}
        for step in range(1, chips // 2 + 1):
            last = step == chips // 2
            for i, by in [(0, 1), (1, -1)] if last else sent:
                if step > 1:
                    if last and step > 2:
                        moving[i, by] = after(sums[1 + i], moving[i, by])
                    elif step in (2, 3) and i == 1:
                        moving[i, by] = after((normed_own, normed)[step - 2], moving[i, by])
                    moving[i, by] = along_ring(moving[i, by], by)
                total = total + product(-by * step, i, moving[i, by])
            sums[step] = total
            if step == chips // 2 - 1:
                cand_ids, slab_owner = after(sums[1], (cand_ids, slab_owner))
    else:
        both = in_core_order(own, sibling, first_core)
        gathered = lax.all_gather(both, "chip", axis=0, tiled=True)
        total = jnp.dot(normed, gathered, preferred_element_type=jnp.float32)

    slab_rows = slab_owner.shape[0]
    slab_ids = jnp.arange(slab_rows, dtype=jnp.int32)[None, :]
    picked = [
        (cand_ids[:, j : j + 1] == slab_ids).astype(jnp.int32) for j in range(cand_ids.shape[1])
    ]
    ids = jnp.concatenate([token_ids[0], sum(picked), picked[0]], axis=1)
    ids = jnp.concatenate([ids, from_sibling(ids)])
    lengths = jnp.sum((ids[:, :length] != 0).astype(jnp.int32), axis=1)
    counts = lengths.astype(jnp.float32)
    masks = ids[:, length:].astype(jnp.float32)

    active = jnp.tanh(total).reshape(seqs, length, half)
    there = jnp.arange(length)[None, :, None] < lengths[:, None, None]
    pooled = jnp.sum(jnp.where(there, active, 0.0), axis=1) / counts[:, None]
    pooled_other = from_sibling(pooled)
    pooled_other = jnp.concatenate([pooled_other[seq_dev:], pooled_other[:seq_dev]])
    whole = in_core_order(pooled, pooled_other, first_core, axis=1)
    pooled_square = jnp.mean(whole * whole, axis=-1, keepdims=True)
    scale = lax.rsqrt(pooled_square + 1e-06)
    unit = whole * scale
    stored = unit.astype(jnp.bfloat16)
    stored = in_core_order(stored[:seq_dev], stored[seq_dev:], first_core)

    kept = slab_blocks(stored, chips)
    kept = jnp.concatenate(kept)
    slab = [kept, from_sibling(kept)]
    earlier = jnp.arange(slab_rows)[:, None] < jnp.arange(slab_rows)[None, :]
    same = slab_owner[:, None] == slab_owner[None, :]
    ranks = jnp.sum((earlier & same).astype(jnp.int32), axis=0)
    owner_place = ring_place(slab_owner // cores, chips)
    seen = lax.rem(owner_place - shift + 2 * chips, chips)
    slots = seen * seqs + lax.rem(slab_owner, cores) * seq_dev + ranks
    moved = (slots[:, None] == jnp.arange(slab_rows)[None, :]).astype(jnp.float32)
    candidate = jnp.dot(masks[:, :slab_rows], moved)
    positive = jnp.dot(masks[:, slab_rows:], moved)
    piece = slab_rows // cores
    pieces = [slice(i * piece, (i + 1) * piece) for i in range(cores)]

    slab_wide = [rows_in.astype(jnp.float32) for rows_in in slab]
    exponent = []
    for rows_in, at in zip(slab_wide, pieces):
        logits = (
            sharpness / embedding * jnp.dot(unit, rows_in.T, precision=lax.Precision.HIGHEST)
        )
        exponent.append(jnp.where(candidate[:, at] > 0.5, jnp.exp(logits), 0.0))
    denominator = sum(jnp.sum(part, axis=-1, keepdims=True) for part in exponent)
    unit_grad = (
        sharpness
        / embedding
        * sum(
            jnp.dot(
                part / denominator - positive[:, at], rows_in, precision=lax.Precision.HIGHEST
            )
            for part, rows_in, at in zip(exponent, slab_wide, pieces)
        )
    )
    inner = jnp.sum(whole * unit_grad, axis=-1, keepdims=True)
    pooled_grad = scale * unit_grad - whole * (scale * scale * scale) * inner / embedding
    pooled_grad = cut(pooled_grad, 1, own_columns, half)
    delta = (pooled_grad / counts[:, None])[:, None, :] * (1.0 - active * active)
    delta = jnp.where(there, delta, 0.0)
    delta = delta.astype(jnp.bfloat16).reshape(seqs * length, half)

    def term(offset, i, delta):
        return lax.dot_general(
            columns(offset, i),
            delta,
            (((0,), (0,)), ((), ())),
            preferred_element_type=jnp.float32,
        )

    if chips <= longest_ring:
        four, three = [(0, 1), (1, -1)], [(1, 1), (0, -1)]
        hops = [(chips // 2, four)]
        for step in range(chips // 2 - 1, 0, -1):
            hops += [(step, three), (step, four)]
        arrived, previous, source = {}, delta, delta
        for hop, (step, ways) in enumerate(hops):
            if hop == max(len(hops) - 2, 1):
                released = after(previous, delta)
                owns = [term(0, i, released) for i in range(2)]
                previous = after(owns, previous)
            totals = []
            for i, by in ways:
                total = term(by * step, i, source)
                if (i, by) in arrived:
                    before = after(previous, arrived[i, by])
                    total = total + before.astype(jnp.float32)
                totals.append(total.astype(jnp.bfloat16))
            if hop == len(hops) - 1:
                totals = after(copied, totals)
            for (i, by), total in zip(ways, totals):
                arrived[i, by] = along_ring(total, by)
            previous = totals
            if hop == 0:
                source = after(totals, delta)
                late, weights = after(arrived[0, 1], (delta, weights))
                copied = passed_on(weights)
            else:
                source = late
        mine, other = [
            owns[i] + arrived[i, 1].astype(jnp.float32) + arrived[i, -1].astype(jnp.float32)
            for i in range(2)
        ]
    else:
        grad = lax.dot_general(
            normed, delta, (((0,), (0,)), ((), ())), preferred_element_type=jnp.float32
        )
        copied = passed_on(weights)
        reduced = lax.psum_scatter(grad, "chip", scatter_dimension=0, tiled=True)
        mine, other = [cut(reduced, 0, part * rows, rows) for part in parts]
    other = from_sibling(other)
    shard = in_core_order(mine, other, first_core, axis=1)
    row_square = jnp.mean(shard * shard, axis=1, keepdims=True)
    normalized = shard * lax.rsqrt(row_square + 1e-06)
    result = jnp.where(trainer, normalized, copied.astype(jnp.float32))
    return result[None]


def solution(mesh):
    groups, devices_fsdp = mesh.devices.shape
    finer = Mesh(
        mesh.devices.reshape(groups, devices_fsdp // cores, cores), ("grp", "chip", "core")
    )
    fsdp = ("chip", "core")
    placed = (
        P("grp", fsdp, None, None),
        P("grp", fsdp, None),
        P("grp", fsdp, None),
        P(),
        P(fsdp, None),
        P(),
    )
    return jax.shard_map(
        shards, mesh=finer, in_specs=placed, out_specs=P("grp", fsdp, None), check_vma=False
    )
```

```python
import functools

import jax
import jax.numpy as jnp
from jax import lax
from jax.experimental import pallas as pl
from jax.experimental.pallas import tpu as pltpu
from jax.sharding import Mesh, PartitionSpec as P

sharpness = 20.0
cores = 2
longest_ring = 16
vmem_limit = 12 << 20


def ring_order(chips):
    return list(range(0, chips, 2)) + list(range(1, chips, 2))[::-1]


def ring_place(chip, chips):
    return jnp.where(chip % 2 == 0, chip // 2, chips - 1 - chip // 2)


def ring_chip(place, chips):
    place = lax.rem(place + 2 * chips, chips)
    return jnp.where(place < chips // 2, 2 * place, 2 * (chips - 1 - place) + 1)


def along_ring(block, by):
    order = ring_order(lax.axis_size("chip"))
    pairs = [(chip, order[(i + by) % len(order)]) for i, chip in enumerate(order)]
    return lax.ppermute(block, "chip", pairs)


def after(first, block):
    return lax.optimization_barrier((first, block))[1]


def passed_on(weights):
    return lax.ppermute(weights.astype(jnp.bfloat16), "grp", [(0, 1)])


def cut(array, axis, start, size):
    starts = [0] * array.ndim
    starts[axis] = start
    sizes = list(array.shape)
    sizes[axis] = size
    return lax.dynamic_slice(array, starts, sizes, allow_negative_indices=False)


def from_sibling(block):
    return lax.ppermute(block, "core", [(0, 1), (1, 0)])


def slab_blocks(stored, chips):
    order = ring_order(chips)
    kept = []
    for j in range(chips // cores):
        pairs = []
        for i, chip in enumerate(order):
            for c in range(cores):
                source = order[(i + j + c * (chips // cores)) % chips]
                pairs.append(((chips + source) * cores + c, chip * cores + c))
        kept.append(lax.ppermute(stored, ("grp", "chip", "core"), pairs))
    return kept


def in_core_order(mine, other, first_core, axis=0):
    return jnp.where(
        first_core,
        jnp.concatenate([mine, other], axis=axis),
        jnp.concatenate([other, mine], axis=axis),
    )


def normalize_kernel(chunk, states_ref, gain_ref, *refs):
    out_ref = refs[-1]

    @pl.loop(0, states_ref.shape[1] // chunk)
    def _(i):
        at = pl.ds(pl.multiple_of(i * chunk, chunk), chunk)
        wide = states_ref[0, at, :].astype(jnp.float32)
        mean_square = jnp.mean(wide * wide, axis=-1, keepdims=True)
        wide = wide * lax.rsqrt(mean_square + 1e-05) * gain_ref[...]
        out_ref[at, :] = wide.astype(jnp.bfloat16)


def normalize(states, gain, part, filled=None):
    seqs, length, width = states.shape
    tokens = seqs * length
    in_specs = [
        pl.BlockSpec((1, length, width), lambda i: (i, 0, 0)),
        pl.BlockSpec((1, width), lambda i: (0, 0)),
    ]
    operands = [states, gain[None]]
    if filled is not None:
        in_specs.append(pl.BlockSpec(memory_space=pl.ANY))
        operands.append(filled)
    return pl.pallas_call(
        functools.partial(normalize_kernel, 16),
        grid=(seqs,),
        in_specs=in_specs,
        out_specs=pl.BlockSpec((length, width), lambda i: (part * seqs + i, 0)),
        out_shape=jax.ShapeDtypeStruct((cores * tokens, width), jnp.bfloat16),
        input_output_aliases={} if filled is None else {2: 0},
        compiler_params=pltpu.CompilerParams(vmem_limit_bytes=vmem_limit),
        cost_estimate=pl.CostEstimate(
            flops=6 * tokens * width, bytes_accessed=4 * tokens * width, transcendentals=tokens
        ),
    )(*operands)


def shards(token_states, token_ids, master, gain, cand_ids, slab_owner):
    trainer = lax.axis_index("grp") == 0
    chips = lax.axis_size("chip")
    chip = lax.axis_index("chip")
    core = lax.axis_index("core")
    place = ring_place(chip, chips)
    states = token_states[0]
    seq_dev, length, width = states.shape
    rows, embedding = master.shape[1:]
    half = embedding // cores
    seqs = cores * seq_dev

    first_core = core == 0
    shift = place + core * (chips // cores)
    own_columns, given_columns = core * half, (1 - core) * half
    parts = (core, 1 - core)
    span = chips // 2 if chips <= longest_ring else 0
    starts = {
        (offset, i): (ring_chip(place + offset, chips) * cores + parts[i]) * rows
        for offset in range(-span, span + 1)
        for i in range(2)
    }
    scalars = [first_core, shift, own_columns, given_columns, trainer, *starts.values()]
    weights = after(scalars, master[0])
    own = cut(weights, 1, own_columns, half).astype(jnp.bfloat16)
    given = cut(weights, 1, given_columns, half).astype(jnp.bfloat16)
    sibling = from_sibling(given)

    other_states = from_sibling(after(own, states))
    sent = [(0, 1), (0, -1), (1, 1), (1, -1)]
    normed_own = normalize(states, gain, 0)
    normed = normalize(other_states, gain, 1, normed_own)
    if chips <= longest_ring:
        moving = {(i, by): along_ring((own, sibling)[i], by) for i, by in sent}

    def columns(offset, i):
        return cut(normed, 1, starts[offset, i], rows)

    def product(offset, i, block):
        return jnp.dot(columns(offset, i), block, preferred_element_type=jnp.float32)

    if chips <= longest_ring:
        total = product(0, 0, own) + product(0, 1, sibling)
        sums = {}
        for step in range(1, chips // 2 + 1):
            last = step == chips // 2
            for i, by in [(0, 1), (1, -1)] if last else sent:
                if step > 1:
                    if last and step > 2:
                        moving[i, by] = after(sums[1 + i], moving[i, by])
                    elif step in (2, 3) and i == 1:
                        moving[i, by] = after((normed_own, normed)[step - 2], moving[i, by])
                    moving[i, by] = along_ring(moving[i, by], by)
                total = total + product(-by * step, i, moving[i, by])
            sums[step] = total
            if step == chips // 2 - 1:
                cand_ids, slab_owner = after(sums[1], (cand_ids, slab_owner))
    else:
        both = in_core_order(own, sibling, first_core)
        gathered = lax.all_gather(both, "chip", axis=0, tiled=True)
        total = jnp.dot(normed, gathered, preferred_element_type=jnp.float32)

    slab_rows = slab_owner.shape[0]
    slab_ids = jnp.arange(slab_rows, dtype=jnp.int32)[None, :]
    picked = [
        (cand_ids[:, j : j + 1] == slab_ids).astype(jnp.int32) for j in range(cand_ids.shape[1])
    ]
    ids = jnp.concatenate([token_ids[0], sum(picked), picked[0]], axis=1)
    ids = jnp.concatenate([ids, from_sibling(ids)])
    lengths = jnp.sum((ids[:, :length] != 0).astype(jnp.int32), axis=1)
    counts = lengths.astype(jnp.float32)
    masks = ids[:, length:].astype(jnp.float32)

    active = jnp.tanh(total).reshape(seqs, length, half)
    there = jnp.arange(length)[None, :, None] < lengths[:, None, None]
    pooled = jnp.sum(jnp.where(there, active, 0.0), axis=1) / counts[:, None]
    pooled_other = from_sibling(pooled)
    pooled_other = jnp.concatenate([pooled_other[seq_dev:], pooled_other[:seq_dev]])
    whole = in_core_order(pooled, pooled_other, first_core, axis=1)
    pooled_square = jnp.mean(whole * whole, axis=-1, keepdims=True)
    scale = lax.rsqrt(pooled_square + 1e-06)
    unit = whole * scale
    stored = unit.astype(jnp.bfloat16)
    stored = in_core_order(stored[:seq_dev], stored[seq_dev:], first_core)

    kept = slab_blocks(stored, chips)
    kept = jnp.concatenate(kept)
    slab = [kept, from_sibling(kept)]
    earlier = jnp.arange(slab_rows)[:, None] < jnp.arange(slab_rows)[None, :]
    same = slab_owner[:, None] == slab_owner[None, :]
    ranks = jnp.sum((earlier & same).astype(jnp.int32), axis=0)
    owner_place = ring_place(slab_owner // cores, chips)
    seen = lax.rem(owner_place - shift + 2 * chips, chips)
    slots = seen * seqs + lax.rem(slab_owner, cores) * seq_dev + ranks
    moved = (slots[:, None] == jnp.arange(slab_rows)[None, :]).astype(jnp.float32)
    candidate = jnp.dot(masks[:, :slab_rows], moved)
    positive = jnp.dot(masks[:, slab_rows:], moved)
    piece = slab_rows // cores
    pieces = [slice(i * piece, (i + 1) * piece) for i in range(cores)]

    slab_wide = [rows_in.astype(jnp.float32) for rows_in in slab]
    exponent = []
    for rows_in, at in zip(slab_wide, pieces):
        logits = (
            sharpness / embedding * jnp.dot(unit, rows_in.T, precision=lax.Precision.HIGHEST)
        )
        exponent.append(jnp.where(candidate[:, at] > 0.5, jnp.exp(logits), 0.0))
    denominator = sum(jnp.sum(part, axis=-1, keepdims=True) for part in exponent)
    unit_grad = (
        sharpness
        / embedding
        * sum(
            jnp.dot(
                part / denominator - positive[:, at], rows_in, precision=lax.Precision.HIGHEST
            )
            for part, rows_in, at in zip(exponent, slab_wide, pieces)
        )
    )
    inner = jnp.sum(whole * unit_grad, axis=-1, keepdims=True)
    pooled_grad = scale * unit_grad - whole * (scale * scale * scale) * inner / embedding
    pooled_grad = cut(pooled_grad, 1, own_columns, half)
    delta = (pooled_grad / counts[:, None])[:, None, :] * (1.0 - active * active)
    delta = jnp.where(there, delta, 0.0)
    delta = delta.astype(jnp.bfloat16).reshape(seqs * length, half)

    def term(offset, i, delta):
        return lax.dot_general(
            columns(offset, i),
            delta,
            (((0,), (0,)), ((), ())),
            preferred_element_type=jnp.float32,
        )

    if chips <= longest_ring:
        four, three = [(0, 1), (1, -1)], [(1, 1), (0, -1)]
        hops = [(chips // 2, four)]
        for step in range(chips // 2 - 1, 0, -1):
            hops += [(step, three), (step, four)]
        arrived, previous, source = {}, delta, delta
        for hop, (step, ways) in enumerate(hops):
            totals = []
            for i, by in ways:
                total = term(by * step, i, source)
                if (i, by) in arrived:
                    before = after(previous, arrived[i, by])
                    total = total + before.astype(jnp.float32)
                totals.append(total.astype(jnp.bfloat16))
            if hop == len(hops) - 1:
                totals = after(copied, totals)
            for (i, by), total in zip(ways, totals):
                arrived[i, by] = along_ring(total, by)
            previous = totals
            if hop == 0:
                source = after(totals, delta)
                late, weights = after(arrived[0, 1], (delta, weights))
                copied = passed_on(weights)
            else:
                source = late
        owns = [term(0, i, late) for i in range(2)]
        arrived[1, 1] = after(owns, arrived[1, 1])
        arrived[0, -1] = after(owns, arrived[0, -1])
        mine, other = [
            owns[i] + arrived[i, 1].astype(jnp.float32) + arrived[i, -1].astype(jnp.float32)
            for i in range(2)
        ]
    else:
        grad = lax.dot_general(
            normed, delta, (((0,), (0,)), ((), ())), preferred_element_type=jnp.float32
        )
        copied = passed_on(weights)
        reduced = lax.psum_scatter(grad, "chip", scatter_dimension=0, tiled=True)
        mine, other = [cut(reduced, 0, part * rows, rows) for part in parts]
    other = from_sibling(other)
    shard = in_core_order(mine, other, first_core, axis=1)
    row_square = jnp.mean(shard * shard, axis=1, keepdims=True)
    normalized = shard * lax.rsqrt(row_square + 1e-06)
    result = jnp.where(trainer, normalized, copied.astype(jnp.float32))
    return result[None]


def solution(mesh):
    groups, devices_fsdp = mesh.devices.shape
    finer = Mesh(
        mesh.devices.reshape(groups, devices_fsdp // cores, cores), ("grp", "chip", "core")
    )
    fsdp = ("chip", "core")
    placed = (
        P("grp", fsdp, None, None),
        P("grp", fsdp, None),
        P("grp", fsdp, None),
        P(),
        P(fsdp, None),
        P(),
    )
    return jax.shard_map(
        shards, mesh=finer, in_specs=placed, out_specs=P("grp", fsdp, None), check_vma=False
    )
```
